32 devices in a mesh: seq: 16 (over z, x, core), row: 2 (over y).
Axes of the slice: x: 2, y: 2, z: 4, core: 2. Of those that a mesh axis runs over, the one named last changes fastest.
Arguments:
- hidden_in: bfloat16 [6, 1024, 1024], P('row', 'seq'), may hold values from -6 to 6
- grad_out: bfloat16 [6, 1024, 1024], P('row', 'seq'), may hold values from -6 to 6
- doc_starts: int32 [6, 8], P('row'), may hold values from 0 to 1023, as said below
- norm_gain: bfloat16 [1024], P(('seq', 'row')), may hold values from 0.5 to 1.5
- in_proj: bfloat16 [4096, 1024], P(('seq', 'row')), may hold values from -0.1875 to 0.1875
- out_proj: bfloat16 [1024, 2048], P(('seq', 'row')), may hold values from -0.25 to 0.25
- conv_weight: bfloat16 [4, 2048], P(None, 'seq'), may hold values from -3 to 3
- conv_bias: bfloat16 [2048], P('seq'), may hold values from -3 to 3
- x_proj: bfloat16 [2048, 96], P('seq'), may hold values from -0.125 to 0.125
- dt_proj: bfloat16 [64, 2048], P(None, 'seq'), may hold values from -0.75 to 0.75
- dt_bias: bfloat16 [2048], P('seq'), may hold values from -6.875 to -2.25
- decay_log: bfloat16 [16, 2048], P(None, 'seq'), may hold values from 0 to 2.765625
- skip_scale: bfloat16 [2048], P('seq'), may hold values from 0.5 to 1.5
Outputs:
- hidden_out: bfloat16 [6, 1024, 1024], P('row', 'seq')
- grad_hidden: float32 [6, 1024, 1024], P('row', 'seq')
- grad_norm_gain: float32 [1024], P(('seq', 'row'))
- grad_in_proj: float32 [4096, 1024], P(('seq', 'row'))
- grad_out_proj: float32 [1024, 2048], P(('seq', 'row'))
- grad_conv_weight: float32 [4, 2048], P(None, 'seq')
- grad_conv_bias: float32 [2048], P('seq')
- grad_x_proj: float32 [2048, 96], P('seq')
- grad_dt_proj: float32 [64, 2048], P(None, 'seq')
- grad_dt_bias: float32 [2048], P('seq')
- grad_decay_log: float32 [16, 2048], P(None, 'seq')
- grad_skip_scale: float32 [2048], P('seq')
- dt_stats: float32 [2, 2048], P(None, 'seq')
The draws below stay inside these ranges and needn't reach their ends.
Inputs may be any that keep to these rules, and one draw needn't show every extreme that they name: doc_starts[r, 0] is 0 and each row's 8 starts rise strictly; in each group of 3 rows that one index of row holds, one row's first document covers every position before its last 64, and that row's last start is 1023.
All inputs are finite; a program needn't handle non-finite values.
Results may differ from the reference program's by a relative error of at most 0.012.
The reference program's roundings to bfloat16 on the way count: a program that leaves them out, or rounds other values in their place, can miss the bound.
Values may be sent and summed in bfloat16 or wider, within the bound.
No kernel may reach another device: no remote copies, remote signals or barrier semaphores. Data moves between devices by JAX's collectives and lax.ppermute only.
A program may use at most 512 MiB of HBM per device.

```python
from functools import partial
import jax
import jax.numpy as jnp
from jax import lax

D = 1024
E = 2048
NSTATE = 16
CONV = 4
DT_RANK = 64
SEG_DEV = 64
DOCS = 8
RG = 3
SEQ_LEN = 1024
ROWS = 6


def drawn_row(row_key):
    chosen_points = jax.random.permutation(row_key, SEQ_LEN - 1)[:DOCS - 1] + 1
    return jnp.concatenate([jnp.zeros((1,), jnp.int32), jnp.sort(chosen_points.astype(jnp.int32))])


def spanning_row(row_key):
    chosen_points = jax.random.permutation(row_key, SEG_DEV - 2)[:DOCS - 2] + (SEQ_LEN - SEG_DEV + 1)
    return jnp.concatenate([jnp.zeros((1,), jnp.int32), jnp.sort(chosen_points.astype(jnp.int32)), jnp.full((1,), SEQ_LEN - 1, jnp.int32)])


def draw_doc_starts(key, part):
    key = jax.random.fold_in(key, 7)
    row_keys = jax.random.split(key, ROWS)
    drawn_rows = jax.vmap(drawn_row)(row_keys)
    span_rows = jax.vmap(spanning_row)(row_keys)
    chosen = jax.random.randint(jax.random.fold_in(key, 1), (ROWS // RG,), 0, RG).astype(jnp.int32)
    row_index = jnp.arange(ROWS, dtype=jnp.int32)
    is_span = row_index % RG == chosen[row_index // RG]
    return jnp.where(is_span[:, None], span_rows, drawn_rows)


def shard_levels(own_key, shape, cuts, smallest, largest):
    def one(position, blocks):
        heights = jax.random.uniform(jax.random.fold_in(jax.random.fold_in(own_key, 6), position), (blocks,), jnp.float32, smallest / len(cuts), largest / len(cuts))
        return jnp.repeat(jnp.exp(heights), shape[position] // blocks).reshape((-1,) + (1,) * (len(shape) - position - 1))

    loudness = one(*cuts[0])
    for cut in cuts[1:]:
        loudness = loudness * one(*cut)
    return loudness


def normal_values(stream_key, shape, scale, limit, cuts=(), kind=jnp.bfloat16):
    entries = scale * jax.random.normal(stream_key, shape, jnp.float32)
    if cuts:
        entries = entries * shard_levels(stream_key, shape, cuts, -0.22, 0.18)
    return jnp.clip(entries, -limit, limit).astype(kind)


def setup_inputs(seed: int = 0) -> dict:
    arg_keys = jax.random.split(jax.random.key(seed), 14)
    hidden_in = normal_values(arg_keys[0], (ROWS, SEQ_LEN, D), 1.0, 6.0, ((0, 2), (1, 16)))
    grad_out = normal_values(arg_keys[1], (ROWS, SEQ_LEN, D), 1.0, 6.0, ((0, 2), (1, 16)))
    doc_starts = draw_doc_starts(jax.random.fold_in(arg_keys[13], 71), 0)
    norm_gain = jnp.clip(1.0 + 0.1 * jax.random.normal(arg_keys[3], (D,), jnp.float32), 0.5, 1.5).astype(jnp.bfloat16)
    in_proj = normal_values(arg_keys[4], (2 * E, D), D ** -0.5, 0.1875, ((0, 32),))
    out_proj = normal_values(arg_keys[5], (D, E), (E // 4) ** -0.5, 0.25, ((0, 32),))
    conv_weight = normal_values(arg_keys[6], (CONV, E), CONV ** -0.5, 3.0, ((1, 16),))
    conv_bias = normal_values(arg_keys[7], (E,), 0.5, 3.0, ((0, 16),))
    x_proj = normal_values(arg_keys[8], (E, DT_RANK + 2 * NSTATE), E ** -0.5, 0.125, ((0, 16),))
    dt_proj = normal_values(arg_keys[9], (DT_RANK, E), DT_RANK ** -0.5, 0.75, ((1, 16),))
    dt_bias = jnp.clip(-6.875 + 4.625 * jax.random.uniform(arg_keys[10], (E,), jnp.float32) ** shard_levels(arg_keys[10], (E,), ((0, 16),), -0.2, 0.2), -6.875, -2.25).astype(jnp.bfloat16)
    decay_log = jnp.clip(2.765625 * jax.random.uniform(arg_keys[11], (NSTATE, E), jnp.float32) ** shard_levels(arg_keys[11], (NSTATE, E), ((1, 16),), -0.2, 0.2), 0.0, 2.765625).astype(jnp.bfloat16)
    skip_scale = jnp.clip(1.0 + 0.1 * jax.random.normal(arg_keys[12], (E,), jnp.float32), 0.5, 1.5).astype(jnp.bfloat16)
    return {"hidden_in": hidden_in, "grad_out": grad_out, "doc_starts": doc_starts, "norm_gain": norm_gain, "in_proj": in_proj, "out_proj": out_proj, "conv_weight": conv_weight, "conv_bias": conv_bias, "x_proj": x_proj, "dt_proj": dt_proj, "dt_bias": dt_bias, "decay_log": decay_log, "skip_scale": skip_scale}


eps_norm = 1e-05
eps_spread = 1e-06
block_len = 128
highest = lax.Precision.HIGHEST

@jax.custom_vjp
def low(v):
    return lax.optimization_barrier(v.astype(jnp.bfloat16)).astype(jnp.float32)

@jax.custom_vjp
def low_back(v):
    return v

def low_keep(v):
    return (low(v), None)

def low_pass(kept, grad):
    return (grad,)

def back_keep(v):
    return (v, None)

def back_low(kept, grad):
    return (low(grad),)
low.defvjp(low_keep, low_pass)
low_back.defvjp(back_keep, back_low)

def doc_marks(row_starts):
    positions = jnp.arange(SEQ_LEN, dtype=jnp.int32)
    return lax.optimization_barrier(jnp.sum((row_starts[None, :] <= positions[:, None]).astype(jnp.int32), axis=1)) - 1

def shifted(values, offset, filler):
    if offset == 0:
        return values
    widths = [(0, 0)] * values.ndim
    widths[0] = (offset, 0)
    return jnp.pad(values, widths, constant_values=filler)[:values.shape[0]]

def selective(dt_vals, x_vals, b_vals, c_vals, keep_mask, decay_log, skip_scale):
    decay_rates = -jnp.exp(decay_log)
    blocks = SEQ_LEN // block_len

    def block_fn(hidden_state, pieces):

        def advance(state_now, inputs):
            dt_now, x_now, b_now, c_now, keep_now = inputs
            decay_now = jnp.exp(dt_now[None, :] * decay_rates) * keep_now
            state_now = decay_now * state_now + b_now[:, None] * (dt_now * x_now)[None, :]
            return (state_now, lax.optimization_barrier(jnp.sum(c_now[:, None] * state_now, axis=0)))
        return lax.scan(advance, hidden_state, pieces)
    pieces = tuple((v.reshape((blocks, block_len) + v.shape[1:]) for v in (dt_vals, x_vals, b_vals, c_vals, keep_mask)))
    _, outputs = lax.scan(jax.checkpoint(block_fn), jnp.zeros((NSTATE, E), jnp.float32), pieces)
    return outputs.reshape(SEQ_LEN, E) + skip_scale * x_vals

def row_forward(doc_ids, keep_mask, residual, norm_gain, in_proj, out_proj, conv_weight, conv_bias, x_proj, dt_proj, dt_bias, decay_log, skip_scale):
    inv_rms = lax.rsqrt(lax.optimization_barrier(jnp.mean(residual * residual, axis=-1, keepdims=True)) + eps_norm)
    normed = low(residual * inv_rms * norm_gain)
    proj_in = low_back(jnp.dot(normed, in_proj.T, precision=highest))
    x_low = low(proj_in[:, :E])
    gate_z = proj_in[:, E:]
    pre_conv = conv_bias + jnp.zeros_like(x_low)
    for offset in range(CONV):
        same_doc = (shifted(doc_ids, offset, -1) == doc_ids).astype(jnp.float32)
        pre_conv = pre_conv + conv_weight[CONV - 1 - offset] * shifted(x_low, offset, 0.0) * same_doc[:, None]
    conv_low = low(jax.nn.silu(pre_conv))
    dtbc = low(low_back(jnp.dot(conv_low, x_proj, precision=highest)))
    dt_low = dtbc[:, :DT_RANK]
    b_vals = dtbc[:, DT_RANK:DT_RANK + NSTATE]
    c_vals = dtbc[:, DT_RANK + NSTATE:]
    pre_dt = low_back(jnp.dot(dt_low, dt_proj, precision=highest) + dt_bias)
    dt_vals = jax.nn.softplus(pre_dt)
    y_vals = low(low_back(selective(dt_vals, conv_low, b_vals, c_vals, keep_mask, decay_log, skip_scale)))
    gated = low(y_vals * jax.nn.silu(gate_z))
    result = residual + jnp.dot(gated, out_proj.T, precision=highest)
    centre = jnp.log(jax.nn.softplus(dt_bias))
    offset_dt = jnp.log(dt_vals) - centre
    return (result, (lax.optimization_barrier(jnp.sum(offset_dt, axis=0)), lax.optimization_barrier(jnp.sum(offset_dt * offset_dt, axis=0))))

def reference(hidden_in, grad_out, doc_starts, norm_gain, in_proj, out_proj, conv_weight, conv_bias, x_proj, dt_proj, dt_bias, decay_log, skip_scale):
    weights = tuple((w.astype(jnp.float32) for w in (norm_gain, in_proj, out_proj, conv_weight, conv_bias, x_proj, dt_proj, dt_bias, decay_log, skip_scale)))

    def per_row(running, row_items):
        hidden_row, grad_row, row_starts = row_items
        doc_ids = doc_marks(row_starts)
        keep_mask = jnp.concatenate([jnp.zeros((1,), jnp.float32), (doc_ids[1:] == doc_ids[:-1]).astype(jnp.float32)])
        result, pullback, stats_row = jax.vjp(partial(row_forward, doc_ids, keep_mask), hidden_row.astype(jnp.float32), *weights, has_aux=True)
        grads = pullback(grad_row.astype(jnp.float32))
        running = tuple((total_now + piece_now for total_now, piece_now in zip(running, tuple(grads[1:]) + tuple(stats_row))))
        return (running, (result.astype(jnp.bfloat16), grads[0]))
    start_sums = tuple((jnp.zeros_like(w) for w in weights)) + (jnp.zeros((E,), jnp.float32), jnp.zeros((E,), jnp.float32))
    totals, (hidden_out, grad_hidden) = lax.scan(per_row, start_sums, (hidden_in, grad_out, doc_starts))
    token_count = ROWS * SEQ_LEN
    mean_off = totals[10] / token_count
    spread = jnp.sqrt(totals[11] / token_count - mean_off * mean_off + eps_spread)
    centre = jnp.log(jax.nn.softplus(weights[7]))
    dt_stats = jnp.stack([centre + mean_off, spread])
    return (hidden_out, grad_hidden, totals[0], totals[1], totals[2], totals[3], totals[4], totals[5], totals[6], totals[7], totals[8], totals[9], dt_stats)
```

```python
from functools import partial

import jax
import jax.numpy as jnp
from jax import lax
from jax.experimental import pallas as pl
from jax.experimental.pallas import tpu as pltpu
from jax.sharding import PartitionSpec as P

E = 2048
NSTATE = 16
CONV = 4
DT_RANK = 64
MAPS = DT_RANK + 2 * NSTATE

eps_norm = 1e-05
eps_spread = 1e-06
BF = jnp.bfloat16
F32 = jnp.float32
LOG2E = 1.4426950408889634
FAR = 1e4
LANES = 128
VMEM = 40 << 20


def params():
    return pltpu.CompilerParams(
        dimension_semantics=("arbitrary", "arbitrary"), vmem_limit_bytes=VMEM
    )


def place_in_doc(starts_ref, row, first, count):
    pos = lax.broadcasted_iota(jnp.int32, (count, LANES), 0) + first
    base = jnp.zeros_like(pos)
    for j in range(1, starts_ref.shape[1]):
        start = starts_ref[row, j]
        base = jnp.where(pos >= start, start, base)
    return pos - base


def large(shape, dtype):
    return pltpu.HBM(shape, dtype)


def still(*values):
    return [pltpu.with_memory_space_constraint(v, pltpu.HBM) for v in values]


def sigmoid(v):
    return 1.0 / (1.0 + jnp.exp2(v * -LOG2E))


def silu_slope(v):
    s = sigmoid(v)
    return s * (1.0 + v * (1.0 - s))


def softplus(v):
    return jnp.maximum(v, 0.0) + jnp.log1p(jnp.exp2(jnp.abs(v) * -LOG2E))


def dot(a, b, dims):
    return lax.dot_general(a, b, (dims, ((), ())), preferred_element_type=F32)


def whole(shape):
    return pl.BlockSpec(shape, lambda r, c, s, o: (0,) * len(shape))


def own_place():
    s = lax.axis_index("seq")
    return jnp.stack([s // 4, s // 2 % 2, s % 2]).astype(jnp.int32)


def pieces_spec(seg, n, at, row):
    return pl.BlockSpec(
        (2, 1, 1, seg, n), lambda r, c, s, o: (0, at(c) ^ o[0], r + row, 0, 0)
    )


def put_pieces(own, value, keep, send):
    seg = keep.shape[3]
    first = own[2] == 0
    for x in range(2):
        even = value[2 * x * seg : (2 * x + 1) * seg]
        odd = value[(2 * x + 1) * seg : (2 * x + 2) * seg]
        keep[x ^ own[1], 0, 0] = jnp.where(first, even, odd).astype(keep.dtype)
        send[x ^ own[1], 0, 0] = jnp.where(first, odd, even).astype(send.dtype)


def take_pieces(own, near, far, out):
    seg = near.shape[3]
    first = own[2] == 0
    for x in range(2):
        a = near[x ^ own[1], 0, 0].astype(F32)
        b = far[x ^ own[1], 0, 0].astype(F32)
        out[2 * x * seg : (2 * x + 1) * seg, :] = jnp.where(first, a, b)
        out[(2 * x + 1) * seg : (2 * x + 2) * seg, :] = jnp.where(first, b, a)


def gate_kernel(*refs):
    pass


def gate(values, others):
    place = pl.BlockSpec(memory_space=pl.ANY)
    return pl.pallas_call(
        gate_kernel,
        in_specs=[place] * (len(values) + len(others)),
        out_specs=[place] * len(values),
        out_shape=[jax.ShapeDtypeStruct(v.shape, v.dtype) for v in values],
        input_output_aliases={i: i for i in range(len(values))},
        compiler_params=pltpu.CompilerParams(vmem_limit_bytes=1 << 16),
        cost_estimate=pl.CostEstimate(flops=1, bytes_accessed=1, transcendentals=0),
        name="gate",
    )(*values, *others)


PARTS = 6


def row_copies(own, parts, slots, sems, row):
    place = own[0] * 4 + own[1] * 2 + own[2]
    head = parts[0].shape[1]
    seg = parts[0].shape[2]
    copies = []
    for d in range(16):
        z, x, core = d >> 2, d >> 1 & 1, d & 1
        if row < head:
            piece = parts[core * 2 + x].at[z, row]
        else:
            piece = parts[4 + core].at[z, x, row - head]
        copies.append(
            pltpu.make_async_copy(
                piece,
                slots.at[row, pl.ds(pl.multiple_of((place ^ d) * seg, seg), seg)],
                sems.at[row, d],
            )
        )
    return copies


def bring_row(own, pieces, slots, sems):
    r, c = pl.program_id(0), pl.program_id(1)

    @pl.when((c == 0) & (r == 0))
    def _():
        for row in range(slots.shape[0]):
            for copy in row_copies(own, pieces, slots, sems, row):
                copy.start()

    for row in range(slots.shape[0]):

        @pl.when((c == 0) & (r == row))
        def _(row=row):
            for copy in row_copies(own, pieces, slots, sems, row):
                copy.wait()


def front_kernel(starts, own, *refs):
    pieces, refs = refs[:PARTS], refs[PARTS:]
    gain, weight, conv_w, conv_b, xproj = refs[:5]
    normed_o, x_o, z_o, conv_o, keep_o, send_o, xs, slots, sems = refs[-9:]
    r, c = pl.program_id(0), pl.program_id(1)
    t = x_o.shape[1]
    ch = conv_w.shape[1]
    bring_row(own, pieces, slots, sems)
    res = slots[r, pl.ds(pl.multiple_of(c * t, t), t), :].astype(F32)
    inv = lax.rsqrt(jnp.mean(res * res, axis=-1, keepdims=True) + eps_norm)
    normed = (res * inv * gain[...]).astype(BF)
    normed_o[0] = normed
    proj = dot(normed, weight[...], ((1,), (1,)))
    z_o[0] = proj[:, ch:]
    x_low = proj[:, :ch].astype(BF)
    x_o[0] = x_low

    @pl.when(c == 0)
    def _():
        xs[0:8, :] = jnp.zeros((8, ch), F32)

    @pl.when(c > 0)
    def _():
        xs[0:8, :] = xs[t : t + 8, :]

    xs[8 : 8 + t, :] = x_low.astype(F32)
    place = place_in_doc(starts, r, c * t, t)
    pre = conv_b[...] + conv_w[CONV - 1 : CONV, :] * xs[8 : 8 + t, :]
    for k in range(1, CONV):
        lag = conv_w[CONV - 1 - k : CONV - k, :] * xs[8 - k : 8 - k + t, :]
        pre = pre + jnp.where(place >= k, lag, 0.0)
    conv = (pre * sigmoid(pre)).astype(BF)
    conv_o[0] = conv
    put_pieces(own, dot(conv, xproj[...], ((1,), (0,))), keep_o, send_o)


def front(after, starts, own, pieces, gain, weight, conv_w, conv_b, xproj):
    _, _, seg, width = pieces[0].shape
    rows = starts.shape[0]
    ch = conv_w.shape[1]
    length = 16 * seg
    t = 4 * seg
    tok = lambda n: pl.BlockSpec((1, t, n), lambda r, c, s, o: (r, c, 0))
    piece = pieces_spec(seg, MAPS, lambda c: c, 0)
    return pl.pallas_call(
        front_kernel,
        grid_spec=pltpu.PrefetchScalarGridSpec(
            num_scalar_prefetch=2,
            grid=(rows, length // t),
            in_specs=[
                *[pl.BlockSpec(memory_space=pl.ANY)] * PARTS,
                whole(gain.shape),
                whole(weight.shape),
                whole(conv_w.shape),
                whole(conv_b.shape),
                whole(xproj.shape),
                *[pl.BlockSpec(memory_space=pl.ANY)] * len(after),
            ],
            out_specs=[tok(width), tok(ch), tok(ch), tok(ch), piece, piece],
            scratch_shapes=[
                pltpu.VMEM((t + 8, ch), F32),
                pltpu.VMEM((rows, length, width), BF),
                pltpu.SemaphoreType.DMA((rows, 16)),
            ],
        ),
        out_shape=[
            large((rows, length, width), BF),
            large((rows, length, ch), BF),
            large((rows, length, ch), F32),
            large((rows, length, ch), BF),
            jax.ShapeDtypeStruct((2, 4, rows, seg, MAPS), F32),
            jax.ShapeDtypeStruct((2, 4, rows, seg, MAPS), F32),
        ],
        compiler_params=params(),
        cost_estimate=pl.CostEstimate(flops=1, bytes_accessed=1, transcendentals=0),
        name="front",
    )(starts, own, *pieces, gain, weight, conv_w, conv_b, xproj, *after)


def maps_across(dtbc):
    pick = lax.broadcasted_iota(jnp.int32, (2 * NSTATE, MAPS), 0) + DT_RANK
    pick = (pick == lax.broadcasted_iota(jnp.int32, (2 * NSTATE, MAPS), 1)).astype(BF)
    return dot(pick, dtbc, ((1,), (1,)))


def forward_kernel(
    starts, own, near, far, dtproj, dtbias, decay, skip, conv, z, stats_i, *refs, row,
):
    (
        gated_o, y_o, states_o, last_o, stats_o,
        state, dtk_s, dtx_s, y_s, across_s, low_s,
    ) = refs[-11:]
    r, c = pl.program_id(0), pl.program_id(1)
    t, ch = conv.shape[1], conv.shape[2]

    @pl.when(c == 0)
    def _():
        state[...] = jnp.zeros_like(state)

    @pl.when((c == 0) & (r == 0))
    def _():
        stats_o[...] = stats_i[...]

    rate = -LOG2E * jnp.exp(decay[...])
    take_pieces(own, near, far, low_s)
    low = low_s[...].astype(BF)
    dt = softplus(dot(low[:, :DT_RANK], dtproj[...], ((1,), (0,))) + dtbias[...])
    off = jnp.log(dt) - jnp.log(softplus(dtbias[...]))
    stats_o[0:1, :] += jnp.sum(off, axis=0, keepdims=True)
    stats_o[1:2, :] += jnp.sum(off * off, axis=0, keepdims=True)
    x = conv[0].astype(F32)
    place = place_in_doc(starts, r + row, c * t, t)
    dtk_s[...] = jnp.where(place >= 1, dt, FAR)
    dtx_s[...] = dt * x
    across_s[...] = maps_across(low)

    def some(block, s):
        base = pl.multiple_of(block * LANES, LANES)
        both = across_s[:, pl.ds(base, LANES)]
        b, cm = both[:NSTATE], both[NSTATE:]
        for i in range(LANES):
            a = jnp.exp2(dtk_s[pl.ds(base + i, 1), :] * rate)
            states_o[0, base + i] = s
            u = dtx_s[pl.ds(base + i, 1), :] * jnp.broadcast_to(b[:, i : i + 1], (NSTATE, ch))
            s = a * s + u
            ys = s * jnp.broadcast_to(cm[:, i : i + 1], (NSTATE, ch))
            y_s[pl.ds(base * 8 + i * 8, 8), :] = ys[:8] + ys[8:]
        return s

    s = lax.fori_loop(0, t // LANES, some, state[...])
    state[...] = s
    last_o[0] = s
    y = y_s[pl.ds(0, t, stride=8), :]
    for j in range(1, 8):
        y = y + y_s[pl.ds(j, t, stride=8), :]
    y_low = (y + skip[...] * x).astype(BF)
    y_o[0] = y_low
    zz = z[0]
    gated_o[0] = (y_low.astype(F32) * (zz * sigmoid(zz))).astype(BF)


def forward_scan(
    row, rows, after, so_far, starts, own, near, far, dtproj, dtbias, decay, skip, conv, z
):
    conv, z = still(conv, z)
    rows_all, length, ch = conv.shape
    done, sums_so_far = so_far
    fixed = 11
    t = length // 4
    seg = t // 4
    tok = lambda n: pl.BlockSpec((1, t, n), lambda r, c, s, o: (r + row, c, 0))
    piece = pieces_spec(seg, MAPS, lambda c: c, row)
    return pl.pallas_call(
        partial(forward_kernel, row=row),
        grid_spec=pltpu.PrefetchScalarGridSpec(
            num_scalar_prefetch=2,
            grid=(rows, length // t),
            in_specs=[
                piece,
                piece,
                whole(dtproj.shape),
                whole(dtbias.shape),
                whole(decay.shape),
                whole(skip.shape),
                tok(ch),
                tok(ch),
                whole((8, ch)),
                *[pl.BlockSpec(memory_space=pl.ANY)] * (len(done) + len(after)),
            ],
            out_specs=[
                tok(ch),
                tok(ch),
                pl.BlockSpec((1, t, NSTATE, ch), lambda r, c, s, o: (r + row, c, 0, 0)),
                pl.BlockSpec((1, NSTATE, ch), lambda r, c, s, o: (r + row, 0, 0)),
                whole((8, ch)),
            ],
            scratch_shapes=[
                pltpu.VMEM((NSTATE, ch), F32),
                pltpu.VMEM((t, ch), F32),
                pltpu.VMEM((t, ch), F32),
                pltpu.VMEM((t * 8, ch), F32),
                pltpu.VMEM((2 * NSTATE, t), F32),
                pltpu.VMEM((t, MAPS), F32),
            ],
        ),
        out_shape=[
            large((rows_all, length, ch), BF),
            large((rows_all, length, ch), BF),
            large((rows_all, length, NSTATE, ch), F32),
            jax.ShapeDtypeStruct((rows_all, NSTATE, ch), F32),
            jax.ShapeDtypeStruct((8, ch), F32),
        ],
        input_output_aliases={fixed + i: i for i in range(len(done))},
        compiler_params=params(),
        cost_estimate=pl.CostEstimate(flops=1, bytes_accessed=1, transcendentals=0),
        name="forward_scan",
    )(
        starts, own, near, far, dtproj, dtbias, decay, skip, conv, z, *sums_so_far, *done, *after
    )


def backward_kernel(
    starts, own, near, far, dtproj, dtbias, decay, skip, conv, z, y, gg, states, last, sums,
    gdtproj_i, misc_i, *refs, row,
):
    (
        ggate_o, gxs_o, keep_o, send_o, gdtproj_o, misc_o,
        back, after, dtk_s, dt_s, dtx_s, gy_s, p1_s, p2_s, gb_s, gc_s, across_s, low_s,
    ) = refs[-18:]
    r, c = pl.program_id(0), pl.program_id(1)
    chunks = pl.num_programs(1)
    t, ch = conv.shape[1], conv.shape[2]

    @pl.when(c == 0)
    def _():
        back[...] = jnp.zeros_like(back)
        after[...] = last[0]

    @pl.when((c == 0) & (r == 0))
    def _():
        gdtproj_o[...] = gdtproj_i[...]
        misc_o[...] = misc_i[...]

    neg = -jnp.exp(decay[...])
    rate = LOG2E * neg
    take_pieces(own, near, far, low_s)
    low = low_s[...].astype(BF)
    pre = dot(low[:, :DT_RANK], dtproj[...], ((1,), (0,))) + dtbias[...]
    dt = softplus(pre)
    x = conv[0].astype(F32)
    place = place_in_doc(starts, r + row, (chunks - 1 - c) * t, t)
    dtk_s[...] = jnp.where(place >= 1, dt, FAR)
    dt_s[...] = dt
    dtx_s[...] = dt * x
    zz = z[0]
    ggv = gg[0]
    sg = sigmoid(zz)
    gy = (ggv * (zz * sg)).astype(BF).astype(F32)
    ggate_o[0] = (ggv * y[0].astype(F32) * (sg * (1.0 + zz * (1.0 - sg)))).astype(BF)
    gy_s[...] = gy
    across_s[...] = maps_across(low)

    def some(block, carry):
        h, s_next, acc = carry
        base = pl.multiple_of(t - LANES - block * LANES, LANES)
        both = across_s[:, pl.ds(base, LANES)]
        b, cm = both[:NSTATE], both[NSTATE:]
        for i in range(LANES - 1, -1, -1):
            at = base + i
            gyr = gy_s[pl.ds(at, 1), :]
            g = gyr * jnp.broadcast_to(cm[:, i : i + 1], (NSTATE, ch)) + h
            h = jnp.exp2(dtk_s[pl.ds(at, 1), :] * rate) * g
            s_prev = states[0, at]
            q = h * s_prev
            acc = acc + q * dt_s[pl.ds(at, 1), :]
            aq = q * neg
            bg = g * jnp.broadcast_to(b[:, i : i + 1], (NSTATE, ch))
            p2_s[pl.ds(base * 8 + i * 8, 8), :] = aq[:8] + aq[8:]
            p1_s[pl.ds(base * 8 + i * 8, 8), :] = bg[:8] + bg[8:]
            gb_s[pl.ds(base * NSTATE + i * NSTATE, NSTATE), :] = g * dtx_s[pl.ds(at, 1), :]
            gc_s[pl.ds(base * NSTATE + i * NSTATE, NSTATE), :] = gyr * s_next
            s_next = s_prev
        return h, s_next, acc

    h, s_next, acc = lax.fori_loop(
        0, t // LANES, some, (back[...], after[...], jnp.zeros((NSTATE, ch), F32))
    )
    back[...] = h
    after[...] = s_next
    p1 = p1_s[pl.ds(0, t, stride=8), :]
    p2 = p2_s[pl.ds(0, t, stride=8), :]
    for j in range(1, 8):
        p1 = p1 + p1_s[pl.ds(j, t, stride=8), :]
        p2 = p2 + p2_s[pl.ds(j, t, stride=8), :]
    gxs_o[0] = dt * p1 + skip[...] * gy
    gpre = ((p2 + x * p1) * sigmoid(pre)).astype(BF)
    gdtproj_o[...] += dot(low[:, :DT_RANK], gpre, ((0,), (0,)))
    misc_o[0:NSTATE, :] += neg * acc
    misc_o[NSTATE : NSTATE + 1, :] += jnp.sum(gpre.astype(F32), axis=0, keepdims=True)
    misc_o[NSTATE + 1 : NSTATE + 2, :] += jnp.sum(gy * x, axis=0, keepdims=True)
    total = dot(gpre, sums[0:ch, :], ((1,), (0,)))
    for n in range(NSTATE):
        one = gb_s[pl.ds(n, t, stride=NSTATE), :].astype(BF)
        two = gc_s[pl.ds(n, t, stride=NSTATE), :].astype(BF)
        total = total + dot(one, sums[(1 + n) * ch : (2 + n) * ch, :], ((1,), (0,)))
        total = total + dot(
            two, sums[(1 + NSTATE + n) * ch : (2 + NSTATE + n) * ch, :], ((1,), (0,))
        )
    put_pieces(own, total, keep_o, send_o)


def sum_columns(dtproj):
    ch = dtproj.shape[1]
    which = jnp.arange(2 * NSTATE * ch) // ch + DT_RANK
    ones = (which[:, None] == jnp.arange(MAPS)[None, :]).astype(BF)
    wide = jnp.pad(dtproj.T, ((0, 0), (0, 2 * NSTATE)))
    return jnp.concatenate([wide, ones], axis=0)


def backward_scan(
    row, rows, after, so_far, starts, own, near, far, dtproj, dtbias, decay, skip, conv, z, y, gg,
    states, last, sums,
):
    conv, z, y, gg, states = still(conv, z, y, gg, states)
    rows_all, length, ch = conv.shape
    done, sums_so_far = so_far
    t = length // 4
    seg = t // 4
    chunks = length // t
    tok = lambda n: pl.BlockSpec((1, t, n), lambda r, c, s, o: (r + row, chunks - 1 - c, 0))
    piece = pieces_spec(seg, MAPS, lambda c: chunks - 1 - c, row)
    fixed = 17
    return pl.pallas_call(
        partial(backward_kernel, row=row),
        grid_spec=pltpu.PrefetchScalarGridSpec(
            num_scalar_prefetch=2,
            grid=(rows, chunks),
            in_specs=[
                piece,
                piece,
                whole(dtproj.shape),
                whole(dtbias.shape),
                whole(decay.shape),
                whole(skip.shape),
                tok(ch),
                tok(ch),
                tok(ch),
                tok(ch),
                pl.BlockSpec((1, t, NSTATE, ch), lambda r, c, s, o: (r + row, chunks - 1 - c, 0, 0)),
                pl.BlockSpec((1, NSTATE, ch), lambda r, c, s, o: (r + row, 0, 0)),
                whole(sums.shape),
                whole((DT_RANK, ch)),
                whole((24, ch)),
                *[pl.BlockSpec(memory_space=pl.ANY)] * (len(done) + len(after)),
            ],
            out_specs=[
                tok(ch),
                tok(ch),
                piece,
                piece,
                whole((DT_RANK, ch)),
                whole((24, ch)),
            ],
            scratch_shapes=[
                pltpu.VMEM((NSTATE, ch), F32),
                pltpu.VMEM((NSTATE, ch), F32),
                pltpu.VMEM((t, ch), F32),
                pltpu.VMEM((t, ch), F32),
                pltpu.VMEM((t, ch), F32),
                pltpu.VMEM((t, ch), F32),
                pltpu.VMEM((t * 8, ch), F32),
                pltpu.VMEM((t * 8, ch), F32),
                pltpu.VMEM((t * NSTATE, ch), F32),
                pltpu.VMEM((t * NSTATE, ch), F32),
                pltpu.VMEM((2 * NSTATE, t), F32),
                pltpu.VMEM((t, MAPS), F32),
            ],
        ),
        out_shape=[
            large((rows_all, length, ch), BF),
            large((rows_all, length, ch), F32),
            jax.ShapeDtypeStruct((2, 4, rows_all, seg, MAPS), F32),
            jax.ShapeDtypeStruct((2, 4, rows_all, seg, MAPS), F32),
            jax.ShapeDtypeStruct((DT_RANK, ch), F32),
            jax.ShapeDtypeStruct((24, ch), F32),
        ],
        input_output_aliases={fixed + i: i for i in range(len(done))},
        compiler_params=params(),
        cost_estimate=pl.CostEstimate(flops=1, bytes_accessed=1, transcendentals=0),
        name="backward_scan",
    )(
        starts, own, near, far, dtproj, dtbias, decay, skip, conv, z, y, gg, states, last, sums, *sums_so_far, *done, *after,
    )


def tail_kernel(
    starts, own, near, far, conv, gxs, ggate, x, before, normed, weight, conv_w, conv_b, xproj,
    gin_i, gxproj_i, misc_i, *refs, row,
):
    keep_o, send_o, gin_o, gxproj_o, misc_o, xs, gm_s, low_s = refs[-8:]
    r, c = pl.program_id(0), pl.program_id(1)
    chunks = pl.num_programs(1)
    t, ch = conv.shape[1], conv.shape[2]

    @pl.when((c == 0) & (r == 0))
    def _():
        gin_o[...] = gin_i[...]
        gxproj_o[...] = gxproj_i[...]
        misc_o[...] = misc_i[...]

    @pl.when(c == 0)
    def _():
        gm_s[:, t : t + 8, :] = jnp.zeros((CONV - 1, 8, ch), F32)

    @pl.when(c > 0)
    def _():
        gm_s[:, t : t + 8, :] = gm_s[:, 0:8, :]

    xs[0:16, :] = before[0].astype(F32)
    xs[16 : 16 + t, :] = x[0].astype(F32)
    place = place_in_doc(starts, r + row, (chunks - 1 - c) * t, t)
    lags = [xs[16 : 16 + t, :]]
    pre = conv_b[...] + conv_w[CONV - 1 : CONV, :] * lags[0]
    for k in range(1, CONV):
        lags.append(jnp.where(place >= k, xs[16 - k : 16 - k + t, :], 0.0))
        pre = pre + conv_w[CONV - 1 - k : CONV - k, :] * lags[k]
    take_pieces(own, near, far, low_s)
    low = low_s[...].astype(BF)
    gpre = (gxs[0] + dot(low, xproj[...], ((1,), (1,)))) * silu_slope(pre)
    gxproj_o[...] += dot(conv[0], low, ((0,), (0,)))
    gx = conv_w[CONV - 1 : CONV, :] * gpre
    for k in range(CONV):
        misc_o[CONV - 1 - k : CONV - k, :] += jnp.sum(gpre * lags[k], axis=0, keepdims=True)
        if k:
            gm_s[k - 1, 0:t, :] = jnp.where(place >= k, gpre, 0.0)
            gx = gx + conv_w[CONV - 1 - k : CONV - k, :] * gm_s[k - 1, k : k + t, :]
    misc_o[CONV : CONV + 1, :] += jnp.sum(gpre, axis=0, keepdims=True)
    gproj = jnp.concatenate([gx.astype(BF), ggate[0]], axis=1)
    gin_o[...] += dot(gproj, normed[0], ((0,), (0,)))
    put_pieces(own, dot(gproj, weight[...], ((1,), (0,))), keep_o, send_o)


def tail(
    row, rows, after, so_far, starts, own, near, far, conv, gxs, ggate, x, normed, weight, conv_w, conv_b, xproj
):
    conv, gxs, ggate, x, normed = still(conv, gxs, ggate, x, normed)
    _, length, width = normed.shape
    ch = conv.shape[2]
    t = length // 4
    seg = t // 4
    chunks = length // t
    tok = lambda n: pl.BlockSpec((1, t, n), lambda r, c, s, o: (r + row, chunks - 1 - c, 0))
    piece = lambda n, row: pieces_spec(seg, n, lambda c: chunks - 1 - c, row)
    before = pl.BlockSpec(
        (1, 16, ch),
        lambda r, c, s, o: (r + row, jnp.maximum((chunks - 1 - c) * (t // 16) - 1, 0), 0),
    )
    return pl.pallas_call(
        partial(tail_kernel, row=row),
        grid_spec=pltpu.PrefetchScalarGridSpec(
            num_scalar_prefetch=2,
            grid=(rows, chunks),
            in_specs=[
                piece(MAPS, row),
                piece(MAPS, row),
                tok(ch),
                tok(ch),
                tok(ch),
                tok(ch),
                before,
                tok(width),
                whole(weight.shape),
                whole(conv_w.shape),
                whole(conv_b.shape),
                whole(xproj.shape),
                whole(weight.shape),
                whole((ch, MAPS)),
                whole((8, ch)),
                *[pl.BlockSpec(memory_space=pl.ANY)] * len(after),
            ],
            out_specs=[
                piece(width, 0),
                piece(width, 0),
                whole(weight.shape),
                whole((ch, MAPS)),
                whole((8, ch)),
            ],
            scratch_shapes=[
                pltpu.VMEM((t + 16, ch), F32),
                pltpu.VMEM((CONV - 1, t + 8, ch), F32),
                pltpu.VMEM((t, MAPS), F32),
            ],
        ),
        out_shape=[
            large((2, 4, rows, seg, width), BF),
            large((2, 4, rows, seg, width), BF),
            jax.ShapeDtypeStruct(weight.shape, F32),
            jax.ShapeDtypeStruct((ch, MAPS), F32),
            jax.ShapeDtypeStruct((8, ch), F32),
        ],
        compiler_params=params(),
        cost_estimate=pl.CostEstimate(flops=1, bytes_accessed=1, transcendentals=0),
        name="tail",
    )(
        starts, own, near, far, conv, gxs, ggate, x, x, normed, weight, conv_w, conv_b, xproj, *so_far, *after,
    )


def mix_kernel(own, gated, cols, *refs):
    keep_o, send_o = refs[-2:]
    put_pieces(own, dot(gated[0], cols[...], ((1,), (1,))), keep_o, send_o)


def mix(row, rows, after, own, gated, cols):
    (gated,) = still(gated)
    _, length, ch = gated.shape
    width = cols.shape[0]
    t = length // 4
    seg = t // 4
    piece = pl.BlockSpec((2, 1, 1, seg, width), lambda r, c, o: (0, c ^ o[0], r, 0, 0))
    return pl.pallas_call(
        mix_kernel,
        grid_spec=pltpu.PrefetchScalarGridSpec(
            num_scalar_prefetch=1,
            grid=(rows, length // t),
            in_specs=[
                pl.BlockSpec((1, t, ch), lambda r, c, o: (r + row, c, 0)),
                pl.BlockSpec(cols.shape, lambda r, c, o: (0, 0)),
                *[pl.BlockSpec(memory_space=pl.ANY)] * len(after),
            ],
            out_specs=[piece, piece],
        ),
        out_shape=[
            large((2, 4, rows, seg, width), BF),
            large((2, 4, rows, seg, width), BF),
        ],
        compiler_params=params(),
        cost_estimate=pl.CostEstimate(flops=1, bytes_accessed=1, transcendentals=0),
        name="mix",
    )(own, gated, cols, *after)


def turn_kernel(own, *refs):
    pieces = refs[:PARTS]
    cols = refs[PARTS]
    gg_o, gout_o, slots, sems = refs[-4:]
    r, c = pl.program_id(0), pl.program_id(1)
    t = gg_o.shape[1]
    bring_row(own, pieces, slots, sems)
    part = slots[r, pl.ds(pl.multiple_of(c * t, t), t), :]
    gout_o[0] = part
    gg_o[0] = dot(part, cols[...], ((1,), (0,)))


def turn(rows, after, own, pieces, cols):
    _, _, seg, width = pieces[0].shape
    ch = cols.shape[1]
    length = 16 * seg
    t = 4 * seg
    tok = lambda n: pl.BlockSpec((1, t, n), lambda r, c, o: (r, c, 0))
    return pl.pallas_call(
        turn_kernel,
        grid_spec=pltpu.PrefetchScalarGridSpec(
            num_scalar_prefetch=1,
            grid=(rows, length // t),
            in_specs=[
                *[pl.BlockSpec(memory_space=pl.ANY)] * PARTS,
                pl.BlockSpec(cols.shape, lambda r, c, o: (0, 0)),
                *[pl.BlockSpec(memory_space=pl.ANY)] * len(after),
            ],
            out_specs=[tok(ch), tok(width)],
            scratch_shapes=[
                pltpu.VMEM((rows, length, width), BF),
                pltpu.SemaphoreType.DMA((rows, 16)),
            ],
        ),
        out_shape=[
            large((rows, length, ch), F32),
            large((rows, length, width), BF),
        ],
        compiler_params=params(),
        cost_estimate=pl.CostEstimate(flops=1, bytes_accessed=1, transcendentals=0),
        name="turn",
    )(own, *pieces, cols, *after)


def cross(v, bits):
    return lax.ppermute(v, "seq", [(s, s ^ bits) for s in range(16)])


def swap_row(v):
    return lax.ppermute(v, "row", [(0, 1), (1, 0)])


def total_of_all(v):
    v = v + swap_row(v)
    for bits in (1, 2, 4, 8):
        v = v + cross(v, bits)
    return v


def sum_pieces(keep, send, sent, others):
    (acc,) = gate([keep.astype(F32) + cross(send, 1).astype(F32)], others)
    acc = acc[0] + cross(acc[1].astype(sent), 2).astype(F32)
    total = acc[0]
    for k in (1, 2, 3):
        total = total + cross(acc[k].astype(sent), 4 * k).astype(F32)
    return total


def spread_pieces(own_piece):
    line = jnp.stack([own_piece] + [cross(own_piece, 4 * k) for k in (1, 2, 3)])
    near = jnp.stack([line, cross(line, 2)])
    return near, cross(near, 1)


def gather_start(v, after):
    head = v.shape[0] - v.shape[0] // 3
    return gate([v[:head], v[head:]], after)


def gather_first(a, b):
    return a, b, cross_z([a] * 3), cross(b, 2)


def gather_pause(a, b, line, across):
    return jnp.stack([a, *line]), jnp.stack([b, across])


def gather_second(a, b):
    return a, b, cross(a, 2), cross_z([b] * 3)


def gather_third(a, b, across, line):
    a, b = [a, across], jnp.stack([b, *line])
    return [*a, *[cross(p, 1) for p in a], b, cross(b, 1)]


def up(v):
    return v.astype(F32)


class Sum:
    def __init__(self, keep, send):
        self.keep, self.near = keep, cross(send, 1)
        self.head = keep.shape[2] - keep.shape[2] // 3

    def part(self, *at):
        return up(self.keep[at]) + up(self.near[at])

    def first(self, others):
        (self.near,) = gate([self.near], others)
        a, b = slice(0, self.head), slice(self.head, None)
        sent = [self.part(1, slice(None), a).astype(BF)]
        sent += [self.part(slice(None), k, b).astype(BF) for k in (1, 2, 3)]
        self.second_of = [cross(sent[0], 2), *cross_z(sent[1:])]
        return sent

    def second(self, others):
        across, *line = gate(self.second_of, others)
        a, b = slice(0, self.head), slice(self.head, None)
        sent = [(self.part(0, k, a) + up(across[k])).astype(BF) for k in (1, 2, 3)]
        sent.append((self.part(1, 0, b) + sum(up(v[1]) for v in line)).astype(BF))
        self.third_of = [*cross_z(sent[:3]), cross(sent[3], 2)]
        self.a = self.part(0, 0, a) + up(across[0])
        self.b = self.part(0, 0, b) + sum(up(v[0]) for v in line)
        return sent

    def third(self, others):
        *line, across = gate(self.third_of, others)
        return jnp.concatenate([self.a + sum(up(v) for v in line), self.b + up(across)])


def cross_z(pieces):
    return [cross(v, 4 * k) for k, v in zip((1, 2, 3), pieces)]


def channel_plan(
    hidden_in, grad_out, doc_starts, norm_gain, in_proj, out_proj, conv_weight, conv_bias,
    x_proj, dt_proj, dt_bias, decay_log, skip_scale,
):
    row_count, seg_len, width = hidden_in.shape
    shards = lax.axis_size("seq")
    full_len = seg_len * shards
    ch = conv_weight.shape[1]
    first = lax.axis_index("row") == 0
    both = ("seq", "row")
    place = 2 * lax.axis_index("seq") + lax.axis_index("row")
    own = own_place()
    gain_len = norm_gain.shape[0]

    to_shard = [(i, 2 * (i % shards) + i // shards) for i in range(2 * shards)]
    mine = lax.ppermute(in_proj, both, to_shard)
    head = row_count - row_count // 3
    hid = gather_first(*gate([hidden_in[:head], hidden_in[head:]], []))
    spot = jnp.zeros((2 * shards, gain_len), F32)
    spot = lax.dynamic_update_slice(spot, norm_gain.astype(F32)[None], (place, 0))
    spot = spot + swap_row(spot)
    *hid, mine, spot = gate([*hid[:2], *hid[2], hid[3], mine, spot + sum(cross_z([spot] * 3))], [])
    hid = gather_second(*gather_pause(*hid[:2], hid[2:5], hid[5]))
    other = swap_row(mine)
    weight = jnp.concatenate([jnp.where(first, mine, other), jnp.where(first, other, mine)])
    other = swap_row(out_proj)
    pair = jnp.concatenate([jnp.where(first, out_proj, other), jnp.where(first, other, out_proj)])
    spot = spot + cross(spot, 1)
    sent = [grad_out[:head], grad_out[head:]]
    vectors = [
        conv_weight.astype(F32),
        conv_bias.astype(F32)[None],
        dt_bias.astype(F32)[None],
        decay_log.astype(F32),
        skip_scale.astype(F32)[None],
        sum_columns(dt_proj),
        x_proj,
    ]
    held = gate([*hid[:3], *hid[3], weight, pair, spot, *sent, *vectors], [])
    hid, (weight, pair, spot, *sent), vectors = held[:6], held[6:11], held[11:]
    gain_whole = (spot + cross(spot, 2)).reshape(1, width)
    conv_w, conv_b, dtb, decay, skip, sums, x_proj = vectors
    hid = gather_third(*hid[:3], hid[3:6])
    sent = gate(sent, [*hid, gain_whole])
    gout = gather_first(*sent)

    normed, x, z, conv, keep, send = front(
        sent, doc_starts, own, hid, gain_whole, weight, conv_w, conv_b, x_proj
    )
    keep, send, *gout = gate([keep, send, *gout[:2], *gout[2], gout[3]], [])
    gout = gather_pause(*gout[:2], gout[2:5], gout[5])
    low = sum_pieces(keep, send, F32, []).astype(BF)
    near, far = spread_pieces(low)
    pair, *gout = gate([pair, *gout], [far])
    gout = gather_second(*gout)
    out_cols = lax.all_to_all(pair, "seq", split_axis=1, concat_axis=0, tiled=True)

    gated, y, states, last, stats = forward_scan(
        0, row_count, [gout[0], gout[1], pair], ([], (jnp.zeros((8, ch), F32),)), doc_starts, own, near, far, dt_proj,
        dtb, decay, skip, conv, z,
    )
    gated, out_cols, *gout = gate([gated, out_cols, *gout[:3], *gout[3]], [])
    gout = gather_third(*gout[:3], gout[3:])
    keep, send = mix(0, row_count, [], own, gated, out_cols)
    keep, send, *gout = gate([keep, send, *gout], [])
    mixed = Sum(keep, send)
    gg, gout = turn(row_count, [], own, gout, out_cols)
    after = mixed.first([gg])
    back = [], (jnp.zeros((DT_RANK, ch), F32), jnp.zeros((24, ch), F32))
    for r in range(row_count):
        out = backward_scan(
            r, 1, after, back, doc_starts, own, near, far, dt_proj, dtb, decay, skip,
            conv, z, y, gg, states, last, sums,
        )
        back = out[:4], out[4:]
        after = mixed.second([out[0]]) if r == row_count - 2 else []
    ggate, gxs, keep, send = back[0]
    gdtproj, misc = back[1]
    mixed = mixed.third([gxs])
    keep, send, gout, gated = gate([keep, send, gout, gated], [mixed])
    low = sum_pieces(keep, send, BF, []).astype(BF)
    gout_cols = jnp.einsum("rtd,rtc->dc", gout, gated, preferred_element_type=F32)
    parts = gout_cols.reshape(shards, 2, width // (2 * shards), ch)
    keep = jnp.where(first, parts[:, 0], parts[:, 1])
    send = jnp.where(first, parts[:, 1], parts[:, 0])
    out_half = (keep + swap_row(send)).astype(BF)
    near, far = spread_pieces(low)
    tail_sums = (jnp.zeros(weight.shape, F32), jnp.zeros((ch, MAPS), F32), jnp.zeros((8, ch), F32))
    keep, send, gin, gxproj, cmisc = tail(
        0, row_count, [out_half], tail_sums, doc_starts, own, near, far, conv, gxs, ggate, x, normed,
        weight, conv_w, conv_b, x_proj,
    )
    gnormed = Sum(keep, send)
    grad_gain = jnp.sum(weight.astype(F32) * gin, axis=0) / gain_whole[0]
    grad_gain = grad_gain.reshape(2 * shards, gain_len)
    grad_gain = grad_gain + swap_row(grad_gain)
    grad_gain = grad_gain + cross(grad_gain, 1)
    keep = jnp.where(first, gin[:ch], gin[ch:])
    send = jnp.where(first, gin[ch:], gin[:ch])
    in_half = (keep + swap_row(send.astype(BF)).astype(F32)).astype(BF)
    small = jnp.concatenate([gdtproj, misc, stats, cmisc, jnp.transpose(gxproj)])
    small = small + swap_row(small)
    gnormed.first([])
    gnormed.second([in_half, small, grad_gain])
    gnormed = gnormed.third([])
    grad_gain, in_half, out_half = gate([grad_gain, in_half, out_half], [gnormed])
    grad_gain = grad_gain + cross(grad_gain, 2)
    grad_gain = grad_gain + sum(cross_z([grad_gain] * 3))
    out_share = lax.all_to_all(out_half, "seq", split_axis=0, concat_axis=0, tiled=True)
    to_owner = [(b, a) for a, b in to_shard]
    in_share = lax.ppermute(in_half, both, to_owner).astype(F32)
    out_share = jnp.transpose(out_share.astype(F32), (1, 0, 2)).reshape(width // (2 * shards), E)

    residual = hidden_in.astype(F32)
    hidden_out = (residual + mixed).astype(BF)
    inv_rms = lax.rsqrt(jnp.mean(residual * residual, axis=-1, keepdims=True) + eps_norm)
    scaled = residual * inv_rms
    grad_scaled = gnormed * gain_whole
    grad_hidden = grad_out.astype(F32) + inv_rms * (
        grad_scaled - scaled * jnp.mean(grad_scaled * scaled, axis=-1, keepdims=True)
    )
    grad_gain = lax.dynamic_slice(grad_gain, (place, 0), (1, gain_len))[0]
    gdtproj, misc, stats, cmisc, gxproj = jnp.split(
        small, [DT_RANK, DT_RANK + 24, DT_RANK + 32, DT_RANK + 40]
    )
    token_count = full_len * row_count * 2
    mean_off = stats[0] / token_count
    spread = jnp.sqrt(stats[1] / token_count - mean_off * mean_off + eps_spread)
    centre = jnp.log(jax.nn.softplus(dt_bias.astype(F32)))
    return (
        hidden_out,
        grad_hidden,
        grad_gain,
        in_share,
        out_share,
        cmisc[:CONV],
        cmisc[CONV],
        jnp.transpose(gxproj),
        gdtproj,
        misc[NSTATE],
        misc[:NSTATE],
        misc[NSTATE + 1],
        jnp.stack([centre + mean_off, spread]),
    )


block_len = 16


def lagged(values, offset, filler):
    if offset == 0:
        return values
    widths = [(0, 0)] * values.ndim
    widths[1] = (offset, 0)
    return jnp.pad(values, widths, constant_values=filler)[:, : values.shape[1]]


def leading(values, offset):
    if offset == 0:
        return values
    widths = [(0, 0)] * values.ndim
    widths[1] = (0, offset)
    return jnp.pad(values, widths)[:, offset:]


def slope_of_silu(values):
    logistic = jax.nn.sigmoid(values)
    return logistic * (1.0 + values * (1.0 - logistic))


def block_scan(decay_rates, dt_row, x_row, b_row, c_row, keep_row):
    length, channels = dt_row.shape
    blocks = length // block_len

    def regroup(values):
        grouped = values.reshape((blocks, block_len) + values.shape[1:])
        return jnp.moveaxis(grouped, 0, -1)

    dt_q, x_q, b_q, c_q, keep_q = (regroup(v) for v in (dt_row, x_row, b_row, c_row, keep_row))

    def decay_at(dt_now, keep_now):
        return jnp.exp(dt_now[None, :, :] * decay_rates[:, :, None]) * keep_now[None, None, :]

    def local_pass(running, inputs):
        state_now, product = running
        dt_now, x_now, b_now, keep_now = inputs
        decay_now = decay_at(dt_now, keep_now)
        state_now = decay_now * state_now + b_now[:, None, :] * (dt_now * x_now)[None, :, :]
        return ((state_now, decay_now * product), None)

    empty_state = jnp.zeros((NSTATE, channels, blocks), jnp.float32)
    (block_ends, block_decay), _ = lax.scan(
        local_pass, (empty_state, jnp.ones_like(empty_state)), (dt_q, x_q, b_q, keep_q)
    )

    def combine(earlier, later):
        return (earlier[0] * later[0], later[0] * earlier[1] + later[1])

    _, reached = lax.associative_scan(combine, (block_decay, block_ends), axis=2)
    starting = jnp.concatenate([jnp.zeros_like(reached[:, :, :1]), reached[:, :, :-1]], axis=2)

    def full_pass(state_now, inputs):
        dt_now, x_now, b_now, c_now, keep_now = inputs
        state_now = (
            decay_at(dt_now, keep_now) * state_now
            + b_now[:, None, :] * (dt_now * x_now)[None, :, :]
        )
        return (state_now, jnp.sum(c_now[:, None, :] * state_now, axis=0))

    _, outputs = lax.scan(full_pass, starting, (dt_q, x_q, b_q, c_q, keep_q))
    return jnp.moveaxis(outputs, 2, 0).reshape(length, channels)


def scan_all(dt_vals, x_vals, b_vals, c_vals, decay_full, skip_full, keep_mask):
    decay_rates = -jnp.exp(decay_full)
    per_row = jax.checkpoint(block_scan)

    def one_row(row_items):
        return per_row(decay_rates, *row_items)

    outputs = lax.map(one_row, (dt_vals, x_vals, b_vals, c_vals, keep_mask))
    return outputs + skip_full * x_vals


def token_plan(
    hidden_in,
    grad_out,
    doc_starts,
    norm_gain,
    in_proj,
    out_proj,
    conv_weight,
    conv_bias,
    x_proj,
    dt_proj,
    dt_bias,
    decay_log,
    skip_scale,
):
    row_count, seg_len, model_width = hidden_in.shape
    full_len = seg_len * lax.axis_size("seq")
    gain_whole, in_whole, out_whole = (
        lax.all_gather(norm_gain, ("seq", "row"), axis=0, tiled=True),
        lax.all_gather(in_proj, ("seq", "row"), axis=0, tiled=True),
        lax.all_gather(out_proj, ("seq", "row"), axis=0, tiled=True),
    )
    residual = hidden_in.astype(jnp.float32)
    inv_rms = lax.rsqrt(jnp.mean(residual * residual, axis=-1, keepdims=True) + eps_norm)
    scaled = residual * inv_rms
    gain_full = gain_whole.astype(jnp.float32)
    normed = (scaled * gain_full).astype(jnp.bfloat16)
    proj_in = jnp.einsum("rtd,fd->rtf", normed, in_whole, preferred_element_type=jnp.float32)
    x_tokens = proj_in[..., :E].astype(jnp.bfloat16)
    gate_z = proj_in[..., E:]
    x_chan = lax.all_to_all(x_tokens, "seq", split_axis=2, concat_axis=1, tiled=True)
    positions = lax.broadcasted_iota(jnp.int32, (1, full_len, 1), 1)
    doc_ids = jnp.sum((doc_starts[:, None, :] <= positions).astype(jnp.int32), axis=2) - 1
    same_docs = [
        (lagged(doc_ids, offset, -1) == doc_ids).astype(jnp.float32)[..., None]
        for offset in range(CONV)
    ]
    keep_mask = same_docs[1][..., 0]
    x_vals = x_chan.astype(jnp.float32)
    conv_full = conv_weight.astype(jnp.float32)
    pre_conv = conv_bias.astype(jnp.float32) + jnp.zeros_like(x_vals)
    for offset in range(CONV):
        pre_conv = (
            pre_conv
            + conv_full[CONV - 1 - offset] * lagged(x_vals, offset, 0.0) * same_docs[offset]
        )
    conv_low = jax.nn.silu(pre_conv).astype(jnp.bfloat16)
    part_sums = jnp.einsum("rtc,cm->rtm", conv_low, x_proj, preferred_element_type=jnp.float32)
    dtbc = lax.psum(part_sums, "seq").astype(jnp.bfloat16)
    dt_low = dtbc[..., :DT_RANK]
    b_vals = dtbc[..., DT_RANK : DT_RANK + NSTATE].astype(jnp.float32)
    c_vals = dtbc[..., DT_RANK + NSTATE :].astype(jnp.float32)
    pre_dt = jnp.einsum(
        "rtk,kc->rtc", dt_low, dt_proj, preferred_element_type=jnp.float32
    ) + dt_bias.astype(jnp.float32)
    dt_vals = jax.nn.softplus(pre_dt)
    y_vals, pullback = jax.vjp(
        partial(scan_all, keep_mask=keep_mask),
        dt_vals,
        conv_low.astype(jnp.float32),
        b_vals,
        c_vals,
        decay_log.astype(jnp.float32),
        skip_scale.astype(jnp.float32),
    )
    y_tokens = lax.all_to_all(
        y_vals.astype(jnp.bfloat16), "seq", split_axis=1, concat_axis=2, tiled=True
    )
    y_token_vals = y_tokens.astype(jnp.float32)
    gate_act = jax.nn.silu(gate_z)
    gated = (y_token_vals * gate_act).astype(jnp.bfloat16)
    mixed = jnp.einsum("rte,de->rtd", gated, out_whole, preferred_element_type=jnp.float32)
    hidden_out = (residual + mixed).astype(jnp.bfloat16)
    grad_out_proj = jnp.einsum("rtd,rte->de", grad_out, gated, preferred_element_type=jnp.float32)
    grad_gated = jnp.einsum("rtd,de->rte", grad_out, out_whole, preferred_element_type=jnp.float32)
    grad_y = (grad_gated * gate_act).astype(jnp.bfloat16)
    grad_gate = (grad_gated * y_token_vals * slope_of_silu(gate_z)).astype(jnp.bfloat16)
    grad_y_chan = lax.all_to_all(grad_y, "seq", split_axis=2, concat_axis=1, tiled=True)
    grad_dt_scan, grad_x_scan, grad_b, grad_c, grad_decay, grad_skip = pullback(
        grad_y_chan.astype(jnp.float32)
    )
    grad_pre_dt = (grad_dt_scan * jax.nn.sigmoid(pre_dt)).astype(jnp.bfloat16)
    grad_dt_low = jnp.einsum(
        "rtc,kc->rtk", grad_pre_dt, dt_proj, preferred_element_type=jnp.float32
    )
    grad_dt_proj = jnp.einsum(
        "rtk,rtc->kc", dt_low, grad_pre_dt, preferred_element_type=jnp.float32
    )
    grad_dt_bias = jnp.sum(grad_pre_dt.astype(jnp.float32), axis=(0, 1))
    grad_parts = jnp.concatenate([grad_dt_low, grad_b, grad_c], axis=-1)
    grad_share = lax.psum_scatter(grad_parts, "seq", scatter_dimension=1, tiled=True)
    grad_dtbc = lax.all_gather(grad_share.astype(jnp.bfloat16), "seq", axis=1, tiled=True)
    grad_x_proj = jnp.einsum("rtc,rtm->cm", conv_low, grad_dtbc, preferred_element_type=jnp.float32)
    grad_conv_out = grad_x_scan + jnp.einsum(
        "rtm,cm->rtc", grad_dtbc, x_proj, preferred_element_type=jnp.float32
    )
    grad_pre_conv = grad_conv_out * slope_of_silu(pre_conv)
    grad_conv_bias = jnp.sum(grad_pre_conv, axis=(0, 1))
    conv_rows = [None] * CONV
    grad_x = jnp.zeros_like(grad_pre_conv)
    for offset in range(CONV):
        masked = grad_pre_conv * same_docs[offset]
        conv_rows[CONV - 1 - offset] = jnp.sum(masked * lagged(x_vals, offset, 0.0), axis=(0, 1))
        grad_x = grad_x + conv_full[CONV - 1 - offset] * leading(masked, offset)
    grad_conv_weight = jnp.stack(conv_rows)
    grad_x_tokens = lax.all_to_all(
        grad_x.astype(jnp.bfloat16), "seq", split_axis=1, concat_axis=2, tiled=True
    )
    grad_proj = jnp.concatenate([grad_x_tokens, grad_gate], axis=-1)
    grad_in_proj = jnp.einsum("rtf,rtd->fd", grad_proj, normed, preferred_element_type=jnp.float32)
    grad_normed = jnp.einsum("rtf,fd->rtd", grad_proj, in_whole, preferred_element_type=jnp.float32)
    grad_gain = jnp.sum(grad_normed * scaled, axis=(0, 1))
    grad_scaled = grad_normed * gain_full
    grad_hidden = grad_out.astype(jnp.float32) + inv_rms * (
        grad_scaled - scaled * jnp.mean(grad_scaled * scaled, axis=-1, keepdims=True)
    )
    gain_share, in_share, out_share = (
        lax.psum_scatter(grad_gain, ("seq", "row"), scatter_dimension=0, tiled=True),
        lax.psum_scatter(grad_in_proj, ("seq", "row"), scatter_dimension=0, tiled=True),
        lax.psum_scatter(grad_out_proj, ("seq", "row"), scatter_dimension=0, tiled=True),
    )
    centre = jnp.log(jax.nn.softplus(dt_bias.astype(jnp.float32)))
    offset_dt = jnp.log(dt_vals) - centre
    first_sum = jnp.sum(offset_dt, axis=(0, 1))
    second_sum = jnp.sum(offset_dt * offset_dt, axis=(0, 1))
    summed = lax.psum(
        (
            grad_conv_weight,
            grad_conv_bias,
            grad_x_proj,
            grad_dt_proj,
            grad_dt_bias,
            grad_decay,
            grad_skip,
            first_sum,
            second_sum,
        ),
        "row",
    )
    token_count = full_len * row_count * lax.axis_size("row")
    mean_off = summed[7] / token_count
    spread = jnp.sqrt(summed[8] / token_count - mean_off * mean_off + eps_spread)
    dt_stats = jnp.stack([centre + mean_off, spread])
    return (
        hidden_out,
        grad_hidden,
        gain_share,
        in_share,
        out_share,
        summed[0],
        summed[1],
        summed[2],
        summed[3],
        summed[4],
        summed[5],
        summed[6],
        dt_stats,
    )


def solution(mesh):
    fits = mesh.shape["seq"] == 16 and mesh.shape["row"] == 2
    plan = channel_plan if fits else token_plan
    return jax.shard_map(
        plan,
        mesh=mesh,
        in_specs=(
            P("row", "seq", None),
            P("row", "seq", None),
            P("row", None),
            P(("seq", "row")),
            P(("seq", "row"), None),
            P(("seq", "row"), None),
            P(None, "seq"),
            P("seq"),
            P("seq", None),
            P(None, "seq"),
            P("seq"),
            P(None, "seq"),
            P("seq"),
        ),
        out_specs=(
            P("row", "seq", None),
            P("row", "seq", None),
            P(("seq", "row")),
            P(("seq", "row"), None),
            P(("seq", "row"), None),
            P(None, "seq"),
            P("seq"),
            P("seq", None),
            P(None, "seq"),
            P("seq"),
            P(None, "seq"),
            P("seq"),
            P(None, "seq"),
        ),
        check_vma=False,
    )
```

```python
from functools import partial

import jax
import jax.numpy as jnp
from jax import lax
from jax.experimental import pallas as pl
from jax.experimental.pallas import tpu as pltpu
from jax.sharding import PartitionSpec as P

E = 2048
NSTATE = 16
CONV = 4
DT_RANK = 64
MAPS = DT_RANK + 2 * NSTATE

eps_norm = 1e-05
eps_spread = 1e-06
BF = jnp.bfloat16
F32 = jnp.float32
LOG2E = 1.4426950408889634
FAR = 1e4
LANES = 128
VMEM = 28 << 20


def params(dims=2):
    return pltpu.CompilerParams(
        dimension_semantics=("arbitrary",) * dims, vmem_limit_bytes=VMEM
    )


def place_in_doc(starts_ref, row, first, count):
    pos = lax.broadcasted_iota(jnp.int32, (count, LANES), 0) + first
    base = jnp.zeros_like(pos)
    for j in range(1, starts_ref.shape[1]):
        start = starts_ref[row, j]
        base = jnp.where(pos >= start, start, base)
    return pos - base


def large(shape, dtype):
    return pltpu.HBM(shape, dtype)


def still(*values):
    return [pltpu.with_memory_space_constraint(v, pltpu.HBM) for v in values]


def sigmoid(v):
    return 1.0 / (1.0 + jnp.exp2(v * -LOG2E))


def silu_slope(v):
    s = sigmoid(v)
    return s * (1.0 + v * (1.0 - s))


def softplus(v):
    return jnp.maximum(v, 0.0) + jnp.log1p(jnp.exp2(jnp.abs(v) * -LOG2E))


def dot(a, b, dims):
    return lax.dot_general(a, b, (dims, ((), ())), preferred_element_type=F32)


def own_place():
    s = lax.axis_index("seq")
    return jnp.stack([s // 4, s // 2 % 2, s % 2]).astype(jnp.int32)


def gate_kernel(*refs):
    pass


def gate(values, others):
    place = pl.BlockSpec(memory_space=pl.ANY)
    return pl.pallas_call(
        gate_kernel,
        in_specs=[place] * (len(values) + len(others)),
        out_specs=[place] * len(values),
        out_shape=[jax.ShapeDtypeStruct(v.shape, v.dtype) for v in values],
        input_output_aliases={i: i for i in range(len(values))},
        compiler_params=pltpu.CompilerParams(vmem_limit_bytes=1 << 16),
        cost_estimate=pl.CostEstimate(flops=1, bytes_accessed=1, transcendentals=0),
        name="gate",
    )(*values, *others)


def put_pieces(own, value, keep, send):
    rows, seg = keep.shape[2], keep.shape[3]
    first = own[2] == 0
    for r in range(rows):
        for x in range(2):
            at = (r * 4 + 2 * x) * seg
            even, odd = value[at : at + seg], value[at + seg : at + 2 * seg]
            keep[x ^ own[1], 0, r] = jnp.where(first, even, odd).astype(keep.dtype)
            send[x ^ own[1], 0, r] = jnp.where(first, odd, even).astype(send.dtype)


def take_pieces(own, near, far, out):
    rows, seg = near.shape[2], near.shape[3]
    first = own[2] == 0
    for r in range(rows):
        for x in range(2):
            at = (r * 4 + 2 * x) * seg
            a = near[x ^ own[1], 0, r].astype(F32)
            b = far[x ^ own[1], 0, r].astype(F32)
            out[at : at + seg, :] = jnp.where(first, a, b)
            out[at + seg : at + 2 * seg, :] = jnp.where(first, b, a)


def pieces_spec(rows, seg, n, at):
    return pl.BlockSpec((2, 1, rows, seg, n), lambda c, s, o: (0, at(c) ^ o[0], 0, 0, 0))


def fixed_block(shape):
    return pl.BlockSpec(shape, lambda c, s, o: (0,) * len(shape))


def front_kernel(
    starts, own, hid, gain, weight, conv_w, conv_b, xproj,
    normed_o, x_o, z_o, conv_o, keep_o, send_o,
    xs,
):
    c = pl.program_id(0)
    rows, t, ch = x_o.shape
    width = normed_o.shape[2]

    @pl.when(c == 0)
    def _():
        xs[:, 0:8, :] = jnp.zeros((rows, 8, ch), F32)

    @pl.when(c > 0)
    def _():
        xs[:, 0:8, :] = xs[:, t : t + 8, :]

    res = hid[...].reshape(rows * t, width).astype(F32)
    inv = lax.rsqrt(jnp.mean(res * res, axis=-1, keepdims=True) + eps_norm)
    normed = (res * inv * gain[...]).astype(BF)
    normed_o[...] = normed.reshape(rows, t, width)
    proj = dot(normed, weight[...], ((1,), (1,)))
    z_o[...] = proj[:, ch:].reshape(rows, t, ch)
    x_low = proj[:, :ch].astype(BF).reshape(rows, t, ch)
    x_o[...] = x_low
    xs[:, 8 : 8 + t, :] = x_low.astype(F32)
    for r in range(rows):
        place = place_in_doc(starts, r, c * t, t)
        pre = conv_b[...] + conv_w[CONV - 1 : CONV, :] * xs[r, 8 : 8 + t, :]
        for k in range(1, CONV):
            lag = conv_w[CONV - 1 - k : CONV - k, :] * xs[r, 8 - k : 8 - k + t, :]
            pre = pre + jnp.where(place >= k, lag, 0.0)
        conv_o[r] = (pre * sigmoid(pre)).astype(BF)
    conv = conv_o[...].reshape(rows * t, ch)
    put_pieces(own, dot(conv, xproj[...], ((1,), (0,))), keep_o, send_o)


def front(starts, own, hid, gain, weight, conv_w, conv_b, xproj):
    (hid,) = still(hid)
    rows, length, width = hid.shape
    ch = conv_w.shape[1]
    t = length // 4
    seg = t // 4
    tok = lambda n: pl.BlockSpec((rows, t, n), lambda c, s, o: (0, c, 0))
    piece = pieces_spec(rows, seg, MAPS, lambda c: c)
    return pl.pallas_call(
        front_kernel,
        grid_spec=pltpu.PrefetchScalarGridSpec(
            num_scalar_prefetch=2,
            grid=(length // t,),
            in_specs=[
                tok(width),
                fixed_block(gain.shape),
                fixed_block(weight.shape),
                fixed_block(conv_w.shape),
                fixed_block(conv_b.shape),
                fixed_block(xproj.shape),
            ],
            out_specs=[tok(width), tok(ch), tok(ch), tok(ch), piece, piece],
            scratch_shapes=[pltpu.VMEM((rows, t + 8, ch), F32)],
        ),
        out_shape=[
            large((rows, length, width), BF),
            large((rows, length, ch), BF),
            large((rows, length, ch), F32),
            large((rows, length, ch), BF),
            jax.ShapeDtypeStruct((2, 4, rows, seg, MAPS), F32),
            jax.ShapeDtypeStruct((2, 4, rows, seg, MAPS), F32),
        ],
        compiler_params=params(1),
        cost_estimate=pl.CostEstimate(flops=1, bytes_accessed=1, transcendentals=0),
        name="front",
    )(starts, own, hid, gain, weight, conv_w, conv_b, xproj)


def maps_across(low):
    pick = lax.broadcasted_iota(jnp.int32, (2 * NSTATE, MAPS), 0) + DT_RANK
    pick = (pick == lax.broadcasted_iota(jnp.int32, (2 * NSTATE, MAPS), 1)).astype(BF)
    return dot(pick, low, ((1,), (1,)))


def half_spec(rows, seg, n, at):
    return pl.BlockSpec(
        (1, 1, rows, seg, n),
        lambda c, s, o: (at(c) % 2 ^ o[1], at(c) // 2 ^ o[0], 0, 0, 0),
    )


def put_halves(own, value, keep, send):
    rows, seg = keep.shape[2], keep.shape[3]
    first = own[2] == 0
    for r in range(rows):
        even = value[2 * r * seg : (2 * r + 1) * seg]
        odd = value[(2 * r + 1) * seg : (2 * r + 2) * seg]
        keep[0, 0, r] = jnp.where(first, even, odd).astype(keep.dtype)
        send[0, 0, r] = jnp.where(first, odd, even).astype(send.dtype)


def take_halves(own, near, far, out):
    rows, seg = near.shape[2], near.shape[3]
    first = own[2] == 0
    for r in range(rows):
        a = near[0, 0, r].astype(F32)
        b = far[0, 0, r].astype(F32)
        out[2 * r * seg : (2 * r + 1) * seg, :] = jnp.where(first, a, b)
        out[(2 * r + 1) * seg : (2 * r + 2) * seg, :] = jnp.where(first, b, a)


def fold(parts):
    row = lax.broadcasted_iota(jnp.int32, parts[0].shape, 0)
    upper = row < 4
    parts = [
        jnp.where(upper, a, b) + pltpu.roll(jnp.where(upper, b, a), 4, 0)
        for a, b in zip(parts[:4], parts[4:])
    ]
    for step in (2, 1):
        half = len(parts) // 2
        upper = row & step == 0
        parts = [
            jnp.where(upper, a + pltpu.roll(a, 8 - step, 0), b + pltpu.roll(b, step, 0))
            for a, b in zip(parts[:half], parts[half:])
        ]
    return parts[0]


def spread_maps(low, first, out):
    count, ch = low.shape[0], out.shape[1]
    pick = lax.broadcasted_iota(jnp.int32, (MAPS, NSTATE * ch), 1) // ch + first
    pick = (pick == lax.broadcasted_iota(jnp.int32, (MAPS, NSTATE * ch), 0)).astype(BF)
    wide = dot(low, pick, ((1,), (0,)))
    for b in range(count // 8):
        for n in range(NSTATE):
            row = (b * NSTATE + n) * 8
            out[row : row + 8, :] = wide[b * 8 : b * 8 + 8, n * ch : (n + 1) * ch]


def forward_kernel(starts, own, near, far, dtproj, dtbias, decay, skip, conv, z, *refs):
    (
        gated_o, y_o, states_o, last_o, stats_o,
        state, dtk_s, dtx_s, y_s, across_s, low_s, cm_s,
    ) = refs[-12:]
    c = pl.program_id(0)
    rows, t, ch = conv.shape

    @pl.when(c == 0)
    def _():
        state[...] = jnp.zeros_like(state)
        stats_o[...] = jnp.zeros_like(stats_o)

    rate = -LOG2E * jnp.exp(decay[...])
    take_halves(own, near, far, low_s)
    low = low_s[...].astype(BF)
    dt = softplus(dot(low[:, :DT_RANK], dtproj[...], ((1,), (0,))) + dtbias[...])
    off = jnp.log(dt) - jnp.log(softplus(dtbias[...]))
    stats_o[0:1, :] += jnp.sum(off, axis=0, keepdims=True)
    stats_o[1:2, :] += jnp.sum(off * off, axis=0, keepdims=True)
    x = conv[...].astype(F32).reshape(rows * t, ch)
    for r in range(rows):
        place = place_in_doc(starts, r, c * t, t)
        dtk_s[r * t : (r + 1) * t, :] = jnp.where(place >= 1, dt[r * t : (r + 1) * t], FAR)
    dtx_s[...] = dt * x
    across_s[...] = maps_across(low)
    spread_maps(low, DT_RANK + NSTATE, cm_s)

    def every_step(states):
        states, sums = list(states), [None] * rows
        maps = [across_s[:, r * t : (r + 1) * t] for r in range(rows)]
        for i in range(t):
            for r in range(rows):
                if i % 8 == 0:
                    sums[r] = []
                at = r * t + i
                s = states[r]
                a = jnp.exp2(dtk_s[pl.ds(at, 1), :] * rate)
                states_o[r, i] = s
                b = jnp.broadcast_to(maps[r][:NSTATE, i : i + 1], (NSTATE, ch))
                s = a * s + dtx_s[pl.ds(at, 1), :] * b
                ys = s * cm_s[pl.ds(at // 8 * 8 * NSTATE + at % 8, NSTATE, stride=8), :]
                sums[r].append(ys[:8] + ys[8:])
                if i % 8 == 7:
                    y_s[pl.ds(r * t + i - 7, 8), :] = fold(sums[r])
                states[r] = s
        return tuple(states)

    states = every_step(tuple(state[r] for r in range(rows)))
    for r in range(rows):
        state[r] = states[r]
        last_o[r] = states[r]
    y_low = (y_s[...] + skip[...] * x).astype(BF)
    y_o[...] = y_low.reshape(rows, t, ch)
    zz = z[...].reshape(rows * t, ch)
    gated_o[...] = (y_low.astype(F32) * (zz * sigmoid(zz))).astype(BF).reshape(rows, t, ch)


def forward_scan(after, starts, own, near, far, dtproj, dtbias, decay, skip, conv, z):
    conv, z = still(conv, z)
    rows, length, ch = conv.shape
    t = length // 8
    seg = t // 2
    tok = lambda n: pl.BlockSpec((rows, t, n), lambda c, s, o: (0, c, 0))
    half = half_spec(rows, seg, MAPS, lambda c: c)
    return pl.pallas_call(
        forward_kernel,
        grid_spec=pltpu.PrefetchScalarGridSpec(
            num_scalar_prefetch=2,
            grid=(length // t,),
            in_specs=[
                half,
                half,
                fixed_block(dtproj.shape),
                fixed_block(dtbias.shape),
                fixed_block(decay.shape),
                fixed_block(skip.shape),
                tok(ch),
                tok(ch),
                *[pl.BlockSpec(memory_space=pl.ANY)] * len(after),
            ],
            out_specs=[
                tok(ch),
                tok(ch),
                pl.BlockSpec((rows, t, NSTATE, ch), lambda c, s, o: (0, c, 0, 0)),
                fixed_block((rows, NSTATE, ch)),
                fixed_block((8, ch)),
            ],
            scratch_shapes=[
                pltpu.VMEM((rows, NSTATE, ch), F32),
                pltpu.VMEM((rows * t, ch), F32),
                pltpu.VMEM((rows * t, ch), F32),
                pltpu.VMEM((rows * t, ch), F32),
                pltpu.VMEM((2 * NSTATE, rows * t), F32),
                pltpu.VMEM((rows * t, MAPS), F32),
                pltpu.VMEM((rows * t * NSTATE, ch), F32),
            ],
        ),
        out_shape=[
            large((rows, length, ch), BF),
            large((rows, length, ch), BF),
            large((rows, length, NSTATE, ch), F32),
            jax.ShapeDtypeStruct((rows, NSTATE, ch), F32),
            jax.ShapeDtypeStruct((8, ch), F32),
        ],
        compiler_params=params(1),
        cost_estimate=pl.CostEstimate(flops=1, bytes_accessed=1, transcendentals=0),
        name="forward_scan",
    )(starts, own, near, far, dtproj, dtbias, decay, skip, conv, z, *after)


def backward_kernel(
    starts, own, near, far, dtproj, dtbias, decay, skip, conv, z, y, gg, states, wide,
    gdtproj_i, misc_i, back_i, next_i, *refs, top,
):
    (
        ggate_o, gxs_o, keep_o, send_o, gdtproj_o, misc_o, back_o, next_o,
        dtk_s, dt_s, dtx_s, gy_s, p1_s, p2_s, gb_s, gc_s, fold_s, across_s, low_s,
    ) = refs[-19:]
    c = pl.program_id(0)
    rows, t, ch = conv.shape
    count = rows * t

    @pl.when(c == 0)
    def _():
        back_o[...] = back_i[...]
        next_o[...] = next_i[...]
        gdtproj_o[...] = gdtproj_i[...]
        misc_o[...] = misc_i[...]

    neg = -jnp.exp(decay[...])
    rate = LOG2E * neg
    take_halves(own, near, far, low_s)
    low = low_s[...].astype(BF)
    pre = dot(low[:, :DT_RANK], dtproj[...], ((1,), (0,))) + dtbias[...]
    dt = softplus(pre)
    x = conv[...].astype(F32).reshape(count, ch)
    for r in range(rows):
        place = place_in_doc(starts, r, (top - c) * t, t)
        dtk_s[r * t : (r + 1) * t, :] = jnp.where(place >= 1, dt[r * t : (r + 1) * t], FAR)
    dt_s[...] = dt
    dtx_s[...] = dt * x
    zz = z[...].reshape(count, ch)
    ggv = gg[...].reshape(count, ch)
    sg = sigmoid(zz)
    gy = (ggv * (zz * sg)).astype(BF).astype(F32)
    yv = y[...].astype(F32).reshape(count, ch)
    ggate = (ggv * yv * (sg * (1.0 + zz * (1.0 - sg)))).astype(BF)
    ggate_o[...] = ggate.reshape(rows, t, ch)
    gy_s[...] = gy
    across_s[...] = maps_across(low)

    def every_step(carry):
        hs, s_nexts, acc = list(carry[0]), list(carry[1]), carry[2]
        p1s, p2s = [None] * rows, [None] * rows
        maps = [across_s[:, r * t : (r + 1) * t] for r in range(rows)]
        for i in range(t - 1, -1, -1):
            for r in range(rows):
                at = r * t + i
                gyr = gy_s[pl.ds(at, 1), :]
                g = gyr * jnp.broadcast_to(maps[r][NSTATE:, i : i + 1], (NSTATE, ch)) + hs[r]
                h = jnp.exp2(dtk_s[pl.ds(at, 1), :] * rate) * g
                s_prev = states[r, i]
                q = h * s_prev
                acc = acc + q * dt_s[pl.ds(at, 1), :]
                aq = q * neg
                bg = g * jnp.broadcast_to(maps[r][:NSTATE, i : i + 1], (NSTATE, ch))
                if i % 8 == 7:
                    p1s[r], p2s[r] = [], []
                p1s[r].insert(0, bg[:8] + bg[8:])
                p2s[r].insert(0, aq[:8] + aq[8:])
                if i % 8 == 0:
                    whole8 = pl.ds(at, 8)
                    p1_s[whole8, :] = fold(p1s[r])
                    p2_s[whole8, :] = fold(p2s[r])
                tile = pl.ds(at * NSTATE, NSTATE)
                gb_s[tile, :] = (g * dtx_s[pl.ds(at, 1), :]).astype(BF)
                gc_s[tile, :] = (gyr * s_nexts[r]).astype(BF)
                hs[r], s_nexts[r] = h, s_prev
        return tuple(hs), tuple(s_nexts), acc

    hs, s_nexts, acc = every_step(
        (
            tuple(back_o[r] for r in range(rows)),
            tuple(next_o[r] for r in range(rows)),
            jnp.zeros((NSTATE, ch), F32),
        ),
    )
    for r in range(rows):
        back_o[r] = hs[r]
        next_o[r] = s_nexts[r]
    p1, p2 = p1_s[...], p2_s[...]
    gxs_o[...] = (dt * p1 + skip[...] * gy).reshape(rows, t, ch)
    gpre = ((p2 + x * p1) * sigmoid(pre)).astype(BF)
    gdtproj_o[...] += dot(low[:, :DT_RANK], gpre, ((0,), (0,)))
    misc_o[0:NSTATE, :] += neg * acc
    misc_o[NSTATE : NSTATE + 1, :] += jnp.sum(gpre.astype(F32), axis=0, keepdims=True)
    misc_o[NSTATE + 1 : NSTATE + 2, :] += jnp.sum(gy * x, axis=0, keepdims=True)
    ones = jnp.ones((ch, ch), BF)
    entry = lax.broadcasted_iota(jnp.int32, (1, NSTATE, ch), 1) + DT_RANK
    lane = lax.broadcasted_iota(jnp.int32, (1, NSTATE, ch), 2)
    maps = jnp.zeros((count, NSTATE, ch), F32)
    for ref in (gb_s, gc_s):
        every = dot(ref[...], ones, ((1,), (0,))).reshape(count, NSTATE, ch)
        maps = jnp.where(lane == entry, every, maps)
        entry = entry + NSTATE
    fold_s[...] = (maps[:, :8] + maps[:, 8:]).reshape(count * 8, ch)
    total = dot(gpre, wide[...], ((1,), (0,)))
    for j in range(8):
        total = total + fold_s[pl.ds(j, count, stride=8), :][:, :MAPS]
    put_halves(own, total, keep_o, send_o)


def widened(dtproj):
    return jnp.pad(dtproj.T, ((0, 0), (0, 2 * NSTATE)))


def backward_scan(
    top, chunks, after, so_far, starts, own, near, far, dtproj, dtbias, decay, skip, conv, z, y,
    gg, states, wide,
):
    conv, z, y, gg, states = still(conv, z, y, gg, states)
    rows, length, ch = conv.shape
    t = length // 8
    seg = t // 2
    done, passed = so_far
    fixed = 18
    tok = lambda n: pl.BlockSpec((rows, t, n), lambda c, s, o: (0, top - c, 0))
    half = half_spec(rows, seg, MAPS, lambda c: top - c)
    small = [(DT_RANK, ch), (24, ch), (rows, NSTATE, ch), (rows, NSTATE, ch)]
    return pl.pallas_call(
        partial(backward_kernel, top=top),
        grid_spec=pltpu.PrefetchScalarGridSpec(
            num_scalar_prefetch=2,
            grid=(chunks,),
            in_specs=[
                half,
                half,
                fixed_block(dtproj.shape),
                fixed_block(dtbias.shape),
                fixed_block(decay.shape),
                fixed_block(skip.shape),
                tok(ch),
                tok(ch),
                tok(ch),
                tok(ch),
                pl.BlockSpec((rows, t, NSTATE, ch), lambda c, s, o: (0, top - c, 0, 0)),
                fixed_block(wide.shape),
                *[fixed_block(s) for s in small],
                *[pl.BlockSpec(memory_space=pl.ANY)] * (len(done) + len(after)),
            ],
            out_specs=[tok(ch), tok(ch), half, half, *[fixed_block(s) for s in small]],
            scratch_shapes=[
                pltpu.VMEM((rows * t, ch), F32),
                pltpu.VMEM((rows * t, ch), F32),
                pltpu.VMEM((rows * t, ch), F32),
                pltpu.VMEM((rows * t, ch), F32),
                pltpu.VMEM((rows * t, ch), F32),
                pltpu.VMEM((rows * t, ch), F32),
                pltpu.VMEM((rows * t * NSTATE, ch), BF),
                pltpu.VMEM((rows * t * NSTATE, ch), BF),
                pltpu.VMEM((rows * t * 8, ch), F32),
                pltpu.VMEM((2 * NSTATE, rows * t), F32),
                pltpu.VMEM((rows * t, MAPS), F32),
            ],
        ),
        out_shape=[
            large((rows, length, ch), BF),
            large((rows, length, ch), F32),
            jax.ShapeDtypeStruct((2, 4, rows, seg, MAPS), F32),
            jax.ShapeDtypeStruct((2, 4, rows, seg, MAPS), F32),
            *[jax.ShapeDtypeStruct(s, F32) for s in small],
        ],
        input_output_aliases={fixed + i: i for i in range(len(done))},
        compiler_params=params(1),
        cost_estimate=pl.CostEstimate(flops=1, bytes_accessed=1, transcendentals=0),
        name="backward_scan",
    )(
        starts, own, near, far, dtproj, dtbias, decay, skip, conv, z, y, gg, states, wide,
        *passed, *done, *after,
    )


def tail_kernel(
    starts, own, near, far, conv, gxs, ggate, x, before, normed, weight, conv_w, conv_b, xproj, *refs
):
    keep_o, send_o, gin_o, gxproj_o, misc_o, xs, gm_s, low_s, gx_s = refs[-9:]
    c = pl.program_id(0)
    chunks = pl.num_programs(0)
    rows, t, ch = conv.shape
    count = rows * t

    @pl.when(c == 0)
    def _():
        gin_o[...] = jnp.zeros_like(gin_o)
        gxproj_o[...] = jnp.zeros_like(gxproj_o)
        misc_o[...] = jnp.zeros_like(misc_o)
        gm_s[:, :, t : t + 8, :] = jnp.zeros((CONV - 1, rows, 8, ch), F32)

    @pl.when(c > 0)
    def _():
        gm_s[:, :, t : t + 8, :] = gm_s[:, :, 0:8, :]

    xs[:, 0:16, :] = before[...].astype(F32)
    xs[:, 16 : 16 + t, :] = x[...].astype(F32)
    take_pieces(own, near, far, low_s)
    low = low_s[...].astype(BF)
    gconv = gxs[...].reshape(count, ch) + dot(low, xproj[...], ((1,), (1,)))
    gxproj_o[...] += dot(conv[...].reshape(count, ch), low, ((0,), (0,)))
    for r in range(rows):
        place = place_in_doc(starts, r, (chunks - 1 - c) * t, t)
        lags = [xs[r, 16 : 16 + t, :]]
        pre = conv_b[...] + conv_w[CONV - 1 : CONV, :] * lags[0]
        for k in range(1, CONV):
            lags.append(jnp.where(place >= k, xs[r, 16 - k : 16 - k + t, :], 0.0))
            pre = pre + conv_w[CONV - 1 - k : CONV - k, :] * lags[k]
        gpre = gconv[r * t : (r + 1) * t] * silu_slope(pre)
        gx = conv_w[CONV - 1 : CONV, :] * gpre
        for k in range(CONV):
            misc_o[CONV - 1 - k : CONV - k, :] += jnp.sum(gpre * lags[k], axis=0, keepdims=True)
            if k:
                gm_s[k - 1, r, 0:t, :] = jnp.where(place >= k, gpre, 0.0)
                gx = gx + conv_w[CONV - 1 - k : CONV - k, :] * gm_s[k - 1, r, k : k + t, :]
        misc_o[CONV : CONV + 1, :] += jnp.sum(gpre, axis=0, keepdims=True)
        gx_s[r * t : (r + 1) * t, :] = gx.astype(BF)
    gproj = jnp.concatenate([gx_s[...], ggate[...].reshape(count, ch)], axis=1)
    gin_o[...] += dot(gproj, normed[...].reshape(count, normed.shape[2]), ((0,), (0,)))
    put_pieces(own, dot(gproj, weight[...], ((1,), (0,))), keep_o, send_o)


def tail(after, starts, own, near, far, conv, gxs, ggate, x, normed, weight, conv_w, conv_b, xproj):
    conv, gxs, ggate, x, normed = still(conv, gxs, ggate, x, normed)
    rows, length, width = normed.shape
    ch = conv.shape[2]
    t = length // 4
    seg = t // 4
    last = length // t - 1
    tok = lambda n: pl.BlockSpec((rows, t, n), lambda c, s, o: (0, last - c, 0))
    piece = lambda n: pieces_spec(rows, seg, n, lambda c: last - c)
    before = pl.BlockSpec(
        (rows, 16, ch), lambda c, s, o: (0, jnp.maximum((last - c) * (t // 16) - 1, 0), 0)
    )
    return pl.pallas_call(
        tail_kernel,
        grid_spec=pltpu.PrefetchScalarGridSpec(
            num_scalar_prefetch=2,
            grid=(length // t,),
            in_specs=[
                piece(MAPS),
                piece(MAPS),
                tok(ch),
                tok(ch),
                tok(ch),
                tok(ch),
                before,
                tok(width),
                fixed_block(weight.shape),
                fixed_block(conv_w.shape),
                fixed_block(conv_b.shape),
                fixed_block(xproj.shape),
                *[pl.BlockSpec(memory_space=pl.ANY)] * len(after),
            ],
            out_specs=[
                piece(width),
                piece(width),
                fixed_block(weight.shape),
                fixed_block((ch, MAPS)),
                fixed_block((8, ch)),
            ],
            scratch_shapes=[
                pltpu.VMEM((rows, t + 16, ch), F32),
                pltpu.VMEM((CONV - 1, rows, t + 8, ch), F32),
                pltpu.VMEM((rows * t, MAPS), F32),
                pltpu.VMEM((rows * t, ch), BF),
            ],
        ),
        out_shape=[
            large((2, 4, rows, seg, width), BF),
            large((2, 4, rows, seg, width), BF),
            jax.ShapeDtypeStruct(weight.shape, F32),
            jax.ShapeDtypeStruct((ch, MAPS), F32),
            jax.ShapeDtypeStruct((8, ch), F32),
        ],
        compiler_params=params(1),
        cost_estimate=pl.CostEstimate(flops=1, bytes_accessed=1, transcendentals=0),
        name="tail",
    )(starts, own, near, far, conv, gxs, ggate, x, x, normed, weight, conv_w, conv_b, xproj, *after)


def cross(v, bits):
    return lax.ppermute(v, "seq", [(s, s ^ bits) for s in range(16)])


def swap_row(v):
    return lax.ppermute(v, "row", [(0, 1), (1, 0)])


def total_of_all(v):
    v = v + swap_row(v)
    for bits in (1, 2, 4, 8):
        v = v + cross(v, bits)
    return v


def sum_pieces(keep, send, sent, others):
    (acc,) = gate([keep.astype(F32) + cross(send, 1).astype(F32)], others)
    acc = acc[0] + cross(acc[1].astype(sent), 2).astype(F32)
    total = acc[0]
    for k in (1, 2, 3):
        total = total + cross(acc[k].astype(sent), 4 * k).astype(F32)
    return total


def spread_pieces(own_piece):
    line = jnp.stack([own_piece] + [cross(own_piece, 4 * k) for k in (1, 2, 3)])
    near = jnp.stack([line, cross(line, 2)])
    return near, cross(near, 1)


def gather_tokens(v):
    return lax.all_gather(v, "seq", axis=1, tiled=True)


def up(v):
    return v.astype(F32)


class Sum:
    def __init__(self, keep, send):
        self.keep, self.near = keep, cross(send, 1)
        self.head = keep.shape[2] - keep.shape[2] // 3

    def part(self, *at):
        return up(self.keep[at]) + up(self.near[at])

    def first(self, others):
        (self.near,) = gate([self.near], others)
        a, b = slice(0, self.head), slice(self.head, None)
        sent = [self.part(1, slice(None), a).astype(BF)]
        sent += [self.part(slice(None), k, b).astype(BF) for k in (1, 2, 3)]
        self.second_of = [cross(sent[0], 2), *cross_z(sent[1:])]
        return sent

    def second(self, others):
        across, *line = gate(self.second_of, others)
        a, b = slice(0, self.head), slice(self.head, None)
        sent = [(self.part(0, k, a) + up(across[k])).astype(BF) for k in (1, 2, 3)]
        sent.append((self.part(1, 0, b) + sum(up(v[1]) for v in line)).astype(BF))
        self.third_of = [*cross_z(sent[:3]), cross(sent[3], 2)]
        self.a = self.part(0, 0, a) + up(across[0])
        self.b = self.part(0, 0, b) + sum(up(v[0]) for v in line)
        return sent

    def third(self, others):
        *line, across = gate(self.third_of, others)
        return jnp.concatenate([self.a + sum(up(v) for v in line), self.b + up(across)])


def cross_z(pieces):
    return [cross(v, 4 * k) for k, v in zip((1, 2, 3), pieces)]


def channel_plan(
    hidden_in, grad_out, doc_starts, norm_gain, in_proj, out_proj, conv_weight, conv_bias,
    x_proj, dt_proj, dt_bias, decay_log, skip_scale,
):
    row_count, seg_len, width = hidden_in.shape
    shards = lax.axis_size("seq")
    full_len = seg_len * shards
    ch = conv_weight.shape[1]
    first = lax.axis_index("row") == 0
    both = ("seq", "row")
    place = 2 * lax.axis_index("seq") + lax.axis_index("row")
    own = own_place()
    gain_len = norm_gain.shape[0]

    hid = gather_tokens(hidden_in)
    gout = gather_tokens(grad_out)
    to_shard = [(i, 2 * (i % shards) + i // shards) for i in range(2 * shards)]
    mine = lax.ppermute(in_proj, both, to_shard)
    other = swap_row(mine)
    weight = jnp.concatenate([jnp.where(first, mine, other), jnp.where(first, other, mine)])
    other = swap_row(out_proj)
    pair = jnp.concatenate([jnp.where(first, out_proj, other), jnp.where(first, other, out_proj)])
    out_cols = lax.all_to_all(pair, "seq", split_axis=1, concat_axis=0, tiled=True)
    spot = jnp.zeros((2 * shards, gain_len), F32)
    spot = lax.dynamic_update_slice(spot, norm_gain.astype(F32)[None], (place, 0))
    gain_whole = total_of_all(spot).reshape(1, width)
    vectors = [
        conv_weight.astype(F32),
        conv_bias.astype(F32)[None],
        dt_bias.astype(F32)[None],
        decay_log.astype(F32),
        skip_scale.astype(F32)[None],
        widened(dt_proj),
        x_proj,
    ]
    weight, gain_whole, out_cols, *vectors = gate([weight, gain_whole, out_cols, *vectors], [])
    conv_w, conv_b, dtb, decay, skip, wide, x_proj = vectors

    normed, x, z, conv, keep, send = front(
        doc_starts, own, hid, gain_whole, weight, conv_w, conv_b, x_proj
    )
    low = sum_pieces(keep, send, F32, []).astype(BF)
    near, far = spread_pieces(low)
    gated, y, states, last, stats = forward_scan(
        [], doc_starts, own, near, far, dt_proj, dtb, decay, skip, conv, z
    )
    mixed = jnp.einsum("rtc,dc->rtd", gated, out_cols, preferred_element_type=F32).astype(BF)
    (cols,) = gate([out_cols], [mixed])
    mixed = lax.psum_scatter(mixed, "seq", scatter_dimension=1, tiled=True)
    gg = jnp.einsum("rtd,dc->rtc", gout, cols, preferred_element_type=F32)
    passed = [jnp.zeros((DT_RANK, ch), F32), jnp.zeros((24, ch), F32), jnp.zeros_like(last), last]
    ggate, gxs, keep, send, gdtproj, misc, _, _ = backward_scan(
        7, 8, [], ([], passed), doc_starts, own, near, far, dt_proj, dtb, decay, skip, conv, z, y,
        gg, states, wide,
    )
    keep, send, gated = gate([keep, send, gated], [])
    low = sum_pieces(keep, send, BF, []).astype(BF)
    gout_cols = jnp.einsum("rtd,rtc->dc", gout, gated, preferred_element_type=F32)
    parts = gout_cols.reshape(shards, 2, width // (2 * shards), ch)
    keep = jnp.where(first, parts[:, 0], parts[:, 1])
    send = jnp.where(first, parts[:, 1], parts[:, 0])
    out_half = (keep + swap_row(send)).astype(BF)
    near, far = spread_pieces(low)
    keep, send, gin, gxproj, cmisc = tail(
        [out_half], doc_starts, own, near, far, conv, gxs, ggate, x, normed, weight, conv_w, conv_b,
        x_proj,
    )
    gnormed = Sum(keep, send)
    gnormed.first([])
    held = [gin, gdtproj, misc, stats, cmisc, gxproj]
    gin, gdtproj, misc, stats, cmisc, gxproj = gate(held, [gnormed.second_of[1]])
    grad_gain = jnp.sum(weight.astype(F32) * gin, axis=0) / gain_whole[0]
    grad_gain = grad_gain.reshape(2 * shards, gain_len)
    grad_gain = grad_gain + swap_row(grad_gain)
    grad_gain = grad_gain + cross(grad_gain, 1)
    keep = jnp.where(first, gin[:ch], gin[ch:])
    send = jnp.where(first, gin[ch:], gin[:ch])
    in_half = (keep + swap_row(send.astype(BF)).astype(F32)).astype(BF)
    small = jnp.concatenate([gdtproj, misc, stats, cmisc, jnp.transpose(gxproj)])
    small = small + swap_row(small)
    gnormed.second([in_half, small, grad_gain])
    grad_gain, out_half = gate([grad_gain, out_half], [gnormed.third_of[0]])
    out_share = lax.all_to_all(out_half, "seq", split_axis=0, concat_axis=0, tiled=True)
    grad_gain = grad_gain + cross(grad_gain, 2)
    *gnormed.third_of, grad_gain = gate([*gnormed.third_of, grad_gain], [])
    gnormed = gnormed.third([])
    in_half, grad_gain = gate([in_half, grad_gain], [gnormed])
    to_owner = [(b, a) for a, b in to_shard]
    in_share = lax.ppermute(in_half, both, to_owner).astype(F32)
    grad_gain = grad_gain + sum(cross_z([grad_gain] * 3))
    out_share = jnp.transpose(out_share.astype(F32), (1, 0, 2)).reshape(width // (2 * shards), E)

    residual = hidden_in.astype(F32)
    hidden_out = (residual + mixed.astype(F32)).astype(BF)
    inv_rms = lax.rsqrt(jnp.mean(residual * residual, axis=-1, keepdims=True) + eps_norm)
    scaled = residual * inv_rms
    grad_scaled = gnormed * gain_whole
    grad_hidden = grad_out.astype(F32) + inv_rms * (
        grad_scaled - scaled * jnp.mean(grad_scaled * scaled, axis=-1, keepdims=True)
    )
    grad_gain = lax.dynamic_slice(grad_gain, (place, 0), (1, gain_len))[0]
    gdtproj, misc, stats, cmisc, gxproj = jnp.split(
        small, [DT_RANK, DT_RANK + 24, DT_RANK + 32, DT_RANK + 40]
    )
    token_count = full_len * row_count * 2
    mean_off = stats[0] / token_count
    spread = jnp.sqrt(stats[1] / token_count - mean_off * mean_off + eps_spread)
    centre = jnp.log(jax.nn.softplus(dt_bias.astype(F32)))
    return (
        hidden_out,
        grad_hidden,
        grad_gain,
        in_share,
        out_share,
        cmisc[:CONV],
        cmisc[CONV],
        jnp.transpose(gxproj),
        gdtproj,
        misc[NSTATE],
        misc[:NSTATE],
        misc[NSTATE + 1],
        jnp.stack([centre + mean_off, spread]),
    )


block_len = 16


def lagged(values, offset, filler):
    if offset == 0:
        return values
    widths = [(0, 0)] * values.ndim
    widths[1] = (offset, 0)
    return jnp.pad(values, widths, constant_values=filler)[:, : values.shape[1]]


def leading(values, offset):
    if offset == 0:
        return values
    widths = [(0, 0)] * values.ndim
    widths[1] = (0, offset)
    return jnp.pad(values, widths)[:, offset:]


def slope_of_silu(values):
    logistic = jax.nn.sigmoid(values)
    return logistic * (1.0 + values * (1.0 - logistic))


def block_scan(decay_rates, dt_row, x_row, b_row, c_row, keep_row):
    length, channels = dt_row.shape
    blocks = length // block_len

    def regroup(values):
        grouped = values.reshape((blocks, block_len) + values.shape[1:])
        return jnp.moveaxis(grouped, 0, -1)

    dt_q, x_q, b_q, c_q, keep_q = (regroup(v) for v in (dt_row, x_row, b_row, c_row, keep_row))

    def decay_at(dt_now, keep_now):
        return jnp.exp(dt_now[None, :, :] * decay_rates[:, :, None]) * keep_now[None, None, :]

    def local_pass(running, inputs):
        state_now, product = running
        dt_now, x_now, b_now, keep_now = inputs
        decay_now = decay_at(dt_now, keep_now)
        state_now = decay_now * state_now + b_now[:, None, :] * (dt_now * x_now)[None, :, :]
        return ((state_now, decay_now * product), None)

    empty_state = jnp.zeros((NSTATE, channels, blocks), jnp.float32)
    (block_ends, block_decay), _ = lax.scan(
        local_pass, (empty_state, jnp.ones_like(empty_state)), (dt_q, x_q, b_q, keep_q)
    )

    def combine(earlier, later):
        return (earlier[0] * later[0], later[0] * earlier[1] + later[1])

    _, reached = lax.associative_scan(combine, (block_decay, block_ends), axis=2)
    starting = jnp.concatenate([jnp.zeros_like(reached[:, :, :1]), reached[:, :, :-1]], axis=2)

    def full_pass(state_now, inputs):
        dt_now, x_now, b_now, c_now, keep_now = inputs
        state_now = (
            decay_at(dt_now, keep_now) * state_now
            + b_now[:, None, :] * (dt_now * x_now)[None, :, :]
        )
        return (state_now, jnp.sum(c_now[:, None, :] * state_now, axis=0))

    _, outputs = lax.scan(full_pass, starting, (dt_q, x_q, b_q, c_q, keep_q))
    return jnp.moveaxis(outputs, 2, 0).reshape(length, channels)


def scan_all(dt_vals, x_vals, b_vals, c_vals, decay_full, skip_full, keep_mask):
    decay_rates = -jnp.exp(decay_full)
    per_row = jax.checkpoint(block_scan)

    def one_row(row_items):
        return per_row(decay_rates, *row_items)

    outputs = lax.map(one_row, (dt_vals, x_vals, b_vals, c_vals, keep_mask))
    return outputs + skip_full * x_vals


def token_plan(
    hidden_in,
    grad_out,
    doc_starts,
    norm_gain,
    in_proj,
    out_proj,
    conv_weight,
    conv_bias,
    x_proj,
    dt_proj,
    dt_bias,
    decay_log,
    skip_scale,
):
    row_count, seg_len, model_width = hidden_in.shape
    full_len = seg_len * lax.axis_size("seq")
    gain_whole, in_whole, out_whole = (
        lax.all_gather(norm_gain, ("seq", "row"), axis=0, tiled=True),
        lax.all_gather(in_proj, ("seq", "row"), axis=0, tiled=True),
        lax.all_gather(out_proj, ("seq", "row"), axis=0, tiled=True),
    )
    residual = hidden_in.astype(jnp.float32)
    inv_rms = lax.rsqrt(jnp.mean(residual * residual, axis=-1, keepdims=True) + eps_norm)
    scaled = residual * inv_rms
    gain_full = gain_whole.astype(jnp.float32)
    normed = (scaled * gain_full).astype(jnp.bfloat16)
    proj_in = jnp.einsum("rtd,fd->rtf", normed, in_whole, preferred_element_type=jnp.float32)
    x_tokens = proj_in[..., :E].astype(jnp.bfloat16)
    gate_z = proj_in[..., E:]
    x_chan = lax.all_to_all(x_tokens, "seq", split_axis=2, concat_axis=1, tiled=True)
    positions = lax.broadcasted_iota(jnp.int32, (1, full_len, 1), 1)
    doc_ids = jnp.sum((doc_starts[:, None, :] <= positions).astype(jnp.int32), axis=2) - 1
    same_docs = [
        (lagged(doc_ids, offset, -1) == doc_ids).astype(jnp.float32)[..., None]
        for offset in range(CONV)
    ]
    keep_mask = same_docs[1][..., 0]
    x_vals = x_chan.astype(jnp.float32)
    conv_full = conv_weight.astype(jnp.float32)
    pre_conv = conv_bias.astype(jnp.float32) + jnp.zeros_like(x_vals)
    for offset in range(CONV):
        pre_conv = (
            pre_conv
            + conv_full[CONV - 1 - offset] * lagged(x_vals, offset, 0.0) * same_docs[offset]
        )
    conv_low = jax.nn.silu(pre_conv).astype(jnp.bfloat16)
    part_sums = jnp.einsum("rtc,cm->rtm", conv_low, x_proj, preferred_element_type=jnp.float32)
    dtbc = lax.psum(part_sums, "seq").astype(jnp.bfloat16)
    dt_low = dtbc[..., :DT_RANK]
    b_vals = dtbc[..., DT_RANK : DT_RANK + NSTATE].astype(jnp.float32)
    c_vals = dtbc[..., DT_RANK + NSTATE :].astype(jnp.float32)
    pre_dt = jnp.einsum(
        "rtk,kc->rtc", dt_low, dt_proj, preferred_element_type=jnp.float32
    ) + dt_bias.astype(jnp.float32)
    dt_vals = jax.nn.softplus(pre_dt)
    y_vals, pullback = jax.vjp(
        partial(scan_all, keep_mask=keep_mask),
        dt_vals,
        conv_low.astype(jnp.float32),
        b_vals,
        c_vals,
        decay_log.astype(jnp.float32),
        skip_scale.astype(jnp.float32),
    )
    y_tokens = lax.all_to_all(
        y_vals.astype(jnp.bfloat16), "seq", split_axis=1, concat_axis=2, tiled=True
    )
    y_token_vals = y_tokens.astype(jnp.float32)
    gate_act = jax.nn.silu(gate_z)
    gated = (y_token_vals * gate_act).astype(jnp.bfloat16)
    mixed = jnp.einsum("rte,de->rtd", gated, out_whole, preferred_element_type=jnp.float32)
    hidden_out = (residual + mixed).astype(jnp.bfloat16)
    grad_out_proj = jnp.einsum("rtd,rte->de", grad_out, gated, preferred_element_type=jnp.float32)
    grad_gated = jnp.einsum("rtd,de->rte", grad_out, out_whole, preferred_element_type=jnp.float32)
    grad_y = (grad_gated * gate_act).astype(jnp.bfloat16)
    grad_gate = (grad_gated * y_token_vals * slope_of_silu(gate_z)).astype(jnp.bfloat16)
    grad_y_chan = lax.all_to_all(grad_y, "seq", split_axis=2, concat_axis=1, tiled=True)
    grad_dt_scan, grad_x_scan, grad_b, grad_c, grad_decay, grad_skip = pullback(
        grad_y_chan.astype(jnp.float32)
    )
    grad_pre_dt = (grad_dt_scan * jax.nn.sigmoid(pre_dt)).astype(jnp.bfloat16)
    grad_dt_low = jnp.einsum(
        "rtc,kc->rtk", grad_pre_dt, dt_proj, preferred_element_type=jnp.float32
    )
    grad_dt_proj = jnp.einsum(
        "rtk,rtc->kc", dt_low, grad_pre_dt, preferred_element_type=jnp.float32
    )
    grad_dt_bias = jnp.sum(grad_pre_dt.astype(jnp.float32), axis=(0, 1))
    grad_parts = jnp.concatenate([grad_dt_low, grad_b, grad_c], axis=-1)
    grad_share = lax.psum_scatter(grad_parts, "seq", scatter_dimension=1, tiled=True)
    grad_dtbc = lax.all_gather(grad_share.astype(jnp.bfloat16), "seq", axis=1, tiled=True)
    grad_x_proj = jnp.einsum("rtc,rtm->cm", conv_low, grad_dtbc, preferred_element_type=jnp.float32)
    grad_conv_out = grad_x_scan + jnp.einsum(
        "rtm,cm->rtc", grad_dtbc, x_proj, preferred_element_type=jnp.float32
    )
    grad_pre_conv = grad_conv_out * slope_of_silu(pre_conv)
    grad_conv_bias = jnp.sum(grad_pre_conv, axis=(0, 1))
    conv_rows = [None] * CONV
    grad_x = jnp.zeros_like(grad_pre_conv)
    for offset in range(CONV):
        masked = grad_pre_conv * same_docs[offset]
        conv_rows[CONV - 1 - offset] = jnp.sum(masked * lagged(x_vals, offset, 0.0), axis=(0, 1))
        grad_x = grad_x + conv_full[CONV - 1 - offset] * leading(masked, offset)
    grad_conv_weight = jnp.stack(conv_rows)
    grad_x_tokens = lax.all_to_all(
        grad_x.astype(jnp.bfloat16), "seq", split_axis=1, concat_axis=2, tiled=True
    )
    grad_proj = jnp.concatenate([grad_x_tokens, grad_gate], axis=-1)
    grad_in_proj = jnp.einsum("rtf,rtd->fd", grad_proj, normed, preferred_element_type=jnp.float32)
    grad_normed = jnp.einsum("rtf,fd->rtd", grad_proj, in_whole, preferred_element_type=jnp.float32)
    grad_gain = jnp.sum(grad_normed * scaled, axis=(0, 1))
    grad_scaled = grad_normed * gain_full
    grad_hidden = grad_out.astype(jnp.float32) + inv_rms * (
        grad_scaled - scaled * jnp.mean(grad_scaled * scaled, axis=-1, keepdims=True)
    )
    gain_share, in_share, out_share = (
        lax.psum_scatter(grad_gain, ("seq", "row"), scatter_dimension=0, tiled=True),
        lax.psum_scatter(grad_in_proj, ("seq", "row"), scatter_dimension=0, tiled=True),
        lax.psum_scatter(grad_out_proj, ("seq", "row"), scatter_dimension=0, tiled=True),
    )
    centre = jnp.log(jax.nn.softplus(dt_bias.astype(jnp.float32)))
    offset_dt = jnp.log(dt_vals) - centre
    first_sum = jnp.sum(offset_dt, axis=(0, 1))
    second_sum = jnp.sum(offset_dt * offset_dt, axis=(0, 1))
    summed = lax.psum(
        (
            grad_conv_weight,
            grad_conv_bias,
            grad_x_proj,
            grad_dt_proj,
            grad_dt_bias,
            grad_decay,
            grad_skip,
            first_sum,
            second_sum,
        ),
        "row",
    )
    token_count = full_len * row_count * lax.axis_size("row")
    mean_off = summed[7] / token_count
    spread = jnp.sqrt(summed[8] / token_count - mean_off * mean_off + eps_spread)
    dt_stats = jnp.stack([centre + mean_off, spread])
    return (
        hidden_out,
        grad_hidden,
        gain_share,
        in_share,
        out_share,
        summed[0],
        summed[1],
        summed[2],
        summed[3],
        summed[4],
        summed[5],
        summed[6],
        dt_stats,
    )


def solution(mesh):
    fits = mesh.shape["seq"] == 16 and mesh.shape["row"] == 2
    plan = channel_plan if fits else token_plan
    return jax.shard_map(
        plan,
        mesh=mesh,
        in_specs=(
            P("row", "seq", None),
            P("row", "seq", None),
            P("row", None),
            P(("seq", "row")),
            P(("seq", "row"), None),
            P(("seq", "row"), None),
            P(None, "seq"),
            P("seq"),
            P("seq", None),
            P(None, "seq"),
            P("seq"),
            P(None, "seq"),
            P("seq"),
        ),
        out_specs=(
            P("row", "seq", None),
            P("row", "seq", None),
            P(("seq", "row")),
            P(("seq", "row"), None),
            P(("seq", "row"), None),
            P(None, "seq"),
            P("seq"),
            P("seq", None),
            P(None, "seq"),
            P("seq"),
            P(None, "seq"),
            P("seq"),
            P(None, "seq"),
        ),
        check_vma=False,
    )
```

```python
from functools import partial

import jax
import jax.numpy as jnp
from jax import lax
from jax.experimental import pallas as pl
from jax.experimental.pallas import tpu as pltpu
from jax.sharding import PartitionSpec as P

E = 2048
NSTATE = 16
CONV = 4
DT_RANK = 64
MAPS = DT_RANK + 2 * NSTATE

eps_norm = 1e-05
eps_spread = 1e-06
BF = jnp.bfloat16
F32 = jnp.float32
LOG2E = 1.4426950408889634
FAR = 1e4
LANES = 128
VMEM = 28 << 20


def params(dims=2):
    return pltpu.CompilerParams(
        dimension_semantics=("arbitrary",) * dims, vmem_limit_bytes=VMEM
    )


def place_in_doc(starts_ref, row, first, count):
    pos = lax.broadcasted_iota(jnp.int32, (count, LANES), 0) + first
    base = jnp.zeros_like(pos)
    for j in range(1, starts_ref.shape[1]):
        start = starts_ref[row, j]
        base = jnp.where(pos >= start, start, base)
    return pos - base


def large(shape, dtype):
    return pltpu.HBM(shape, dtype)


def still(*values):
    return [pltpu.with_memory_space_constraint(v, pltpu.HBM) for v in values]


def sigmoid(v):
    return 1.0 / (1.0 + jnp.exp2(v * -LOG2E))


def silu_slope(v):
    s = sigmoid(v)
    return s * (1.0 + v * (1.0 - s))


def softplus(v):
    return jnp.maximum(v, 0.0) + jnp.log1p(jnp.exp2(jnp.abs(v) * -LOG2E))


def dot(a, b, dims):
    return lax.dot_general(a, b, (dims, ((), ())), preferred_element_type=F32)


def own_place():
    s = lax.axis_index("seq")
    return jnp.stack([s // 4, s // 2 % 2, s % 2]).astype(jnp.int32)


def gate_kernel(*refs):
    pass


def gate(values, others):
    place = pl.BlockSpec(memory_space=pl.ANY)
    return pl.pallas_call(
        gate_kernel,
        in_specs=[place] * (len(values) + len(others)),
        out_specs=[place] * len(values),
        out_shape=[jax.ShapeDtypeStruct(v.shape, v.dtype) for v in values],
        input_output_aliases={i: i for i in range(len(values))},
        compiler_params=pltpu.CompilerParams(vmem_limit_bytes=1 << 16),
        cost_estimate=pl.CostEstimate(flops=1, bytes_accessed=1, transcendentals=0),
        name="gate",
    )(*values, *others)


def put_pieces(own, value, keep, send):
    rows, seg = keep.shape[2], keep.shape[3]
    first = own[2] == 0
    for r in range(rows):
        for x in range(2):
            at = (r * 4 + 2 * x) * seg
            even, odd = value[at : at + seg], value[at + seg : at + 2 * seg]
            keep[x ^ own[1], 0, r] = jnp.where(first, even, odd).astype(keep.dtype)
            send[x ^ own[1], 0, r] = jnp.where(first, odd, even).astype(send.dtype)


def take_pieces(own, near, far, out):
    rows, seg = near.shape[2], near.shape[3]
    first = own[2] == 0
    for r in range(rows):
        for x in range(2):
            at = (r * 4 + 2 * x) * seg
            a = near[x ^ own[1], 0, r].astype(F32)
            b = far[x ^ own[1], 0, r].astype(F32)
            out[at : at + seg, :] = jnp.where(first, a, b)
            out[at + seg : at + 2 * seg, :] = jnp.where(first, b, a)


def pieces_spec(rows, seg, n, at):
    return pl.BlockSpec((2, 1, rows, seg, n), lambda c, s, o: (0, at(c) ^ o[0], 0, 0, 0))


def fixed_block(shape):
    return pl.BlockSpec(shape, lambda c, s, o: (0,) * len(shape))


def front_kernel(
    starts, own, hid, gain, weight, conv_w, conv_b, xproj,
    normed_o, x_o, z_o, conv_o, keep_o, send_o,
    xs,
):
    c = pl.program_id(0)
    rows, t, ch = x_o.shape
    width = normed_o.shape[2]

    @pl.when(c == 0)
    def _():
        xs[:, 0:8, :] = jnp.zeros((rows, 8, ch), F32)

    @pl.when(c > 0)
    def _():
        xs[:, 0:8, :] = xs[:, t : t + 8, :]

    res = hid[...].reshape(rows * t, width).astype(F32)
    inv = lax.rsqrt(jnp.mean(res * res, axis=-1, keepdims=True) + eps_norm)
    normed = (res * inv * gain[...]).astype(BF)
    normed_o[...] = normed.reshape(rows, t, width)
    proj = dot(normed, weight[...], ((1,), (1,)))
    z_o[...] = proj[:, ch:].reshape(rows, t, ch)
    x_low = proj[:, :ch].astype(BF).reshape(rows, t, ch)
    x_o[...] = x_low
    xs[:, 8 : 8 + t, :] = x_low.astype(F32)
    for r in range(rows):
        place = place_in_doc(starts, r, c * t, t)
        pre = conv_b[...] + conv_w[CONV - 1 : CONV, :] * xs[r, 8 : 8 + t, :]
        for k in range(1, CONV):
            lag = conv_w[CONV - 1 - k : CONV - k, :] * xs[r, 8 - k : 8 - k + t, :]
            pre = pre + jnp.where(place >= k, lag, 0.0)
        conv_o[r] = (pre * sigmoid(pre)).astype(BF)
    conv = conv_o[...].reshape(rows * t, ch)
    put_pieces(own, dot(conv, xproj[...], ((1,), (0,))), keep_o, send_o)


def front(starts, own, hid, gain, weight, conv_w, conv_b, xproj):
    (hid,) = still(hid)
    rows, length, width = hid.shape
    ch = conv_w.shape[1]
    t = length // 4
    seg = t // 4
    tok = lambda n: pl.BlockSpec((rows, t, n), lambda c, s, o: (0, c, 0))
    piece = pieces_spec(rows, seg, MAPS, lambda c: c)
    return pl.pallas_call(
        front_kernel,
        grid_spec=pltpu.PrefetchScalarGridSpec(
            num_scalar_prefetch=2,
            grid=(length // t,),
            in_specs=[
                tok(width),
                fixed_block(gain.shape),
                fixed_block(weight.shape),
                fixed_block(conv_w.shape),
                fixed_block(conv_b.shape),
                fixed_block(xproj.shape),
            ],
            out_specs=[tok(width), tok(ch), tok(ch), tok(ch), piece, piece],
            scratch_shapes=[pltpu.VMEM((rows, t + 8, ch), F32)],
        ),
        out_shape=[
            large((rows, length, width), BF),
            large((rows, length, ch), BF),
            large((rows, length, ch), F32),
            large((rows, length, ch), BF),
            jax.ShapeDtypeStruct((2, 4, rows, seg, MAPS), F32),
            jax.ShapeDtypeStruct((2, 4, rows, seg, MAPS), F32),
        ],
        compiler_params=params(1),
        cost_estimate=pl.CostEstimate(flops=1, bytes_accessed=1, transcendentals=0),
        name="front",
    )(starts, own, hid, gain, weight, conv_w, conv_b, xproj)


def maps_across(low):
    pick = lax.broadcasted_iota(jnp.int32, (2 * NSTATE, MAPS), 0) + DT_RANK
    pick = (pick == lax.broadcasted_iota(jnp.int32, (2 * NSTATE, MAPS), 1)).astype(BF)
    return dot(pick, low, ((1,), (1,)))


def half_spec(rows, seg, n, at):
    return pl.BlockSpec(
        (1, 1, rows, seg, n),
        lambda c, s, o: (at(c) % 2 ^ o[1], at(c) // 2 ^ o[0], 0, 0, 0),
    )


def put_halves(own, value, keep, send):
    rows, seg = keep.shape[2], keep.shape[3]
    first = own[2] == 0
    for r in range(rows):
        even = value[2 * r * seg : (2 * r + 1) * seg]
        odd = value[(2 * r + 1) * seg : (2 * r + 2) * seg]
        keep[0, 0, r] = jnp.where(first, even, odd).astype(keep.dtype)
        send[0, 0, r] = jnp.where(first, odd, even).astype(send.dtype)


def take_halves(own, near, far, out):
    rows, seg = near.shape[2], near.shape[3]
    first = own[2] == 0
    for r in range(rows):
        a = near[0, 0, r].astype(F32)
        b = far[0, 0, r].astype(F32)
        out[2 * r * seg : (2 * r + 1) * seg, :] = jnp.where(first, a, b)
        out[(2 * r + 1) * seg : (2 * r + 2) * seg, :] = jnp.where(first, b, a)


def fold(parts):
    row = lax.broadcasted_iota(jnp.int32, parts[0].shape, 0)
    upper = row < 4
    parts = [
        jnp.where(upper, a, b) + pltpu.roll(jnp.where(upper, b, a), 4, 0)
        for a, b in zip(parts[:4], parts[4:])
    ]
    for step in (2, 1):
        half = len(parts) // 2
        upper = row & step == 0
        parts = [
            jnp.where(upper, a + pltpu.roll(a, 8 - step, 0), b + pltpu.roll(b, step, 0))
            for a, b in zip(parts[:half], parts[half:])
        ]
    return parts[0]


def spread_maps(low, first, out):
    count, ch = low.shape[0], out.shape[1]
    pick = lax.broadcasted_iota(jnp.int32, (MAPS, NSTATE * ch), 1) // ch + first
    pick = (pick == lax.broadcasted_iota(jnp.int32, (MAPS, NSTATE * ch), 0)).astype(BF)
    wide = dot(low, pick, ((1,), (0,)))
    for b in range(count // 8):
        for n in range(NSTATE):
            row = (b * NSTATE + n) * 8
            out[row : row + 8, :] = wide[b * 8 : b * 8 + 8, n * ch : (n + 1) * ch]


def forward_kernel(starts, own, near, far, dtproj, dtbias, decay, skip, conv, z, cols, *refs):
    (
        gated_o, y_o, states_o, mixed_o, last_o, stats_o,
        state, dtk_s, dtx_s, y_s, across_s, low_s, cm_s,
    ) = refs[-13:]
    c = pl.program_id(0)
    rows, t, ch = conv.shape

    @pl.when(c == 0)
    def _():
        state[...] = jnp.zeros_like(state)
        stats_o[...] = jnp.zeros_like(stats_o)

    rate = -LOG2E * jnp.exp(decay[...])
    take_halves(own, near, far, low_s)
    low = low_s[...].astype(BF)
    dt = softplus(dot(low[:, :DT_RANK], dtproj[...], ((1,), (0,))) + dtbias[...])
    off = jnp.log(dt) - jnp.log(softplus(dtbias[...]))
    stats_o[0:1, :] += jnp.sum(off, axis=0, keepdims=True)
    stats_o[1:2, :] += jnp.sum(off * off, axis=0, keepdims=True)
    x = conv[...].astype(F32).reshape(rows * t, ch)
    for r in range(rows):
        place = place_in_doc(starts, r, c * t, t)
        dtk_s[r * t : (r + 1) * t, :] = jnp.where(place >= 1, dt[r * t : (r + 1) * t], FAR)
    dtx_s[...] = dt * x
    across_s[...] = maps_across(low)
    spread_maps(low, DT_RANK + NSTATE, cm_s)

    def every_step(states):
        states, sums = list(states), [None] * rows
        maps = [across_s[:, r * t : (r + 1) * t] for r in range(rows)]
        for i in range(t):
            for r in range(rows):
                if i % 8 == 0:
                    sums[r] = []
                at = r * t + i
                s = states[r]
                a = jnp.exp2(dtk_s[pl.ds(at, 1), :] * rate)
                states_o[r, i] = s
                b = jnp.broadcast_to(maps[r][:NSTATE, i : i + 1], (NSTATE, ch))
                s = a * s + dtx_s[pl.ds(at, 1), :] * b
                ys = s * cm_s[pl.ds(at // 8 * 8 * NSTATE + at % 8, NSTATE, stride=8), :]
                sums[r].append(ys[:8] + ys[8:])
                if i % 8 == 7:
                    y_s[pl.ds(r * t + i - 7, 8), :] = fold(sums[r])
                states[r] = s
        return tuple(states)

    states = every_step(tuple(state[r] for r in range(rows)))
    for r in range(rows):
        state[r] = states[r]
        last_o[r] = states[r]
    y_low = (y_s[...] + skip[...] * x).astype(BF)
    y_o[...] = y_low.reshape(rows, t, ch)
    zz = z[...].reshape(rows * t, ch)
    gated = (y_low.astype(F32) * (zz * sigmoid(zz))).astype(BF)
    gated_o[...] = gated.reshape(rows, t, ch)
    mixed = dot(gated, cols[...], ((1,), (1,))).astype(BF)
    mixed_o[...] = mixed.reshape(rows, t, cols.shape[0])


def forward_scan(after, starts, own, near, far, dtproj, dtbias, decay, skip, conv, z, cols):
    conv, z = still(conv, z)
    rows, length, ch = conv.shape
    t = length // 8
    seg = t // 2
    tok = lambda n: pl.BlockSpec((rows, t, n), lambda c, s, o: (0, c, 0))
    half = half_spec(rows, seg, MAPS, lambda c: c)
    return pl.pallas_call(
        forward_kernel,
        grid_spec=pltpu.PrefetchScalarGridSpec(
            num_scalar_prefetch=2,
            grid=(length // t,),
            in_specs=[
                half,
                half,
                fixed_block(dtproj.shape),
                fixed_block(dtbias.shape),
                fixed_block(decay.shape),
                fixed_block(skip.shape),
                tok(ch),
                tok(ch),
                fixed_block(cols.shape),
                *[pl.BlockSpec(memory_space=pl.ANY)] * len(after),
            ],
            out_specs=[
                tok(ch),
                tok(ch),
                pl.BlockSpec((rows, t, NSTATE, ch), lambda c, s, o: (0, c, 0, 0)),
                tok(cols.shape[0]),
                fixed_block((rows, NSTATE, ch)),
                fixed_block((8, ch)),
            ],
            scratch_shapes=[
                pltpu.VMEM((rows, NSTATE, ch), F32),
                pltpu.VMEM((rows * t, ch), F32),
                pltpu.VMEM((rows * t, ch), F32),
                pltpu.VMEM((rows * t, ch), F32),
                pltpu.VMEM((2 * NSTATE, rows * t), F32),
                pltpu.VMEM((rows * t, MAPS), F32),
                pltpu.VMEM((rows * t * NSTATE, ch), F32),
            ],
        ),
        out_shape=[
            large((rows, length, ch), BF),
            large((rows, length, ch), BF),
            large((rows, length, NSTATE, ch), F32),
            large((rows, length, cols.shape[0]), BF),
            jax.ShapeDtypeStruct((rows, NSTATE, ch), F32),
            jax.ShapeDtypeStruct((8, ch), F32),
        ],
        compiler_params=params(1),
        cost_estimate=pl.CostEstimate(flops=1, bytes_accessed=1, transcendentals=0),
        name="forward_scan",
    )(starts, own, near, far, dtproj, dtbias, decay, skip, conv, z, cols, *after)


def backward_kernel(
    starts, own, near, far, dtproj, dtbias, decay, skip, conv, z, y, gout, cols, states, wide,
    gdtproj_i, misc_i, back_i, next_i, *refs, top,
):
    (
        ggate_o, gxs_o, keep_o, send_o, gdtproj_o, misc_o, back_o, next_o,
        dtk_s, dt_s, dtx_s, gy_s, p1_s, p2_s, gb_s, gc_s, fold_s, across_s, low_s,
    ) = refs[-19:]
    c = pl.program_id(0)
    rows, t, ch = conv.shape
    count = rows * t

    @pl.when(c == 0)
    def _():
        back_o[...] = back_i[...]
        next_o[...] = next_i[...]
        gdtproj_o[...] = gdtproj_i[...]
        misc_o[...] = misc_i[...]

    neg = -jnp.exp(decay[...])
    rate = LOG2E * neg
    take_halves(own, near, far, low_s)
    low = low_s[...].astype(BF)
    pre = dot(low[:, :DT_RANK], dtproj[...], ((1,), (0,))) + dtbias[...]
    dt = softplus(pre)
    x = conv[...].astype(F32).reshape(count, ch)
    for r in range(rows):
        place = place_in_doc(starts, r, (top - c) * t, t)
        dtk_s[r * t : (r + 1) * t, :] = jnp.where(place >= 1, dt[r * t : (r + 1) * t], FAR)
    dt_s[...] = dt
    dtx_s[...] = dt * x
    zz = z[...].reshape(count, ch)
    ggv = dot(gout[...].reshape(count, gout.shape[2]), cols[...], ((1,), (0,)))
    sg = sigmoid(zz)
    gy = (ggv * (zz * sg)).astype(BF).astype(F32)
    yv = y[...].astype(F32).reshape(count, ch)
    ggate = (ggv * yv * (sg * (1.0 + zz * (1.0 - sg)))).astype(BF)
    ggate_o[...] = ggate.reshape(rows, t, ch)
    gy_s[...] = gy
    across_s[...] = maps_across(low)

    def every_step(carry):
        hs, s_nexts, acc = list(carry[0]), list(carry[1]), carry[2]
        p1s, p2s = [None] * rows, [None] * rows
        maps = [across_s[:, r * t : (r + 1) * t] for r in range(rows)]
        for i in range(t - 1, -1, -1):
            for r in range(rows):
                at = r * t + i
                gyr = gy_s[pl.ds(at, 1), :]
                g = gyr * jnp.broadcast_to(maps[r][NSTATE:, i : i + 1], (NSTATE, ch)) + hs[r]
                h = jnp.exp2(dtk_s[pl.ds(at, 1), :] * rate) * g
                s_prev = states[r, i]
                q = h * s_prev
                acc = acc + q * dt_s[pl.ds(at, 1), :]
                aq = q * neg
                bg = g * jnp.broadcast_to(maps[r][:NSTATE, i : i + 1], (NSTATE, ch))
                if i % 8 == 7:
                    p1s[r], p2s[r] = [], []
                p1s[r].insert(0, bg[:8] + bg[8:])
                p2s[r].insert(0, aq[:8] + aq[8:])
                if i % 8 == 0:
                    whole8 = pl.ds(at, 8)
                    p1_s[whole8, :] = fold(p1s[r])
                    p2_s[whole8, :] = fold(p2s[r])
                tile = pl.ds(at * NSTATE, NSTATE)
                gb_s[tile, :] = (g * dtx_s[pl.ds(at, 1), :]).astype(BF)
                gc_s[tile, :] = (gyr * s_nexts[r]).astype(BF)
                hs[r], s_nexts[r] = h, s_prev
        return tuple(hs), tuple(s_nexts), acc

    hs, s_nexts, acc = every_step(
        (
            tuple(back_o[r] for r in range(rows)),
            tuple(next_o[r] for r in range(rows)),
            jnp.zeros((NSTATE, ch), F32),
        ),
    )
    for r in range(rows):
        back_o[r] = hs[r]
        next_o[r] = s_nexts[r]
    p1, p2 = p1_s[...], p2_s[...]
    gxs_o[...] = (dt * p1 + skip[...] * gy).reshape(rows, t, ch)
    gpre = ((p2 + x * p1) * sigmoid(pre)).astype(BF)
    gdtproj_o[...] += dot(low[:, :DT_RANK], gpre, ((0,), (0,)))
    misc_o[0:NSTATE, :] += neg * acc
    misc_o[NSTATE : NSTATE + 1, :] += jnp.sum(gpre.astype(F32), axis=0, keepdims=True)
    misc_o[NSTATE + 1 : NSTATE + 2, :] += jnp.sum(gy * x, axis=0, keepdims=True)
    ones = jnp.ones((ch, ch), BF)
    entry = lax.broadcasted_iota(jnp.int32, (1, NSTATE, ch), 1) + DT_RANK
    lane = lax.broadcasted_iota(jnp.int32, (1, NSTATE, ch), 2)
    maps = jnp.zeros((count, NSTATE, ch), F32)
    for ref in (gb_s, gc_s):
        every = dot(ref[...], ones, ((1,), (0,))).reshape(count, NSTATE, ch)
        maps = jnp.where(lane == entry, every, maps)
        entry = entry + NSTATE
    fold_s[...] = (maps[:, :8] + maps[:, 8:]).reshape(count * 8, ch)
    total = dot(gpre, wide[...], ((1,), (0,)))
    for j in range(8):
        total = total + fold_s[pl.ds(j, count, stride=8), :][:, :MAPS]
    put_halves(own, total, keep_o, send_o)


def widened(dtproj):
    return jnp.pad(dtproj.T, ((0, 0), (0, 2 * NSTATE)))


def backward_scan(
    top, chunks, after, so_far, starts, own, near, far, dtproj, dtbias, decay, skip, conv, z, y,
    gout, cols, states, wide,
):
    conv, z, y, gout, states = still(conv, z, y, gout, states)
    rows, length, ch = conv.shape
    t = length // 8
    seg = t // 2
    done, passed = so_far
    fixed = 19
    tok = lambda n: pl.BlockSpec((rows, t, n), lambda c, s, o: (0, top - c, 0))
    half = half_spec(rows, seg, MAPS, lambda c: top - c)
    small = [(DT_RANK, ch), (24, ch), (rows, NSTATE, ch), (rows, NSTATE, ch)]
    return pl.pallas_call(
        partial(backward_kernel, top=top),
        grid_spec=pltpu.PrefetchScalarGridSpec(
            num_scalar_prefetch=2,
            grid=(chunks,),
            in_specs=[
                half,
                half,
                fixed_block(dtproj.shape),
                fixed_block(dtbias.shape),
                fixed_block(decay.shape),
                fixed_block(skip.shape),
                tok(ch),
                tok(ch),
                tok(ch),
                tok(gout.shape[2]),
                fixed_block(cols.shape),
                pl.BlockSpec((rows, t, NSTATE, ch), lambda c, s, o: (0, top - c, 0, 0)),
                fixed_block(wide.shape),
                *[fixed_block(s) for s in small],
                *[pl.BlockSpec(memory_space=pl.ANY)] * (len(done) + len(after)),
            ],
            out_specs=[tok(ch), tok(ch), half, half, *[fixed_block(s) for s in small]],
            scratch_shapes=[
                pltpu.VMEM((rows * t, ch), F32),
                pltpu.VMEM((rows * t, ch), F32),
                pltpu.VMEM((rows * t, ch), F32),
                pltpu.VMEM((rows * t, ch), F32),
                pltpu.VMEM((rows * t, ch), F32),
                pltpu.VMEM((rows * t, ch), F32),
                pltpu.VMEM((rows * t * NSTATE, ch), BF),
                pltpu.VMEM((rows * t * NSTATE, ch), BF),
                pltpu.VMEM((rows * t * 8, ch), F32),
                pltpu.VMEM((2 * NSTATE, rows * t), F32),
                pltpu.VMEM((rows * t, MAPS), F32),
            ],
        ),
        out_shape=[
            large((rows, length, ch), BF),
            large((rows, length, ch), F32),
            jax.ShapeDtypeStruct((2, 4, rows, seg, MAPS), F32),
            jax.ShapeDtypeStruct((2, 4, rows, seg, MAPS), F32),
            *[jax.ShapeDtypeStruct(s, F32) for s in small],
        ],
        input_output_aliases={fixed + i: i for i in range(len(done))},
        compiler_params=params(1),
        cost_estimate=pl.CostEstimate(flops=1, bytes_accessed=1, transcendentals=0),
        name="backward_scan",
    )(
        starts, own, near, far, dtproj, dtbias, decay, skip, conv, z, y, gout, cols, states, wide,
        *passed, *done, *after,
    )


def tail_kernel(
    starts, own, near, far, conv, gxs, ggate, x, before, normed, weight, conv_w, conv_b, xproj, *refs
):
    keep_o, send_o, gin_o, gxproj_o, misc_o, xs, gm_s, low_s, gx_s = refs[-9:]
    c = pl.program_id(0)
    chunks = pl.num_programs(0)
    rows, t, ch = conv.shape
    count = rows * t

    @pl.when(c == 0)
    def _():
        gin_o[...] = jnp.zeros_like(gin_o)
        gxproj_o[...] = jnp.zeros_like(gxproj_o)
        misc_o[...] = jnp.zeros_like(misc_o)
        gm_s[:, :, t : t + 8, :] = jnp.zeros((CONV - 1, rows, 8, ch), F32)

    @pl.when(c > 0)
    def _():
        gm_s[:, :, t : t + 8, :] = gm_s[:, :, 0:8, :]

    xs[:, 0:16, :] = before[...].astype(F32)
    xs[:, 16 : 16 + t, :] = x[...].astype(F32)
    take_pieces(own, near, far, low_s)
    low = low_s[...].astype(BF)
    gconv = gxs[...].reshape(count, ch) + dot(low, xproj[...], ((1,), (1,)))
    gxproj_o[...] += dot(conv[...].reshape(count, ch), low, ((0,), (0,)))
    for r in range(rows):
        place = place_in_doc(starts, r, (chunks - 1 - c) * t, t)
        lags = [xs[r, 16 : 16 + t, :]]
        pre = conv_b[...] + conv_w[CONV - 1 : CONV, :] * lags[0]
        for k in range(1, CONV):
            lags.append(jnp.where(place >= k, xs[r, 16 - k : 16 - k + t, :], 0.0))
            pre = pre + conv_w[CONV - 1 - k : CONV - k, :] * lags[k]
        gpre = gconv[r * t : (r + 1) * t] * silu_slope(pre)
        gx = conv_w[CONV - 1 : CONV, :] * gpre
        for k in range(CONV):
            misc_o[CONV - 1 - k : CONV - k, :] += jnp.sum(gpre * lags[k], axis=0, keepdims=True)
            if k:
                gm_s[k - 1, r, 0:t, :] = jnp.where(place >= k, gpre, 0.0)
                gx = gx + conv_w[CONV - 1 - k : CONV - k, :] * gm_s[k - 1, r, k : k + t, :]
        misc_o[CONV : CONV + 1, :] += jnp.sum(gpre, axis=0, keepdims=True)
        gx_s[r * t : (r + 1) * t, :] = gx.astype(BF)
    gproj = jnp.concatenate([gx_s[...], ggate[...].reshape(count, ch)], axis=1)
    gin_o[...] += dot(gproj, normed[...].reshape(count, normed.shape[2]), ((0,), (0,)))
    put_pieces(own, dot(gproj, weight[...], ((1,), (0,))), keep_o, send_o)


def tail(after, starts, own, near, far, conv, gxs, ggate, x, normed, weight, conv_w, conv_b, xproj):
    conv, gxs, ggate, x, normed = still(conv, gxs, ggate, x, normed)
    rows, length, width = normed.shape
    ch = conv.shape[2]
    t = length // 4
    seg = t // 4
    last = length // t - 1
    tok = lambda n: pl.BlockSpec((rows, t, n), lambda c, s, o: (0, last - c, 0))
    piece = lambda n: pieces_spec(rows, seg, n, lambda c: last - c)
    before = pl.BlockSpec(
        (rows, 16, ch), lambda c, s, o: (0, jnp.maximum((last - c) * (t // 16) - 1, 0), 0)
    )
    return pl.pallas_call(
        tail_kernel,
        grid_spec=pltpu.PrefetchScalarGridSpec(
            num_scalar_prefetch=2,
            grid=(length // t,),
            in_specs=[
                piece(MAPS),
                piece(MAPS),
                tok(ch),
                tok(ch),
                tok(ch),
                tok(ch),
                before,
                tok(width),
                fixed_block(weight.shape),
                fixed_block(conv_w.shape),
                fixed_block(conv_b.shape),
                fixed_block(xproj.shape),
                *[pl.BlockSpec(memory_space=pl.ANY)] * len(after),
            ],
            out_specs=[
                piece(width),
                piece(width),
                fixed_block(weight.shape),
                fixed_block((ch, MAPS)),
                fixed_block((8, ch)),
            ],
            scratch_shapes=[
                pltpu.VMEM((rows, t + 16, ch), F32),
                pltpu.VMEM((CONV - 1, rows, t + 8, ch), F32),
                pltpu.VMEM((rows * t, MAPS), F32),
                pltpu.VMEM((rows * t, ch), BF),
            ],
        ),
        out_shape=[
            large((2, 4, rows, seg, width), BF),
            large((2, 4, rows, seg, width), BF),
            jax.ShapeDtypeStruct(weight.shape, F32),
            jax.ShapeDtypeStruct((ch, MAPS), F32),
            jax.ShapeDtypeStruct((8, ch), F32),
        ],
        compiler_params=params(1),
        cost_estimate=pl.CostEstimate(flops=1, bytes_accessed=1, transcendentals=0),
        name="tail",
    )(starts, own, near, far, conv, gxs, ggate, x, x, normed, weight, conv_w, conv_b, xproj, *after)


def cross(v, bits):
    return lax.ppermute(v, "seq", [(s, s ^ bits) for s in range(16)])


def swap_row(v):
    return lax.ppermute(v, "row", [(0, 1), (1, 0)])


def total_of_all(v):
    v = v + swap_row(v)
    for bits in (1, 2, 4, 8):
        v = v + cross(v, bits)
    return v


def sum_pieces(keep, send, sent, others):
    (acc,) = gate([keep.astype(F32) + cross(send, 1).astype(F32)], others)
    acc = acc[0] + cross(acc[1].astype(sent), 2).astype(F32)
    total = acc[0]
    for k in (1, 2, 3):
        total = total + cross(acc[k].astype(sent), 4 * k).astype(F32)
    return total


def spread_pieces(own_piece):
    line = jnp.stack([own_piece] + [cross(own_piece, 4 * k) for k in (1, 2, 3)])
    near = jnp.stack([line, cross(line, 2)])
    return near, cross(near, 1)


def gather_tokens(v):
    return lax.all_gather(v, "seq", axis=1, tiled=True)


def up(v):
    return v.astype(F32)


class Sum:
    def __init__(self, keep, send):
        self.keep, self.near = keep, cross(send, 1)
        self.head = keep.shape[2] - keep.shape[2] // 3

    def part(self, *at):
        return up(self.keep[at]) + up(self.near[at])

    def first(self, others):
        (self.near,) = gate([self.near], others)
        a, b = slice(0, self.head), slice(self.head, None)
        sent = [self.part(1, slice(None), a).astype(BF)]
        sent += [self.part(slice(None), k, b).astype(BF) for k in (1, 2, 3)]
        self.second_of = [cross(sent[0], 2), *cross_z(sent[1:])]
        return sent

    def second(self, others):
        across, *line = gate(self.second_of, others)
        a, b = slice(0, self.head), slice(self.head, None)
        sent = [(self.part(0, k, a) + up(across[k])).astype(BF) for k in (1, 2, 3)]
        sent.append((self.part(1, 0, b) + sum(up(v[1]) for v in line)).astype(BF))
        self.third_of = [*cross_z(sent[:3]), cross(sent[3], 2)]
        self.a = self.part(0, 0, a) + up(across[0])
        self.b = self.part(0, 0, b) + sum(up(v[0]) for v in line)
        return sent

    def third(self, others):
        *line, across = gate(self.third_of, others)
        return jnp.concatenate([self.a + sum(up(v) for v in line), self.b + up(across)])


def cross_z(pieces):
    return [cross(v, 4 * k) for k, v in zip((1, 2, 3), pieces)]


def channel_plan(
    hidden_in, grad_out, doc_starts, norm_gain, in_proj, out_proj, conv_weight, conv_bias,
    x_proj, dt_proj, dt_bias, decay_log, skip_scale,
):
    row_count, seg_len, width = hidden_in.shape
    shards = lax.axis_size("seq")
    full_len = seg_len * shards
    ch = conv_weight.shape[1]
    first = lax.axis_index("row") == 0
    both = ("seq", "row")
    place = 2 * lax.axis_index("seq") + lax.axis_index("row")
    own = own_place()
    gain_len = norm_gain.shape[0]

    hid = gather_tokens(hidden_in)
    gout = gather_tokens(grad_out)
    to_shard = [(i, 2 * (i % shards) + i // shards) for i in range(2 * shards)]
    mine = lax.ppermute(in_proj, both, to_shard)
    other = swap_row(mine)
    weight = jnp.concatenate([jnp.where(first, mine, other), jnp.where(first, other, mine)])
    other = swap_row(out_proj)
    pair = jnp.concatenate([jnp.where(first, out_proj, other), jnp.where(first, other, out_proj)])
    out_cols = lax.all_to_all(pair, "seq", split_axis=1, concat_axis=0, tiled=True)
    spot = jnp.zeros((2 * shards, gain_len), F32)
    spot = lax.dynamic_update_slice(spot, norm_gain.astype(F32)[None], (place, 0))
    gain_whole = total_of_all(spot).reshape(1, width)
    vectors = [
        conv_weight.astype(F32),
        conv_bias.astype(F32)[None],
        dt_bias.astype(F32)[None],
        decay_log.astype(F32),
        skip_scale.astype(F32)[None],
        widened(dt_proj),
        x_proj,
    ]
    weight, gain_whole, out_cols, *vectors = gate([weight, gain_whole, out_cols, *vectors], [])
    conv_w, conv_b, dtb, decay, skip, wide, x_proj = vectors

    normed, x, z, conv, keep, send = front(
        doc_starts, own, hid, gain_whole, weight, conv_w, conv_b, x_proj
    )
    low = sum_pieces(keep, send, F32, []).astype(BF)
    near, far = spread_pieces(low)
    gated, y, states, mixed, last, stats = forward_scan(
        [], doc_starts, own, near, far, dt_proj, dtb, decay, skip, conv, z, out_cols
    )
    mixed = lax.psum_scatter(mixed, "seq", scatter_dimension=1, tiled=True)
    passed = [jnp.zeros((DT_RANK, ch), F32), jnp.zeros((24, ch), F32), jnp.zeros_like(last), last]
    ggate, gxs, keep, send, gdtproj, misc, _, _ = backward_scan(
        7, 8, [], ([], passed), doc_starts, own, near, far, dt_proj, dtb, decay, skip, conv, z, y,
        gout, out_cols, states, wide,
    )
    keep, send, gated = gate([keep, send, gated], [])
    low = sum_pieces(keep, send, BF, []).astype(BF)
    gout_cols = jnp.einsum("rtd,rtc->dc", gout, gated, preferred_element_type=F32)
    parts = gout_cols.reshape(shards, 2, width // (2 * shards), ch)
    keep = jnp.where(first, parts[:, 0], parts[:, 1])
    send = jnp.where(first, parts[:, 1], parts[:, 0])
    out_half = (keep + swap_row(send)).astype(BF)
    near, far = spread_pieces(low)
    keep, send, gin, gxproj, cmisc = tail(
        [out_half], doc_starts, own, near, far, conv, gxs, ggate, x, normed, weight, conv_w, conv_b,
        x_proj,
    )
    gnormed = Sum(keep, send)
    gnormed.first([])
    held = [gin, gdtproj, misc, stats, cmisc, gxproj]
    gin, gdtproj, misc, stats, cmisc, gxproj = gate(held, [gnormed.second_of[1]])
    grad_gain = jnp.sum(weight.astype(F32) * gin, axis=0) / gain_whole[0]
    grad_gain = grad_gain.reshape(2 * shards, gain_len)
    grad_gain = grad_gain + swap_row(grad_gain)
    grad_gain = grad_gain + cross(grad_gain, 1)
    keep = jnp.where(first, gin[:ch], gin[ch:])
    send = jnp.where(first, gin[ch:], gin[:ch])
    in_half = (keep + swap_row(send.astype(BF)).astype(F32)).astype(BF)
    small = jnp.concatenate([gdtproj, misc, stats, cmisc, jnp.transpose(gxproj)])
    small = small + swap_row(small)
    gnormed.second([in_half, small, grad_gain])
    grad_gain, out_half = gate([grad_gain, out_half], [gnormed.third_of[0]])
    out_share = lax.all_to_all(out_half, "seq", split_axis=0, concat_axis=0, tiled=True)
    grad_gain = grad_gain + cross(grad_gain, 2)
    *gnormed.third_of, grad_gain = gate([*gnormed.third_of, grad_gain], [])
    gnormed = gnormed.third([])
    in_half, grad_gain = gate([in_half, grad_gain], [gnormed])
    to_owner = [(b, a) for a, b in to_shard]
    in_share = lax.ppermute(in_half, both, to_owner).astype(F32)
    grad_gain = grad_gain + sum(cross_z([grad_gain] * 3))
    out_share = jnp.transpose(out_share.astype(F32), (1, 0, 2)).reshape(width // (2 * shards), E)

    residual = hidden_in.astype(F32)
    hidden_out = (residual + mixed.astype(F32)).astype(BF)
    inv_rms = lax.rsqrt(jnp.mean(residual * residual, axis=-1, keepdims=True) + eps_norm)
    scaled = residual * inv_rms
    grad_scaled = gnormed * gain_whole
    grad_hidden = grad_out.astype(F32) + inv_rms * (
        grad_scaled - scaled * jnp.mean(grad_scaled * scaled, axis=-1, keepdims=True)
    )
    grad_gain = lax.dynamic_slice(grad_gain, (place, 0), (1, gain_len))[0]
    gdtproj, misc, stats, cmisc, gxproj = jnp.split(
        small, [DT_RANK, DT_RANK + 24, DT_RANK + 32, DT_RANK + 40]
    )
    token_count = full_len * row_count * 2
    mean_off = stats[0] / token_count
    spread = jnp.sqrt(stats[1] / token_count - mean_off * mean_off + eps_spread)
    centre = jnp.log(jax.nn.softplus(dt_bias.astype(F32)))
    return (
        hidden_out,
        grad_hidden,
        grad_gain,
        in_share,
        out_share,
        cmisc[:CONV],
        cmisc[CONV],
        jnp.transpose(gxproj),
        gdtproj,
        misc[NSTATE],
        misc[:NSTATE],
        misc[NSTATE + 1],
        jnp.stack([centre + mean_off, spread]),
    )


block_len = 16


def lagged(values, offset, filler):
    if offset == 0:
        return values
    widths = [(0, 0)] * values.ndim
    widths[1] = (offset, 0)
    return jnp.pad(values, widths, constant_values=filler)[:, : values.shape[1]]


def leading(values, offset):
    if offset == 0:
        return values
    widths = [(0, 0)] * values.ndim
    widths[1] = (0, offset)
    return jnp.pad(values, widths)[:, offset:]


def slope_of_silu(values):
    logistic = jax.nn.sigmoid(values)
    return logistic * (1.0 + values * (1.0 - logistic))


def block_scan(decay_rates, dt_row, x_row, b_row, c_row, keep_row):
    length, channels = dt_row.shape
    blocks = length // block_len

    def regroup(values):
        grouped = values.reshape((blocks, block_len) + values.shape[1:])
        return jnp.moveaxis(grouped, 0, -1)

    dt_q, x_q, b_q, c_q, keep_q = (regroup(v) for v in (dt_row, x_row, b_row, c_row, keep_row))

    def decay_at(dt_now, keep_now):
        return jnp.exp(dt_now[None, :, :] * decay_rates[:, :, None]) * keep_now[None, None, :]

    def local_pass(running, inputs):
        state_now, product = running
        dt_now, x_now, b_now, keep_now = inputs
        decay_now = decay_at(dt_now, keep_now)
        state_now = decay_now * state_now + b_now[:, None, :] * (dt_now * x_now)[None, :, :]
        return ((state_now, decay_now * product), None)

    empty_state = jnp.zeros((NSTATE, channels, blocks), jnp.float32)
    (block_ends, block_decay), _ = lax.scan(
        local_pass, (empty_state, jnp.ones_like(empty_state)), (dt_q, x_q, b_q, keep_q)
    )

    def combine(earlier, later):
        return (earlier[0] * later[0], later[0] * earlier[1] + later[1])

    _, reached = lax.associative_scan(combine, (block_decay, block_ends), axis=2)
    starting = jnp.concatenate([jnp.zeros_like(reached[:, :, :1]), reached[:, :, :-1]], axis=2)

    def full_pass(state_now, inputs):
        dt_now, x_now, b_now, c_now, keep_now = inputs
        state_now = (
            decay_at(dt_now, keep_now) * state_now
            + b_now[:, None, :] * (dt_now * x_now)[None, :, :]
        )
        return (state_now, jnp.sum(c_now[:, None, :] * state_now, axis=0))

    _, outputs = lax.scan(full_pass, starting, (dt_q, x_q, b_q, c_q, keep_q))
    return jnp.moveaxis(outputs, 2, 0).reshape(length, channels)


def scan_all(dt_vals, x_vals, b_vals, c_vals, decay_full, skip_full, keep_mask):
    decay_rates = -jnp.exp(decay_full)
    per_row = jax.checkpoint(block_scan)

    def one_row(row_items):
        return per_row(decay_rates, *row_items)

    outputs = lax.map(one_row, (dt_vals, x_vals, b_vals, c_vals, keep_mask))
    return outputs + skip_full * x_vals


def token_plan(
    hidden_in,
    grad_out,
    doc_starts,
    norm_gain,
    in_proj,
    out_proj,
    conv_weight,
    conv_bias,
    x_proj,
    dt_proj,
    dt_bias,
    decay_log,
    skip_scale,
):
    row_count, seg_len, model_width = hidden_in.shape
    full_len = seg_len * lax.axis_size("seq")
    gain_whole, in_whole, out_whole = (
        lax.all_gather(norm_gain, ("seq", "row"), axis=0, tiled=True),
        lax.all_gather(in_proj, ("seq", "row"), axis=0, tiled=True),
        lax.all_gather(out_proj, ("seq", "row"), axis=0, tiled=True),
    )
    residual = hidden_in.astype(jnp.float32)
    inv_rms = lax.rsqrt(jnp.mean(residual * residual, axis=-1, keepdims=True) + eps_norm)
    scaled = residual * inv_rms
    gain_full = gain_whole.astype(jnp.float32)
    normed = (scaled * gain_full).astype(jnp.bfloat16)
    proj_in = jnp.einsum("rtd,fd->rtf", normed, in_whole, preferred_element_type=jnp.float32)
    x_tokens = proj_in[..., :E].astype(jnp.bfloat16)
    gate_z = proj_in[..., E:]
    x_chan = lax.all_to_all(x_tokens, "seq", split_axis=2, concat_axis=1, tiled=True)
    positions = lax.broadcasted_iota(jnp.int32, (1, full_len, 1), 1)
    doc_ids = jnp.sum((doc_starts[:, None, :] <= positions).astype(jnp.int32), axis=2) - 1
    same_docs = [
        (lagged(doc_ids, offset, -1) == doc_ids).astype(jnp.float32)[..., None]
        for offset in range(CONV)
    ]
    keep_mask = same_docs[1][..., 0]
    x_vals = x_chan.astype(jnp.float32)
    conv_full = conv_weight.astype(jnp.float32)
    pre_conv = conv_bias.astype(jnp.float32) + jnp.zeros_like(x_vals)
    for offset in range(CONV):
        pre_conv = (
            pre_conv
            + conv_full[CONV - 1 - offset] * lagged(x_vals, offset, 0.0) * same_docs[offset]
        )
    conv_low = jax.nn.silu(pre_conv).astype(jnp.bfloat16)
    part_sums = jnp.einsum("rtc,cm->rtm", conv_low, x_proj, preferred_element_type=jnp.float32)
    dtbc = lax.psum(part_sums, "seq").astype(jnp.bfloat16)
    dt_low = dtbc[..., :DT_RANK]
    b_vals = dtbc[..., DT_RANK : DT_RANK + NSTATE].astype(jnp.float32)
    c_vals = dtbc[..., DT_RANK + NSTATE :].astype(jnp.float32)
    pre_dt = jnp.einsum(
        "rtk,kc->rtc", dt_low, dt_proj, preferred_element_type=jnp.float32
    ) + dt_bias.astype(jnp.float32)
    dt_vals = jax.nn.softplus(pre_dt)
    y_vals, pullback = jax.vjp(
        partial(scan_all, keep_mask=keep_mask),
        dt_vals,
        conv_low.astype(jnp.float32),
        b_vals,
        c_vals,
        decay_log.astype(jnp.float32),
        skip_scale.astype(jnp.float32),
    )
    y_tokens = lax.all_to_all(
        y_vals.astype(jnp.bfloat16), "seq", split_axis=1, concat_axis=2, tiled=True
    )
    y_token_vals = y_tokens.astype(jnp.float32)
    gate_act = jax.nn.silu(gate_z)
    gated = (y_token_vals * gate_act).astype(jnp.bfloat16)
    mixed = jnp.einsum("rte,de->rtd", gated, out_whole, preferred_element_type=jnp.float32)
    hidden_out = (residual + mixed).astype(jnp.bfloat16)
    grad_out_proj = jnp.einsum("rtd,rte->de", grad_out, gated, preferred_element_type=jnp.float32)
    grad_gated = jnp.einsum("rtd,de->rte", grad_out, out_whole, preferred_element_type=jnp.float32)
    grad_y = (grad_gated * gate_act).astype(jnp.bfloat16)
    grad_gate = (grad_gated * y_token_vals * slope_of_silu(gate_z)).astype(jnp.bfloat16)
    grad_y_chan = lax.all_to_all(grad_y, "seq", split_axis=2, concat_axis=1, tiled=True)
    grad_dt_scan, grad_x_scan, grad_b, grad_c, grad_decay, grad_skip = pullback(
        grad_y_chan.astype(jnp.float32)
    )
    grad_pre_dt = (grad_dt_scan * jax.nn.sigmoid(pre_dt)).astype(jnp.bfloat16)
    grad_dt_low = jnp.einsum(
        "rtc,kc->rtk", grad_pre_dt, dt_proj, preferred_element_type=jnp.float32
    )
    grad_dt_proj = jnp.einsum(
        "rtk,rtc->kc", dt_low, grad_pre_dt, preferred_element_type=jnp.float32
    )
    grad_dt_bias = jnp.sum(grad_pre_dt.astype(jnp.float32), axis=(0, 1))
    grad_parts = jnp.concatenate([grad_dt_low, grad_b, grad_c], axis=-1)
    grad_share = lax.psum_scatter(grad_parts, "seq", scatter_dimension=1, tiled=True)
    grad_dtbc = lax.all_gather(grad_share.astype(jnp.bfloat16), "seq", axis=1, tiled=True)
    grad_x_proj = jnp.einsum("rtc,rtm->cm", conv_low, grad_dtbc, preferred_element_type=jnp.float32)
    grad_conv_out = grad_x_scan + jnp.einsum(
        "rtm,cm->rtc", grad_dtbc, x_proj, preferred_element_type=jnp.float32
    )
    grad_pre_conv = grad_conv_out * slope_of_silu(pre_conv)
    grad_conv_bias = jnp.sum(grad_pre_conv, axis=(0, 1))
    conv_rows = [None] * CONV
    grad_x = jnp.zeros_like(grad_pre_conv)
    for offset in range(CONV):
        masked = grad_pre_conv * same_docs[offset]
        conv_rows[CONV - 1 - offset] = jnp.sum(masked * lagged(x_vals, offset, 0.0), axis=(0, 1))
        grad_x = grad_x + conv_full[CONV - 1 - offset] * leading(masked, offset)
    grad_conv_weight = jnp.stack(conv_rows)
    grad_x_tokens = lax.all_to_all(
        grad_x.astype(jnp.bfloat16), "seq", split_axis=1, concat_axis=2, tiled=True
    )
    grad_proj = jnp.concatenate([grad_x_tokens, grad_gate], axis=-1)
    grad_in_proj = jnp.einsum("rtf,rtd->fd", grad_proj, normed, preferred_element_type=jnp.float32)
    grad_normed = jnp.einsum("rtf,fd->rtd", grad_proj, in_whole, preferred_element_type=jnp.float32)
    grad_gain = jnp.sum(grad_normed * scaled, axis=(0, 1))
    grad_scaled = grad_normed * gain_full
    grad_hidden = grad_out.astype(jnp.float32) + inv_rms * (
        grad_scaled - scaled * jnp.mean(grad_scaled * scaled, axis=-1, keepdims=True)
    )
    gain_share, in_share, out_share = (
        lax.psum_scatter(grad_gain, ("seq", "row"), scatter_dimension=0, tiled=True),
        lax.psum_scatter(grad_in_proj, ("seq", "row"), scatter_dimension=0, tiled=True),
        lax.psum_scatter(grad_out_proj, ("seq", "row"), scatter_dimension=0, tiled=True),
    )
    centre = jnp.log(jax.nn.softplus(dt_bias.astype(jnp.float32)))
    offset_dt = jnp.log(dt_vals) - centre
    first_sum = jnp.sum(offset_dt, axis=(0, 1))
    second_sum = jnp.sum(offset_dt * offset_dt, axis=(0, 1))
    summed = lax.psum(
        (
            grad_conv_weight,
            grad_conv_bias,
            grad_x_proj,
            grad_dt_proj,
            grad_dt_bias,
            grad_decay,
            grad_skip,
            first_sum,
            second_sum,
        ),
        "row",
    )
    token_count = full_len * row_count * lax.axis_size("row")
    mean_off = summed[7] / token_count
    spread = jnp.sqrt(summed[8] / token_count - mean_off * mean_off + eps_spread)
    dt_stats = jnp.stack([centre + mean_off, spread])
    return (
        hidden_out,
        grad_hidden,
        gain_share,
        in_share,
        out_share,
        summed[0],
        summed[1],
        summed[2],
        summed[3],
        summed[4],
        summed[5],
        summed[6],
        dt_stats,
    )


def solution(mesh):
    fits = mesh.shape["seq"] == 16 and mesh.shape["row"] == 2
    plan = channel_plan if fits else token_plan
    return jax.shard_map(
        plan,
        mesh=mesh,
        in_specs=(
            P("row", "seq", None),
            P("row", "seq", None),
            P("row", None),
            P(("seq", "row")),
            P(("seq", "row"), None),
            P(("seq", "row"), None),
            P(None, "seq"),
            P("seq"),
            P("seq", None),
            P(None, "seq"),
            P("seq"),
            P(None, "seq"),
            P("seq"),
        ),
        out_specs=(
            P("row", "seq", None),
            P("row", "seq", None),
            P(("seq", "row")),
            P(("seq", "row"), None),
            P(("seq", "row"), None),
            P(None, "seq"),
            P("seq"),
            P("seq", None),
            P(None, "seq"),
            P("seq"),
            P(None, "seq"),
            P("seq"),
            P(None, "seq"),
        ),
        check_vma=False,
    )
```

```python
from functools import partial

import jax
import jax.numpy as jnp
from jax import lax
from jax.experimental import pallas as pl
from jax.experimental.pallas import tpu as pltpu
from jax.sharding import PartitionSpec as P

E = 2048
NSTATE = 16
CONV = 4
DT_RANK = 64
MAPS = DT_RANK + 2 * NSTATE

eps_norm = 1e-05
eps_spread = 1e-06
BF = jnp.bfloat16
F32 = jnp.float32
LOG2E = 1.4426950408889634
FAR = 1e4
LANES = 128
VMEM = 28 << 20


def params(dims=2):
    return pltpu.CompilerParams(
        dimension_semantics=("arbitrary",) * dims, vmem_limit_bytes=VMEM
    )


def place_in_doc(starts_ref, row, first, count):
    pos = lax.broadcasted_iota(jnp.int32, (count, LANES), 0) + first
    base = jnp.zeros_like(pos)
    for j in range(1, starts_ref.shape[1]):
        start = starts_ref[row, j]
        base = jnp.where(pos >= start, start, base)
    return pos - base


def large(shape, dtype):
    return pltpu.HBM(shape, dtype)


def still(*values):
    return [pltpu.with_memory_space_constraint(v, pltpu.HBM) for v in values]


def sigmoid(v):
    return 1.0 / (1.0 + jnp.exp2(v * -LOG2E))


def silu_slope(v):
    s = sigmoid(v)
    return s * (1.0 + v * (1.0 - s))


def softplus(v):
    return jnp.maximum(v, 0.0) + jnp.log1p(jnp.exp2(jnp.abs(v) * -LOG2E))


def dot(a, b, dims):
    return lax.dot_general(a, b, (dims, ((), ())), preferred_element_type=F32)


def own_place():
    s = lax.axis_index("seq")
    return jnp.stack([s // 4, s // 2 % 2, s % 2]).astype(jnp.int32)


def gate_kernel(*refs):
    pass


def gate(values, others):
    place = pl.BlockSpec(memory_space=pl.ANY)
    return pl.pallas_call(
        gate_kernel,
        in_specs=[place] * (len(values) + len(others)),
        out_specs=[place] * len(values),
        out_shape=[jax.ShapeDtypeStruct(v.shape, v.dtype) for v in values],
        input_output_aliases={i: i for i in range(len(values))},
        compiler_params=pltpu.CompilerParams(vmem_limit_bytes=1 << 16),
        cost_estimate=pl.CostEstimate(flops=1, bytes_accessed=1, transcendentals=0),
        name="gate",
    )(*values, *others)


def put_pieces(own, value, keep, send):
    rows, seg = keep.shape[2], keep.shape[3]
    first = own[2] == 0
    for r in range(rows):
        for x in range(2):
            at = (r * 4 + 2 * x) * seg
            even, odd = value[at : at + seg], value[at + seg : at + 2 * seg]
            keep[x ^ own[1], 0, r] = jnp.where(first, even, odd).astype(keep.dtype)
            send[x ^ own[1], 0, r] = jnp.where(first, odd, even).astype(send.dtype)


def take_pieces(own, near, far, out):
    rows, seg = near.shape[2], near.shape[3]
    first = own[2] == 0
    for r in range(rows):
        for x in range(2):
            at = (r * 4 + 2 * x) * seg
            a = near[x ^ own[1], 0, r].astype(F32)
            b = far[x ^ own[1], 0, r].astype(F32)
            out[at : at + seg, :] = jnp.where(first, a, b)
            out[at + seg : at + 2 * seg, :] = jnp.where(first, b, a)


def pieces_spec(rows, seg, n, at):
    return pl.BlockSpec((2, 1, rows, seg, n), lambda c, s, o: (0, at(c) ^ o[0], 0, 0, 0))


def fixed_block(shape):
    return pl.BlockSpec(shape, lambda c, s, o: (0,) * len(shape))


def front_kernel(
    starts, own, hid, gain, weight, conv_w, conv_b, xproj,
    normed_o, x_o, z_o, conv_o, keep_o, send_o,
    xs,
):
    c = pl.program_id(0)
    rows, t, ch = x_o.shape
    width = normed_o.shape[2]

    @pl.when(c == 0)
    def _():
        xs[:, 0:8, :] = jnp.zeros((rows, 8, ch), F32)

    @pl.when(c > 0)
    def _():
        xs[:, 0:8, :] = xs[:, t : t + 8, :]

    res = hid[...].reshape(rows * t, width).astype(F32)
    inv = lax.rsqrt(jnp.mean(res * res, axis=-1, keepdims=True) + eps_norm)
    normed = (res * inv * gain[...]).astype(BF)
    normed_o[...] = normed.reshape(rows, t, width)
    proj = dot(normed, weight[...], ((1,), (1,)))
    z_o[...] = proj[:, ch:].reshape(rows, t, ch)
    x_low = proj[:, :ch].astype(BF).reshape(rows, t, ch)
    x_o[...] = x_low
    xs[:, 8 : 8 + t, :] = x_low.astype(F32)
    for r in range(rows):
        place = place_in_doc(starts, r, c * t, t)
        pre = conv_b[...] + conv_w[CONV - 1 : CONV, :] * xs[r, 8 : 8 + t, :]
        for k in range(1, CONV):
            lag = conv_w[CONV - 1 - k : CONV - k, :] * xs[r, 8 - k : 8 - k + t, :]
            pre = pre + jnp.where(place >= k, lag, 0.0)
        conv_o[r] = (pre * sigmoid(pre)).astype(BF)
    conv = conv_o[...].reshape(rows * t, ch)
    put_pieces(own, dot(conv, xproj[...], ((1,), (0,))), keep_o, send_o)


def front(starts, own, hid, gain, weight, conv_w, conv_b, xproj):
    (hid,) = still(hid)
    rows, length, width = hid.shape
    ch = conv_w.shape[1]
    t = length // 4
    seg = t // 4
    tok = lambda n: pl.BlockSpec((rows, t, n), lambda c, s, o: (0, c, 0))
    piece = pieces_spec(rows, seg, MAPS, lambda c: c)
    return pl.pallas_call(
        front_kernel,
        grid_spec=pltpu.PrefetchScalarGridSpec(
            num_scalar_prefetch=2,
            grid=(length // t,),
            in_specs=[
                tok(width),
                fixed_block(gain.shape),
                fixed_block(weight.shape),
                fixed_block(conv_w.shape),
                fixed_block(conv_b.shape),
                fixed_block(xproj.shape),
            ],
            out_specs=[tok(width), tok(ch), tok(ch), tok(ch), piece, piece],
            scratch_shapes=[pltpu.VMEM((rows, t + 8, ch), F32)],
        ),
        out_shape=[
            large((rows, length, width), BF),
            large((rows, length, ch), BF),
            large((rows, length, ch), F32),
            large((rows, length, ch), BF),
            jax.ShapeDtypeStruct((2, 4, rows, seg, MAPS), F32),
            jax.ShapeDtypeStruct((2, 4, rows, seg, MAPS), F32),
        ],
        compiler_params=params(1),
        cost_estimate=pl.CostEstimate(flops=1, bytes_accessed=1, transcendentals=0),
        name="front",
    )(starts, own, hid, gain, weight, conv_w, conv_b, xproj)


def maps_across(low):
    pick = lax.broadcasted_iota(jnp.int32, (2 * NSTATE, MAPS), 0) + DT_RANK
    pick = (pick == lax.broadcasted_iota(jnp.int32, (2 * NSTATE, MAPS), 1)).astype(BF)
    return dot(pick, low, ((1,), (1,)))


def half_spec(rows, seg, n, at):
    return pl.BlockSpec(
        (1, 1, rows, seg, n),
        lambda c, s, o: (at(c) % 2 ^ o[1], at(c) // 2 ^ o[0], 0, 0, 0),
    )


def put_halves(own, value, keep, send):
    rows, seg = keep.shape[2], keep.shape[3]
    first = own[2] == 0
    for r in range(rows):
        even = value[2 * r * seg : (2 * r + 1) * seg]
        odd = value[(2 * r + 1) * seg : (2 * r + 2) * seg]
        keep[0, 0, r] = jnp.where(first, even, odd).astype(keep.dtype)
        send[0, 0, r] = jnp.where(first, odd, even).astype(send.dtype)


def take_halves(own, near, far, out):
    rows, seg = near.shape[2], near.shape[3]
    first = own[2] == 0
    for r in range(rows):
        a = near[0, 0, r].astype(F32)
        b = far[0, 0, r].astype(F32)
        out[2 * r * seg : (2 * r + 1) * seg, :] = jnp.where(first, a, b)
        out[(2 * r + 1) * seg : (2 * r + 2) * seg, :] = jnp.where(first, b, a)


def fold(parts):
    row = lax.broadcasted_iota(jnp.int32, parts[0].shape, 0)
    upper = row < 4
    parts = [
        jnp.where(upper, a, b) + pltpu.roll(jnp.where(upper, b, a), 4, 0)
        for a, b in zip(parts[:4], parts[4:])
    ]
    for step in (2, 1):
        half = len(parts) // 2
        upper = row & step == 0
        parts = [
            jnp.where(upper, a + pltpu.roll(a, 8 - step, 0), b + pltpu.roll(b, step, 0))
            for a, b in zip(parts[:half], parts[half:])
        ]
    return parts[0]


def spread_maps(low, first, out):
    count, ch = low.shape[0], out.shape[1]
    pick = lax.broadcasted_iota(jnp.int32, (MAPS, NSTATE * ch), 1) // ch + first
    pick = (pick == lax.broadcasted_iota(jnp.int32, (MAPS, NSTATE * ch), 0)).astype(BF)
    wide = dot(low, pick, ((1,), (0,)))
    for b in range(count // 8):
        for n in range(NSTATE):
            row = (b * NSTATE + n) * 8
            out[row : row + 8, :] = wide[b * 8 : b * 8 + 8, n * ch : (n + 1) * ch]


def forward_kernel(starts, own, near, far, dtproj, dtbias, decay, skip, conv, z, cols, *refs):
    (
        gated_o, y_o, states_o, mixed_o, last_o, stats_o,
        state, dtk_s, dtx_s, y_s, across_s, low_s, cm_s,
    ) = refs[-13:]
    c = pl.program_id(0)
    rows, t, ch = conv.shape

    @pl.when(c == 0)
    def _():
        state[...] = jnp.zeros_like(state)
        stats_o[...] = jnp.zeros_like(stats_o)

    rate = -LOG2E * jnp.exp(decay[...])
    take_halves(own, near, far, low_s)
    low = low_s[...].astype(BF)
    dt = softplus(dot(low[:, :DT_RANK], dtproj[...], ((1,), (0,))) + dtbias[...])
    off = jnp.log(dt) - jnp.log(softplus(dtbias[...]))
    stats_o[0:1, :] += jnp.sum(off, axis=0, keepdims=True)
    stats_o[1:2, :] += jnp.sum(off * off, axis=0, keepdims=True)
    x = conv[...].astype(F32).reshape(rows * t, ch)
    for r in range(rows):
        place = place_in_doc(starts, r, c * t, t)
        dtk_s[r * t : (r + 1) * t, :] = jnp.where(place >= 1, dt[r * t : (r + 1) * t], FAR)
    dtx_s[...] = dt * x
    across_s[...] = maps_across(low)
    spread_maps(low, DT_RANK + NSTATE, cm_s)

    def every_step(states):
        states, sums = list(states), [None] * rows
        maps = [across_s[:, r * t : (r + 1) * t] for r in range(rows)]
        for i in range(t):
            for r in range(rows):
                if i % 8 == 0:
                    sums[r] = []
                at = r * t + i
                s = states[r]
                a = jnp.exp2(dtk_s[pl.ds(at, 1), :] * rate)
                states_o[r, i] = s
                b = jnp.broadcast_to(maps[r][:NSTATE, i : i + 1], (NSTATE, ch))
                s = a * s + dtx_s[pl.ds(at, 1), :] * b
                ys = s * cm_s[pl.ds(at // 8 * 8 * NSTATE + at % 8, NSTATE, stride=8), :]
                sums[r].append(ys[:8] + ys[8:])
                if i % 8 == 7:
                    y_s[pl.ds(r * t + i - 7, 8), :] = fold(sums[r])
                states[r] = s
        return tuple(states)

    states = every_step(tuple(state[r] for r in range(rows)))
    for r in range(rows):
        state[r] = states[r]
        last_o[r] = states[r]
    y_low = (y_s[...] + skip[...] * x).astype(BF)
    y_o[...] = y_low.reshape(rows, t, ch)
    zz = z[...].reshape(rows * t, ch)
    gated = (y_low.astype(F32) * (zz * sigmoid(zz))).astype(BF)
    gated_o[...] = gated.reshape(rows, t, ch)
    mixed = dot(gated, cols[...], ((1,), (1,))).astype(BF)
    mixed_o[...] = mixed.reshape(rows, t, cols.shape[0])


def forward_scan(after, starts, own, near, far, dtproj, dtbias, decay, skip, conv, z, cols):
    conv, z = still(conv, z)
    rows, length, ch = conv.shape
    t = length // 8
    seg = t // 2
    tok = lambda n: pl.BlockSpec((rows, t, n), lambda c, s, o: (0, c, 0))
    half = half_spec(rows, seg, MAPS, lambda c: c)
    return pl.pallas_call(
        forward_kernel,
        grid_spec=pltpu.PrefetchScalarGridSpec(
            num_scalar_prefetch=2,
            grid=(length // t,),
            in_specs=[
                half,
                half,
                fixed_block(dtproj.shape),
                fixed_block(dtbias.shape),
                fixed_block(decay.shape),
                fixed_block(skip.shape),
                tok(ch),
                tok(ch),
                fixed_block(cols.shape),
                *[pl.BlockSpec(memory_space=pl.ANY)] * len(after),
            ],
            out_specs=[
                tok(ch),
                tok(ch),
                pl.BlockSpec((rows, t, NSTATE, ch), lambda c, s, o: (0, c, 0, 0)),
                tok(cols.shape[0]),
                fixed_block((rows, NSTATE, ch)),
                fixed_block((8, ch)),
            ],
            scratch_shapes=[
                pltpu.VMEM((rows, NSTATE, ch), F32),
                pltpu.VMEM((rows * t, ch), F32),
                pltpu.VMEM((rows * t, ch), F32),
                pltpu.VMEM((rows * t, ch), F32),
                pltpu.VMEM((2 * NSTATE, rows * t), F32),
                pltpu.VMEM((rows * t, MAPS), F32),
                pltpu.VMEM((rows * t * NSTATE, ch), F32),
            ],
        ),
        out_shape=[
            large((rows, length, ch), BF),
            large((rows, length, ch), BF),
            large((rows, length, NSTATE, ch), F32),
            large((rows, length, cols.shape[0]), BF),
            jax.ShapeDtypeStruct((rows, NSTATE, ch), F32),
            jax.ShapeDtypeStruct((8, ch), F32),
        ],
        compiler_params=params(1),
        cost_estimate=pl.CostEstimate(flops=1, bytes_accessed=1, transcendentals=0),
        name="forward_scan",
    )(starts, own, near, far, dtproj, dtbias, decay, skip, conv, z, cols, *after)


def backward_kernel(
    starts, own, near, far, dtproj, dtbias, decay, skip, conv, z, y, gout, cols, states, wide,
    gdtproj_i, misc_i, back_i, next_i, *refs, top,
):
    (
        ggate_o, gxs_o, keep_o, send_o, gdtproj_o, misc_o, back_o, next_o,
        dtk_s, dt_s, dtx_s, gy_s, p1_s, p2_s, gb_s, gc_s, fold_s, across_s, low_s,
    ) = refs[-19:]
    c = pl.program_id(0)
    rows, t, ch = conv.shape
    count = rows * t

    @pl.when(c == 0)
    def _():
        back_o[...] = back_i[...]
        next_o[...] = next_i[...]
        gdtproj_o[...] = gdtproj_i[...]
        misc_o[...] = misc_i[...]

    neg = -jnp.exp(decay[...])
    rate = LOG2E * neg
    take_halves(own, near, far, low_s)
    low = low_s[...].astype(BF)
    pre = dot(low[:, :DT_RANK], dtproj[...], ((1,), (0,))) + dtbias[...]
    dt = softplus(pre)
    x = conv[...].astype(F32).reshape(count, ch)
    for r in range(rows):
        place = place_in_doc(starts, r, (top - c) * t, t)
        dtk_s[r * t : (r + 1) * t, :] = jnp.where(place >= 1, dt[r * t : (r + 1) * t], FAR)
    dt_s[...] = dt
    dtx_s[...] = dt * x
    zz = z[...].reshape(count, ch)
    ggv = dot(gout[...].reshape(count, gout.shape[2]), cols[...], ((1,), (0,)))
    sg = sigmoid(zz)
    gy = (ggv * (zz * sg)).astype(BF).astype(F32)
    yv = y[...].astype(F32).reshape(count, ch)
    ggate = (ggv * yv * (sg * (1.0 + zz * (1.0 - sg)))).astype(BF)
    ggate_o[...] = ggate.reshape(rows, t, ch)
    gy_s[...] = gy
    across_s[...] = maps_across(low)

    def every_step(carry):
        hs, s_nexts, acc = list(carry[0]), list(carry[1]), carry[2]
        p1s, p2s = [None] * rows, [None] * rows
        maps = [across_s[:, r * t : (r + 1) * t] for r in range(rows)]
        for i in range(t - 1, -1, -1):
            for r in range(rows):
                at = r * t + i
                gyr = gy_s[pl.ds(at, 1), :]
                g = gyr * jnp.broadcast_to(maps[r][NSTATE:, i : i + 1], (NSTATE, ch)) + hs[r]
                h = jnp.exp2(dtk_s[pl.ds(at, 1), :] * rate) * g
                s_prev = states[r, i]
                q = h * s_prev
                acc = acc + q * dt_s[pl.ds(at, 1), :]
                aq = q * neg
                bg = g * jnp.broadcast_to(maps[r][:NSTATE, i : i + 1], (NSTATE, ch))
                if i % 8 == 7:
                    p1s[r], p2s[r] = [], []
                p1s[r].insert(0, bg[:8] + bg[8:])
                p2s[r].insert(0, aq[:8] + aq[8:])
                if i % 8 == 0:
                    whole8 = pl.ds(at, 8)
                    p1_s[whole8, :] = fold(p1s[r])
                    p2_s[whole8, :] = fold(p2s[r])
                tile = pl.ds(at * NSTATE, NSTATE)
                gb_s[tile, :] = (g * dtx_s[pl.ds(at, 1), :]).astype(BF)
                gc_s[tile, :] = (gyr * s_nexts[r]).astype(BF)
                hs[r], s_nexts[r] = h, s_prev
        return tuple(hs), tuple(s_nexts), acc

    hs, s_nexts, acc = every_step(
        (
            tuple(back_o[r] for r in range(rows)),
            tuple(next_o[r] for r in range(rows)),
            jnp.zeros((NSTATE, ch), F32),
        ),
    )
    for r in range(rows):
        back_o[r] = hs[r]
        next_o[r] = s_nexts[r]
    p1, p2 = p1_s[...], p2_s[...]
    gxs_o[...] = (dt * p1 + skip[...] * gy).reshape(rows, t, ch)
    gpre = ((p2 + x * p1) * sigmoid(pre)).astype(BF)
    gdtproj_o[...] += dot(low[:, :DT_RANK], gpre, ((0,), (0,)))
    misc_o[0:NSTATE, :] += neg * acc
    misc_o[NSTATE : NSTATE + 1, :] += jnp.sum(gpre.astype(F32), axis=0, keepdims=True)
    misc_o[NSTATE + 1 : NSTATE + 2, :] += jnp.sum(gy * x, axis=0, keepdims=True)
    ones = jnp.ones((ch, ch), BF)
    entry = lax.broadcasted_iota(jnp.int32, (1, NSTATE, ch), 1) + DT_RANK
    lane = lax.broadcasted_iota(jnp.int32, (1, NSTATE, ch), 2)
    maps = jnp.zeros((count, NSTATE, ch), F32)
    for ref in (gb_s, gc_s):
        every = dot(ref[...], ones, ((1,), (0,))).reshape(count, NSTATE, ch)
        maps = jnp.where(lane == entry, every, maps)
        entry = entry + NSTATE
    fold_s[...] = (maps[:, :8] + maps[:, 8:]).reshape(count * 8, ch)
    total = dot(gpre, wide[...], ((1,), (0,)))
    for j in range(8):
        total = total + fold_s[pl.ds(j, count, stride=8), :][:, :MAPS]
    put_halves(own, total, keep_o, send_o)


def widened(dtproj):
    return jnp.pad(dtproj.T, ((0, 0), (0, 2 * NSTATE)))


def backward_scan(
    top, chunks, after, so_far, starts, own, near, far, dtproj, dtbias, decay, skip, conv, z, y,
    gout, cols, states, wide,
):
    conv, z, y, gout, states = still(conv, z, y, gout, states)
    rows, length, ch = conv.shape
    t = length // 8
    seg = t // 2
    done, passed = so_far
    fixed = 19
    tok = lambda n: pl.BlockSpec((rows, t, n), lambda c, s, o: (0, top - c, 0))
    half = half_spec(rows, seg, MAPS, lambda c: top - c)
    small = [(DT_RANK, ch), (24, ch), (rows, NSTATE, ch), (rows, NSTATE, ch)]
    return pl.pallas_call(
        partial(backward_kernel, top=top),
        grid_spec=pltpu.PrefetchScalarGridSpec(
            num_scalar_prefetch=2,
            grid=(chunks,),
            in_specs=[
                half,
                half,
                fixed_block(dtproj.shape),
                fixed_block(dtbias.shape),
                fixed_block(decay.shape),
                fixed_block(skip.shape),
                tok(ch),
                tok(ch),
                tok(ch),
                tok(gout.shape[2]),
                fixed_block(cols.shape),
                pl.BlockSpec((rows, t, NSTATE, ch), lambda c, s, o: (0, top - c, 0, 0)),
                fixed_block(wide.shape),
                *[fixed_block(s) for s in small],
                *[pl.BlockSpec(memory_space=pl.ANY)] * (len(done) + len(after)),
            ],
            out_specs=[tok(ch), tok(ch), half, half, *[fixed_block(s) for s in small]],
            scratch_shapes=[
                pltpu.VMEM((rows * t, ch), F32),
                pltpu.VMEM((rows * t, ch), F32),
                pltpu.VMEM((rows * t, ch), F32),
                pltpu.VMEM((rows * t, ch), F32),
                pltpu.VMEM((rows * t, ch), F32),
                pltpu.VMEM((rows * t, ch), F32),
                pltpu.VMEM((rows * t * NSTATE, ch), BF),
                pltpu.VMEM((rows * t * NSTATE, ch), BF),
                pltpu.VMEM((rows * t * 8, ch), F32),
                pltpu.VMEM((2 * NSTATE, rows * t), F32),
                pltpu.VMEM((rows * t, MAPS), F32),
            ],
        ),
        out_shape=[
            large((rows, length, ch), BF),
            large((rows, length, ch), F32),
            jax.ShapeDtypeStruct((2, 4, rows, seg, MAPS), F32),
            jax.ShapeDtypeStruct((2, 4, rows, seg, MAPS), F32),
            *[jax.ShapeDtypeStruct(s, F32) for s in small],
        ],
        input_output_aliases={fixed + i: i for i in range(len(done))},
        compiler_params=params(1),
        cost_estimate=pl.CostEstimate(flops=1, bytes_accessed=1, transcendentals=0),
        name="backward_scan",
    )(
        starts, own, near, far, dtproj, dtbias, decay, skip, conv, z, y, gout, cols, states, wide,
        *passed, *done, *after,
    )


def tail_kernel(
    starts, own, near, far, conv, gxs, ggate, x, before, normed, weight, conv_w, conv_b, xproj, *refs
):
    keep_o, send_o, gin_o, gxproj_o, misc_o, xs, gm_s, low_s, gx_s = refs[-9:]
    c = pl.program_id(0)
    chunks = pl.num_programs(0)
    rows, t, ch = conv.shape
    count = rows * t

    @pl.when(c == 0)
    def _():
        gin_o[...] = jnp.zeros_like(gin_o)
        gxproj_o[...] = jnp.zeros_like(gxproj_o)
        misc_o[...] = jnp.zeros_like(misc_o)
        gm_s[:, :, t : t + 8, :] = jnp.zeros((CONV - 1, rows, 8, ch), F32)

    @pl.when(c > 0)
    def _():
        gm_s[:, :, t : t + 8, :] = gm_s[:, :, 0:8, :]

    xs[:, 0:16, :] = before[...].astype(F32)
    xs[:, 16 : 16 + t, :] = x[...].astype(F32)
    take_pieces(own, near, far, low_s)
    low = low_s[...].astype(BF)
    gconv = gxs[...].reshape(count, ch) + dot(low, xproj[...], ((1,), (1,)))
    gxproj_o[...] += dot(conv[...].reshape(count, ch), low, ((0,), (0,)))
    for r in range(rows):
        place = place_in_doc(starts, r, (chunks - 1 - c) * t, t)
        lags = [xs[r, 16 : 16 + t, :]]
        pre = conv_b[...] + conv_w[CONV - 1 : CONV, :] * lags[0]
        for k in range(1, CONV):
            lags.append(jnp.where(place >= k, xs[r, 16 - k : 16 - k + t, :], 0.0))
            pre = pre + conv_w[CONV - 1 - k : CONV - k, :] * lags[k]
        gpre = gconv[r * t : (r + 1) * t] * silu_slope(pre)
        gx = conv_w[CONV - 1 : CONV, :] * gpre
        for k in range(CONV):
            misc_o[CONV - 1 - k : CONV - k, :] += jnp.sum(gpre * lags[k], axis=0, keepdims=True)
            if k:
                gm_s[k - 1, r, 0:t, :] = jnp.where(place >= k, gpre, 0.0)
                gx = gx + conv_w[CONV - 1 - k : CONV - k, :] * gm_s[k - 1, r, k : k + t, :]
        misc_o[CONV : CONV + 1, :] += jnp.sum(gpre, axis=0, keepdims=True)
        gx_s[r * t : (r + 1) * t, :] = gx.astype(BF)
    gproj = jnp.concatenate([gx_s[...], ggate[...].reshape(count, ch)], axis=1)
    gin_o[...] += dot(gproj, normed[...].reshape(count, normed.shape[2]), ((0,), (0,)))
    put_pieces(own, dot(gproj, weight[...], ((1,), (0,))), keep_o, send_o)


def tail(after, starts, own, near, far, conv, gxs, ggate, x, normed, weight, conv_w, conv_b, xproj):
    conv, gxs, ggate, x, normed = still(conv, gxs, ggate, x, normed)
    rows, length, width = normed.shape
    ch = conv.shape[2]
    t = length // 4
    seg = t // 4
    last = length // t - 1
    tok = lambda n: pl.BlockSpec((rows, t, n), lambda c, s, o: (0, last - c, 0))
    piece = lambda n: pieces_spec(rows, seg, n, lambda c: last - c)
    before = pl.BlockSpec(
        (rows, 16, ch), lambda c, s, o: (0, jnp.maximum((last - c) * (t // 16) - 1, 0), 0)
    )
    return pl.pallas_call(
        tail_kernel,
        grid_spec=pltpu.PrefetchScalarGridSpec(
            num_scalar_prefetch=2,
            grid=(length // t,),
            in_specs=[
                piece(MAPS),
                piece(MAPS),
                tok(ch),
                tok(ch),
                tok(ch),
                tok(ch),
                before,
                tok(width),
                fixed_block(weight.shape),
                fixed_block(conv_w.shape),
                fixed_block(conv_b.shape),
                fixed_block(xproj.shape),
                *[pl.BlockSpec(memory_space=pl.ANY)] * len(after),
            ],
            out_specs=[
                piece(width),
                piece(width),
                fixed_block(weight.shape),
                fixed_block((ch, MAPS)),
                fixed_block((8, ch)),
            ],
            scratch_shapes=[
                pltpu.VMEM((rows, t + 16, ch), F32),
                pltpu.VMEM((CONV - 1, rows, t + 8, ch), F32),
                pltpu.VMEM((rows * t, MAPS), F32),
                pltpu.VMEM((rows * t, ch), BF),
            ],
        ),
        out_shape=[
            large((2, 4, rows, seg, width), BF),
            large((2, 4, rows, seg, width), BF),
            jax.ShapeDtypeStruct(weight.shape, F32),
            jax.ShapeDtypeStruct((ch, MAPS), F32),
            jax.ShapeDtypeStruct((8, ch), F32),
        ],
        compiler_params=params(1),
        cost_estimate=pl.CostEstimate(flops=1, bytes_accessed=1, transcendentals=0),
        name="tail",
    )(starts, own, near, far, conv, gxs, ggate, x, x, normed, weight, conv_w, conv_b, xproj, *after)


def cross(v, bits):
    return lax.ppermute(v, "seq", [(s, s ^ bits) for s in range(16)])


def swap_row(v):
    return lax.ppermute(v, "row", [(0, 1), (1, 0)])


def total_of_all(v):
    v = v + swap_row(v)
    for bits in (1, 2, 4, 8):
        v = v + cross(v, bits)
    return v


def sum_pieces(keep, send, sent, others):
    (acc,) = gate([keep.astype(F32) + cross(send, 1).astype(F32)], others)
    acc = acc[0] + cross(acc[1].astype(sent), 2).astype(F32)
    total = acc[0]
    for k in (1, 2, 3):
        total = total + cross(acc[k].astype(sent), 4 * k).astype(F32)
    return total


def spread_pieces(own_piece):
    line = jnp.stack([own_piece] + [cross(own_piece, 4 * k) for k in (1, 2, 3)])
    near = jnp.stack([line, cross(line, 2)])
    return near, cross(near, 1)


def gather_tokens(v):
    return lax.all_gather(v, "seq", axis=1, tiled=True)


def up(v):
    return v.astype(F32)


class Sum:
    def __init__(self, keep, send):
        self.keep, self.near = keep, cross(send, 1)
        self.head = keep.shape[2] - keep.shape[2] // 3

    def part(self, *at):
        return up(self.keep[at]) + up(self.near[at])

    def first(self, others):
        (self.near,) = gate([self.near], others)
        a, b = slice(0, self.head), slice(self.head, None)
        sent = [self.part(1, slice(None), a).astype(BF)]
        sent += [self.part(slice(None), k, b).astype(BF) for k in (1, 2, 3)]
        self.second_of = [cross(sent[0], 2), *cross_z(sent[1:])]
        return sent

    def second(self, others):
        across, *line = gate(self.second_of, others)
        a, b = slice(0, self.head), slice(self.head, None)
        sent = [(self.part(0, k, a) + up(across[k])).astype(BF) for k in (1, 2, 3)]
        sent.append((self.part(1, 0, b) + sum(up(v[1]) for v in line)).astype(BF))
        self.third_of = [*cross_z(sent[:3]), cross(sent[3], 2)]
        self.a = self.part(0, 0, a) + up(across[0])
        self.b = self.part(0, 0, b) + sum(up(v[0]) for v in line)
        return sent

    def third(self, others):
        *line, across = gate(self.third_of, others)
        return jnp.concatenate([self.a + sum(up(v) for v in line), self.b + up(across)])


def cross_z(pieces):
    return [cross(v, 4 * k) for k, v in zip((1, 2, 3), pieces)]


def channel_plan(
    hidden_in, grad_out, doc_starts, norm_gain, in_proj, out_proj, conv_weight, conv_bias,
    x_proj, dt_proj, dt_bias, decay_log, skip_scale,
):
    row_count, seg_len, width = hidden_in.shape
    shards = lax.axis_size("seq")
    full_len = seg_len * shards
    ch = conv_weight.shape[1]
    first = lax.axis_index("row") == 0
    both = ("seq", "row")
    place = 2 * lax.axis_index("seq") + lax.axis_index("row")
    own = own_place()
    gain_len = norm_gain.shape[0]

    hid = gather_tokens(hidden_in)
    gout = gather_tokens(grad_out)
    to_shard = [(i, 2 * (i % shards) + i // shards) for i in range(2 * shards)]
    mine = lax.ppermute(in_proj, both, to_shard)
    other = swap_row(mine)
    weight = jnp.concatenate([jnp.where(first, mine, other), jnp.where(first, other, mine)])
    other = swap_row(out_proj)
    pair = jnp.concatenate([jnp.where(first, out_proj, other), jnp.where(first, other, out_proj)])
    out_cols = lax.all_to_all(pair, "seq", split_axis=1, concat_axis=0, tiled=True)
    spot = jnp.zeros((2 * shards, gain_len), F32)
    spot = lax.dynamic_update_slice(spot, norm_gain.astype(F32)[None], (place, 0))
    gain_whole = total_of_all(spot).reshape(1, width)
    vectors = [
        conv_weight.astype(F32),
        conv_bias.astype(F32)[None],
        dt_bias.astype(F32)[None],
        decay_log.astype(F32),
        skip_scale.astype(F32)[None],
        widened(dt_proj),
        x_proj,
    ]
    weight, gain_whole, out_cols, *vectors = gate([weight, gain_whole, out_cols, *vectors], [])
    conv_w, conv_b, dtb, decay, skip, wide, x_proj = vectors

    normed, x, z, conv, keep, send = front(
        doc_starts, own, hid, gain_whole, weight, conv_w, conv_b, x_proj
    )
    low = sum_pieces(keep, send, F32, []).astype(BF)
    near, far = spread_pieces(low)
    gated, y, states, mixed, last, stats = forward_scan(
        [], doc_starts, own, near, far, dt_proj, dtb, decay, skip, conv, z, out_cols
    )
    mixed = lax.psum_scatter(mixed, "seq", scatter_dimension=1, tiled=True)
    passed = [jnp.zeros((DT_RANK, ch), F32), jnp.zeros((24, ch), F32), jnp.zeros_like(last), last]
    ggate, gxs, keep, send, gdtproj, misc, _, _ = backward_scan(
        7, 8, [], ([], passed), doc_starts, own, near, far, dt_proj, dtb, decay, skip, conv, z, y,
        gout, out_cols, states, wide,
    )
    keep, send, gated = gate([keep, send, gated], [])
    low = sum_pieces(keep, send, BF, []).astype(BF)
    gout_cols = jnp.einsum("rtd,rtc->dc", gout, gated, preferred_element_type=F32)
    parts = gout_cols.reshape(shards, 2, width // (2 * shards), ch)
    keep = jnp.where(first, parts[:, 0], parts[:, 1])
    send = jnp.where(first, parts[:, 1], parts[:, 0])
    out_half = (keep + swap_row(send)).astype(BF)
    near, far = spread_pieces(low)
    keep, send, gin, gxproj, cmisc = tail(
        [out_half], doc_starts, own, near, far, conv, gxs, ggate, x, normed, weight, conv_w, conv_b,
        x_proj,
    )
    gnormed = Sum(keep, send)
    gnormed.first([])
    held = [gin, gdtproj, misc, stats, cmisc, gxproj]
    gin, gdtproj, misc, stats, cmisc, gxproj = gate(held, [gnormed.second_of[1]])
    grad_gain = jnp.sum(weight.astype(F32) * gin, axis=0) / gain_whole[0]
    grad_gain = grad_gain.reshape(2 * shards, gain_len)
    grad_gain = grad_gain + swap_row(grad_gain)
    grad_gain = grad_gain + cross(grad_gain, 1)
    keep = jnp.where(first, gin[:ch], gin[ch:])
    send = jnp.where(first, gin[ch:], gin[:ch])
    in_half = (keep + swap_row(send.astype(BF)).astype(F32)).astype(BF)
    small = jnp.concatenate([gdtproj, misc, stats, cmisc, jnp.transpose(gxproj)])
    small = small + swap_row(small)
    gnormed.second([in_half, small, grad_gain])
    grad_gain, out_half = gate([grad_gain, out_half], [gnormed.third_of[0]])
    out_share = lax.all_to_all(out_half, "seq", split_axis=0, concat_axis=0, tiled=True)
    grad_gain = grad_gain + cross(grad_gain, 2)
    *gnormed.third_of, grad_gain, in_half = gate([*gnormed.third_of, grad_gain, in_half], [])
    gnormed = gnormed.third([])
    to_owner = [(b, a) for a, b in to_shard]
    in_share = lax.ppermute(in_half, both, to_owner).astype(F32)
    grad_gain = grad_gain + sum(cross_z([grad_gain] * 3))
    out_share = jnp.transpose(out_share.astype(F32), (1, 0, 2)).reshape(width // (2 * shards), E)

    residual = hidden_in.astype(F32)
    hidden_out = (residual + mixed.astype(F32)).astype(BF)
    inv_rms = lax.rsqrt(jnp.mean(residual * residual, axis=-1, keepdims=True) + eps_norm)
    scaled = residual * inv_rms
    grad_scaled = gnormed * gain_whole
    grad_hidden = grad_out.astype(F32) + inv_rms * (
        grad_scaled - scaled * jnp.mean(grad_scaled * scaled, axis=-1, keepdims=True)
    )
    grad_gain = lax.dynamic_slice(grad_gain, (place, 0), (1, gain_len))[0]
    gdtproj, misc, stats, cmisc, gxproj = jnp.split(
        small, [DT_RANK, DT_RANK + 24, DT_RANK + 32, DT_RANK + 40]
    )
    token_count = full_len * row_count * 2
    mean_off = stats[0] / token_count
    spread = jnp.sqrt(stats[1] / token_count - mean_off * mean_off + eps_spread)
    centre = jnp.log(jax.nn.softplus(dt_bias.astype(F32)))
    return (
        hidden_out,
        grad_hidden,
        grad_gain,
        in_share,
        out_share,
        cmisc[:CONV],
        cmisc[CONV],
        jnp.transpose(gxproj),
        gdtproj,
        misc[NSTATE],
        misc[:NSTATE],
        misc[NSTATE + 1],
        jnp.stack([centre + mean_off, spread]),
    )


block_len = 16


def lagged(values, offset, filler):
    if offset == 0:
        return values
    widths = [(0, 0)] * values.ndim
    widths[1] = (offset, 0)
    return jnp.pad(values, widths, constant_values=filler)[:, : values.shape[1]]


def leading(values, offset):
    if offset == 0:
        return values
    widths = [(0, 0)] * values.ndim
    widths[1] = (0, offset)
    return jnp.pad(values, widths)[:, offset:]


def slope_of_silu(values):
    logistic = jax.nn.sigmoid(values)
    return logistic * (1.0 + values * (1.0 - logistic))


def block_scan(decay_rates, dt_row, x_row, b_row, c_row, keep_row):
    length, channels = dt_row.shape
    blocks = length // block_len

    def regroup(values):
        grouped = values.reshape((blocks, block_len) + values.shape[1:])
        return jnp.moveaxis(grouped, 0, -1)

    dt_q, x_q, b_q, c_q, keep_q = (regroup(v) for v in (dt_row, x_row, b_row, c_row, keep_row))

    def decay_at(dt_now, keep_now):
        return jnp.exp(dt_now[None, :, :] * decay_rates[:, :, None]) * keep_now[None, None, :]

    def local_pass(running, inputs):
        state_now, product = running
        dt_now, x_now, b_now, keep_now = inputs
        decay_now = decay_at(dt_now, keep_now)
        state_now = decay_now * state_now + b_now[:, None, :] * (dt_now * x_now)[None, :, :]
        return ((state_now, decay_now * product), None)

    empty_state = jnp.zeros((NSTATE, channels, blocks), jnp.float32)
    (block_ends, block_decay), _ = lax.scan(
        local_pass, (empty_state, jnp.ones_like(empty_state)), (dt_q, x_q, b_q, keep_q)
    )

    def combine(earlier, later):
        return (earlier[0] * later[0], later[0] * earlier[1] + later[1])

    _, reached = lax.associative_scan(combine, (block_decay, block_ends), axis=2)
    starting = jnp.concatenate([jnp.zeros_like(reached[:, :, :1]), reached[:, :, :-1]], axis=2)

    def full_pass(state_now, inputs):
        dt_now, x_now, b_now, c_now, keep_now = inputs
        state_now = (
            decay_at(dt_now, keep_now) * state_now
            + b_now[:, None, :] * (dt_now * x_now)[None, :, :]
        )
        return (state_now, jnp.sum(c_now[:, None, :] * state_now, axis=0))

    _, outputs = lax.scan(full_pass, starting, (dt_q, x_q, b_q, c_q, keep_q))
    return jnp.moveaxis(outputs, 2, 0).reshape(length, channels)


def scan_all(dt_vals, x_vals, b_vals, c_vals, decay_full, skip_full, keep_mask):
    decay_rates = -jnp.exp(decay_full)
    per_row = jax.checkpoint(block_scan)

    def one_row(row_items):
        return per_row(decay_rates, *row_items)

    outputs = lax.map(one_row, (dt_vals, x_vals, b_vals, c_vals, keep_mask))
    return outputs + skip_full * x_vals


def token_plan(
    hidden_in,
    grad_out,
    doc_starts,
    norm_gain,
    in_proj,
    out_proj,
    conv_weight,
    conv_bias,
    x_proj,
    dt_proj,
    dt_bias,
    decay_log,
    skip_scale,
):
    row_count, seg_len, model_width = hidden_in.shape
    full_len = seg_len * lax.axis_size("seq")
    gain_whole, in_whole, out_whole = (
        lax.all_gather(norm_gain, ("seq", "row"), axis=0, tiled=True),
        lax.all_gather(in_proj, ("seq", "row"), axis=0, tiled=True),
        lax.all_gather(out_proj, ("seq", "row"), axis=0, tiled=True),
    )
    residual = hidden_in.astype(jnp.float32)
    inv_rms = lax.rsqrt(jnp.mean(residual * residual, axis=-1, keepdims=True) + eps_norm)
    scaled = residual * inv_rms
    gain_full = gain_whole.astype(jnp.float32)
    normed = (scaled * gain_full).astype(jnp.bfloat16)
    proj_in = jnp.einsum("rtd,fd->rtf", normed, in_whole, preferred_element_type=jnp.float32)
    x_tokens = proj_in[..., :E].astype(jnp.bfloat16)
    gate_z = proj_in[..., E:]
    x_chan = lax.all_to_all(x_tokens, "seq", split_axis=2, concat_axis=1, tiled=True)
    positions = lax.broadcasted_iota(jnp.int32, (1, full_len, 1), 1)
    doc_ids = jnp.sum((doc_starts[:, None, :] <= positions).astype(jnp.int32), axis=2) - 1
    same_docs = [
        (lagged(doc_ids, offset, -1) == doc_ids).astype(jnp.float32)[..., None]
        for offset in range(CONV)
    ]
    keep_mask = same_docs[1][..., 0]
    x_vals = x_chan.astype(jnp.float32)
    conv_full = conv_weight.astype(jnp.float32)
    pre_conv = conv_bias.astype(jnp.float32) + jnp.zeros_like(x_vals)
    for offset in range(CONV):
        pre_conv = (
            pre_conv
            + conv_full[CONV - 1 - offset] * lagged(x_vals, offset, 0.0) * same_docs[offset]
        )
    conv_low = jax.nn.silu(pre_conv).astype(jnp.bfloat16)
    part_sums = jnp.einsum("rtc,cm->rtm", conv_low, x_proj, preferred_element_type=jnp.float32)
    dtbc = lax.psum(part_sums, "seq").astype(jnp.bfloat16)
    dt_low = dtbc[..., :DT_RANK]
    b_vals = dtbc[..., DT_RANK : DT_RANK + NSTATE].astype(jnp.float32)
    c_vals = dtbc[..., DT_RANK + NSTATE :].astype(jnp.float32)
    pre_dt = jnp.einsum(
        "rtk,kc->rtc", dt_low, dt_proj, preferred_element_type=jnp.float32
    ) + dt_bias.astype(jnp.float32)
    dt_vals = jax.nn.softplus(pre_dt)
    y_vals, pullback = jax.vjp(
        partial(scan_all, keep_mask=keep_mask),
        dt_vals,
        conv_low.astype(jnp.float32),
        b_vals,
        c_vals,
        decay_log.astype(jnp.float32),
        skip_scale.astype(jnp.float32),
    )
    y_tokens = lax.all_to_all(
        y_vals.astype(jnp.bfloat16), "seq", split_axis=1, concat_axis=2, tiled=True
    )
    y_token_vals = y_tokens.astype(jnp.float32)
    gate_act = jax.nn.silu(gate_z)
    gated = (y_token_vals * gate_act).astype(jnp.bfloat16)
    mixed = jnp.einsum("rte,de->rtd", gated, out_whole, preferred_element_type=jnp.float32)
    hidden_out = (residual + mixed).astype(jnp.bfloat16)
    grad_out_proj = jnp.einsum("rtd,rte->de", grad_out, gated, preferred_element_type=jnp.float32)
    grad_gated = jnp.einsum("rtd,de->rte", grad_out, out_whole, preferred_element_type=jnp.float32)
    grad_y = (grad_gated * gate_act).astype(jnp.bfloat16)
    grad_gate = (grad_gated * y_token_vals * slope_of_silu(gate_z)).astype(jnp.bfloat16)
    grad_y_chan = lax.all_to_all(grad_y, "seq", split_axis=2, concat_axis=1, tiled=True)
    grad_dt_scan, grad_x_scan, grad_b, grad_c, grad_decay, grad_skip = pullback(
        grad_y_chan.astype(jnp.float32)
    )
    grad_pre_dt = (grad_dt_scan * jax.nn.sigmoid(pre_dt)).astype(jnp.bfloat16)
    grad_dt_low = jnp.einsum(
        "rtc,kc->rtk", grad_pre_dt, dt_proj, preferred_element_type=jnp.float32
    )
    grad_dt_proj = jnp.einsum(
        "rtk,rtc->kc", dt_low, grad_pre_dt, preferred_element_type=jnp.float32
    )
    grad_dt_bias = jnp.sum(grad_pre_dt.astype(jnp.float32), axis=(0, 1))
    grad_parts = jnp.concatenate([grad_dt_low, grad_b, grad_c], axis=-1)
    grad_share = lax.psum_scatter(grad_parts, "seq", scatter_dimension=1, tiled=True)
    grad_dtbc = lax.all_gather(grad_share.astype(jnp.bfloat16), "seq", axis=1, tiled=True)
    grad_x_proj = jnp.einsum("rtc,rtm->cm", conv_low, grad_dtbc, preferred_element_type=jnp.float32)
    grad_conv_out = grad_x_scan + jnp.einsum(
        "rtm,cm->rtc", grad_dtbc, x_proj, preferred_element_type=jnp.float32
    )
    grad_pre_conv = grad_conv_out * slope_of_silu(pre_conv)
    grad_conv_bias = jnp.sum(grad_pre_conv, axis=(0, 1))
    conv_rows = [None] * CONV
    grad_x = jnp.zeros_like(grad_pre_conv)
    for offset in range(CONV):
        masked = grad_pre_conv * same_docs[offset]
        conv_rows[CONV - 1 - offset] = jnp.sum(masked * lagged(x_vals, offset, 0.0), axis=(0, 1))
        grad_x = grad_x + conv_full[CONV - 1 - offset] * leading(masked, offset)
    grad_conv_weight = jnp.stack(conv_rows)
    grad_x_tokens = lax.all_to_all(
        grad_x.astype(jnp.bfloat16), "seq", split_axis=1, concat_axis=2, tiled=True
    )
    grad_proj = jnp.concatenate([grad_x_tokens, grad_gate], axis=-1)
    grad_in_proj = jnp.einsum("rtf,rtd->fd", grad_proj, normed, preferred_element_type=jnp.float32)
    grad_normed = jnp.einsum("rtf,fd->rtd", grad_proj, in_whole, preferred_element_type=jnp.float32)
    grad_gain = jnp.sum(grad_normed * scaled, axis=(0, 1))
    grad_scaled = grad_normed * gain_full
    grad_hidden = grad_out.astype(jnp.float32) + inv_rms * (
        grad_scaled - scaled * jnp.mean(grad_scaled * scaled, axis=-1, keepdims=True)
    )
    gain_share, in_share, out_share = (
        lax.psum_scatter(grad_gain, ("seq", "row"), scatter_dimension=0, tiled=True),
        lax.psum_scatter(grad_in_proj, ("seq", "row"), scatter_dimension=0, tiled=True),
        lax.psum_scatter(grad_out_proj, ("seq", "row"), scatter_dimension=0, tiled=True),
    )
    centre = jnp.log(jax.nn.softplus(dt_bias.astype(jnp.float32)))
    offset_dt = jnp.log(dt_vals) - centre
    first_sum = jnp.sum(offset_dt, axis=(0, 1))
    second_sum = jnp.sum(offset_dt * offset_dt, axis=(0, 1))
    summed = lax.psum(
        (
            grad_conv_weight,
            grad_conv_bias,
            grad_x_proj,
            grad_dt_proj,
            grad_dt_bias,
            grad_decay,
            grad_skip,
            first_sum,
            second_sum,
        ),
        "row",
    )
    token_count = full_len * row_count * lax.axis_size("row")
    mean_off = summed[7] / token_count
    spread = jnp.sqrt(summed[8] / token_count - mean_off * mean_off + eps_spread)
    dt_stats = jnp.stack([centre + mean_off, spread])
    return (
        hidden_out,
        grad_hidden,
        gain_share,
        in_share,
        out_share,
        summed[0],
        summed[1],
        summed[2],
        summed[3],
        summed[4],
        summed[5],
        summed[6],
        dt_stats,
    )


def solution(mesh):
    fits = mesh.shape["seq"] == 16 and mesh.shape["row"] == 2
    plan = channel_plan if fits else token_plan
    return jax.shard_map(
        plan,
        mesh=mesh,
        in_specs=(
            P("row", "seq", None),
            P("row", "seq", None),
            P("row", None),
            P(("seq", "row")),
            P(("seq", "row"), None),
            P(("seq", "row"), None),
            P(None, "seq"),
            P("seq"),
            P("seq", None),
            P(None, "seq"),
            P("seq"),
            P(None, "seq"),
            P("seq"),
        ),
        out_specs=(
            P("row", "seq", None),
            P("row", "seq", None),
            P(("seq", "row")),
            P(("seq", "row"), None),
            P(("seq", "row"), None),
            P(None, "seq"),
            P("seq"),
            P("seq", None),
            P(None, "seq"),
            P("seq"),
            P(None, "seq"),
            P("seq"),
            P(None, "seq"),
        ),
        check_vma=False,
    )
```

```python
from functools import partial

import jax
import jax.numpy as jnp
from jax import lax
from jax.experimental import pallas as pl
from jax.experimental.pallas import tpu as pltpu
from jax.sharding import PartitionSpec as P

E = 2048
NSTATE = 16
CONV = 4
DT_RANK = 64
MAPS = DT_RANK + 2 * NSTATE

eps_norm = 1e-05
eps_spread = 1e-06
BF = jnp.bfloat16
F32 = jnp.float32
LOG2E = 1.4426950408889634
FAR = 1e4
LANES = 128
VMEM = 28 << 20


def params(dims=2):
    return pltpu.CompilerParams(
        dimension_semantics=("arbitrary",) * dims, vmem_limit_bytes=VMEM
    )


def place_in_doc(starts_ref, row, first, count):
    pos = lax.broadcasted_iota(jnp.int32, (count, LANES), 0) + first
    base = jnp.zeros_like(pos)
    for j in range(1, starts_ref.shape[1]):
        start = starts_ref[row, j]
        base = jnp.where(pos >= start, start, base)
    return pos - base


def large(shape, dtype):
    return pltpu.HBM(shape, dtype)


def still(*values):
    return [pltpu.with_memory_space_constraint(v, pltpu.HBM) for v in values]


def sigmoid(v):
    return 1.0 / (1.0 + jnp.exp2(v * -LOG2E))


def silu_slope(v):
    s = sigmoid(v)
    return s * (1.0 + v * (1.0 - s))


def softplus(v):
    return jnp.maximum(v, 0.0) + jnp.log1p(jnp.exp2(jnp.abs(v) * -LOG2E))


def dot(a, b, dims):
    return lax.dot_general(a, b, (dims, ((), ())), preferred_element_type=F32)


def own_place():
    s = lax.axis_index("seq")
    return jnp.stack([s // 4, s // 2 % 2, s % 2]).astype(jnp.int32)


def gate_kernel(*refs):
    pass


def gate(values, others):
    place = pl.BlockSpec(memory_space=pl.ANY)
    return pl.pallas_call(
        gate_kernel,
        in_specs=[place] * (len(values) + len(others)),
        out_specs=[place] * len(values),
        out_shape=[jax.ShapeDtypeStruct(v.shape, v.dtype) for v in values],
        input_output_aliases={i: i for i in range(len(values))},
        compiler_params=pltpu.CompilerParams(vmem_limit_bytes=1 << 16),
        cost_estimate=pl.CostEstimate(flops=1, bytes_accessed=1, transcendentals=0),
        name="gate",
    )(*values, *others)


def put_pieces(own, value, keep, send):
    rows, seg = keep.shape[2], keep.shape[3]
    first = own[2] == 0
    for r in range(rows):
        for x in range(2):
            at = (r * 4 + 2 * x) * seg
            even, odd = value[at : at + seg], value[at + seg : at + 2 * seg]
            keep[x ^ own[1], 0, r] = jnp.where(first, even, odd).astype(keep.dtype)
            send[x ^ own[1], 0, r] = jnp.where(first, odd, even).astype(send.dtype)


def take_pieces(own, near, far, out):
    rows, seg = near.shape[2], near.shape[3]
    first = own[2] == 0
    for r in range(rows):
        for x in range(2):
            at = (r * 4 + 2 * x) * seg
            a = near[x ^ own[1], 0, r].astype(F32)
            b = far[x ^ own[1], 0, r].astype(F32)
            out[at : at + seg, :] = jnp.where(first, a, b)
            out[at + seg : at + 2 * seg, :] = jnp.where(first, b, a)


def pieces_spec(rows, seg, n, at):
    return pl.BlockSpec((2, 1, rows, seg, n), lambda c, s, o: (0, at(c) ^ o[0], 0, 0, 0))


def fixed_block(shape):
    return pl.BlockSpec(shape, lambda c, s, o: (0,) * len(shape))


def front_kernel(
    starts, own, hid, gain, weight, conv_w, conv_b, xproj,
    normed_o, x_o, z_o, conv_o, keep_o, send_o,
    xs,
):
    c = pl.program_id(0)
    rows, t, ch = x_o.shape
    width = normed_o.shape[2]

    @pl.when(c == 0)
    def _():
        xs[:, 0:8, :] = jnp.zeros((rows, 8, ch), F32)

    @pl.when(c > 0)
    def _():
        xs[:, 0:8, :] = xs[:, t : t + 8, :]

    res = hid[...].reshape(rows * t, width).astype(F32)
    inv = lax.rsqrt(jnp.mean(res * res, axis=-1, keepdims=True) + eps_norm)
    normed = (res * inv * gain[...]).astype(BF)
    normed_o[...] = normed.reshape(rows, t, width)
    proj = dot(normed, weight[...], ((1,), (1,)))
    z_o[...] = proj[:, ch:].reshape(rows, t, ch)
    x_low = proj[:, :ch].astype(BF).reshape(rows, t, ch)
    x_o[...] = x_low
    xs[:, 8 : 8 + t, :] = x_low.astype(F32)
    for r in range(rows):
        place = place_in_doc(starts, r, c * t, t)
        pre = conv_b[...] + conv_w[CONV - 1 : CONV, :] * xs[r, 8 : 8 + t, :]
        for k in range(1, CONV):
            lag = conv_w[CONV - 1 - k : CONV - k, :] * xs[r, 8 - k : 8 - k + t, :]
            pre = pre + jnp.where(place >= k, lag, 0.0)
        conv_o[r] = (pre * sigmoid(pre)).astype(BF)
    conv = conv_o[...].reshape(rows * t, ch)
    put_pieces(own, dot(conv, xproj[...], ((1,), (0,))), keep_o, send_o)


def front(starts, own, hid, gain, weight, conv_w, conv_b, xproj):
    (hid,) = still(hid)
    rows, length, width = hid.shape
    ch = conv_w.shape[1]
    t = length // 4
    seg = t // 4
    tok = lambda n: pl.BlockSpec((rows, t, n), lambda c, s, o: (0, c, 0))
    piece = pieces_spec(rows, seg, MAPS, lambda c: c)
    return pl.pallas_call(
        front_kernel,
        grid_spec=pltpu.PrefetchScalarGridSpec(
            num_scalar_prefetch=2,
            grid=(length // t,),
            in_specs=[
                tok(width),
                fixed_block(gain.shape),
                fixed_block(weight.shape),
                fixed_block(conv_w.shape),
                fixed_block(conv_b.shape),
                fixed_block(xproj.shape),
            ],
            out_specs=[tok(width), tok(ch), tok(ch), tok(ch), piece, piece],
            scratch_shapes=[pltpu.VMEM((rows, t + 8, ch), F32)],
        ),
        out_shape=[
            large((rows, length, width), BF),
            large((rows, length, ch), BF),
            large((rows, length, ch), F32),
            large((rows, length, ch), BF),
            jax.ShapeDtypeStruct((2, 4, rows, seg, MAPS), F32),
            jax.ShapeDtypeStruct((2, 4, rows, seg, MAPS), F32),
        ],
        compiler_params=params(1),
        cost_estimate=pl.CostEstimate(flops=1, bytes_accessed=1, transcendentals=0),
        name="front",
    )(starts, own, hid, gain, weight, conv_w, conv_b, xproj)


def maps_across(low):
    pick = lax.broadcasted_iota(jnp.int32, (2 * NSTATE, MAPS), 0) + DT_RANK
    pick = (pick == lax.broadcasted_iota(jnp.int32, (2 * NSTATE, MAPS), 1)).astype(BF)
    return dot(pick, low, ((1,), (1,)))


def half_spec(rows, seg, n, at):
    return pl.BlockSpec(
        (1, 1, rows, seg, n),
        lambda c, s, o: (at(c) % 2 ^ o[1], at(c) // 2 ^ o[0], 0, 0, 0),
    )


def put_halves(own, value, keep, send):
    rows, seg = keep.shape[2], keep.shape[3]
    first = own[2] == 0
    for r in range(rows):
        even = value[2 * r * seg : (2 * r + 1) * seg]
        odd = value[(2 * r + 1) * seg : (2 * r + 2) * seg]
        keep[0, 0, r] = jnp.where(first, even, odd).astype(keep.dtype)
        send[0, 0, r] = jnp.where(first, odd, even).astype(send.dtype)


def take_halves(own, near, far, out):
    rows, seg = near.shape[2], near.shape[3]
    first = own[2] == 0
    for r in range(rows):
        a = near[0, 0, r].astype(F32)
        b = far[0, 0, r].astype(F32)
        out[2 * r * seg : (2 * r + 1) * seg, :] = jnp.where(first, a, b)
        out[(2 * r + 1) * seg : (2 * r + 2) * seg, :] = jnp.where(first, b, a)


def fold(parts):
    row = lax.broadcasted_iota(jnp.int32, parts[0].shape, 0)
    upper = row < 4
    parts = [
        jnp.where(upper, a, b) + pltpu.roll(jnp.where(upper, b, a), 4, 0)
        for a, b in zip(parts[:4], parts[4:])
    ]
    for step in (2, 1):
        half = len(parts) // 2
        upper = row & step == 0
        parts = [
            jnp.where(upper, a + pltpu.roll(a, 8 - step, 0), b + pltpu.roll(b, step, 0))
            for a, b in zip(parts[:half], parts[half:])
        ]
    return parts[0]


def spread_maps(low, first, out):
    count, ch = low.shape[0], out.shape[1]
    pick = lax.broadcasted_iota(jnp.int32, (MAPS, NSTATE * ch), 1) // ch + first
    pick = (pick == lax.broadcasted_iota(jnp.int32, (MAPS, NSTATE * ch), 0)).astype(BF)
    wide = dot(low, pick, ((1,), (0,)))
    for b in range(count // 8):
        for n in range(NSTATE):
            row = (b * NSTATE + n) * 8
            out[row : row + 8, :] = wide[b * 8 : b * 8 + 8, n * ch : (n + 1) * ch]


def forward_kernel(starts, own, near, far, dtproj, dtbias, decay, skip, conv, z, cols, *refs):
    (
        gated_o, y_o, states_o, mixed_o, last_o, stats_o,
        state, dtk_s, dtx_s, y_s, across_s, low_s, cm_s,
    ) = refs[-13:]
    c = pl.program_id(0)
    rows, t, ch = conv.shape

    @pl.when(c == 0)
    def _():
        state[...] = jnp.zeros_like(state)
        stats_o[...] = jnp.zeros_like(stats_o)

    rate = -LOG2E * jnp.exp(decay[...])
    take_halves(own, near, far, low_s)
    low = low_s[...].astype(BF)
    dt = softplus(dot(low[:, :DT_RANK], dtproj[...], ((1,), (0,))) + dtbias[...])
    off = jnp.log(dt) - jnp.log(softplus(dtbias[...]))
    stats_o[0:1, :] += jnp.sum(off, axis=0, keepdims=True)
    stats_o[1:2, :] += jnp.sum(off * off, axis=0, keepdims=True)
    x = conv[...].astype(F32).reshape(rows * t, ch)
    for r in range(rows):
        place = place_in_doc(starts, r, c * t, t)
        dtk_s[r * t : (r + 1) * t, :] = jnp.where(place >= 1, dt[r * t : (r + 1) * t], FAR)
    dtx_s[...] = dt * x
    across_s[...] = maps_across(low)
    spread_maps(low, DT_RANK + NSTATE, cm_s)

    def every_step(states):
        states, sums = list(states), [None] * rows
        maps = [across_s[:, r * t : (r + 1) * t] for r in range(rows)]
        for i in range(t):
            for r in range(rows):
                if i % 8 == 0:
                    sums[r] = []
                at = r * t + i
                s = states[r]
                a = jnp.exp2(dtk_s[pl.ds(at, 1), :] * rate)
                states_o[r, i] = s
                b = jnp.broadcast_to(maps[r][:NSTATE, i : i + 1], (NSTATE, ch))
                s = a * s + dtx_s[pl.ds(at, 1), :] * b
                ys = s * cm_s[pl.ds(at // 8 * 8 * NSTATE + at % 8, NSTATE, stride=8), :]
                sums[r].append(ys[:8] + ys[8:])
                if i % 8 == 7:
                    y_s[pl.ds(r * t + i - 7, 8), :] = fold(sums[r])
                states[r] = s
        return tuple(states)

    states = every_step(tuple(state[r] for r in range(rows)))
    for r in range(rows):
        state[r] = states[r]
        last_o[r] = states[r]
    y_low = (y_s[...] + skip[...] * x).astype(BF)
    y_o[...] = y_low.reshape(rows, t, ch)
    zz = z[...].reshape(rows * t, ch)
    gated = (y_low.astype(F32) * (zz * sigmoid(zz))).astype(BF)
    gated_o[...] = gated.reshape(rows, t, ch)
    mixed = dot(gated, cols[...], ((1,), (1,))).astype(BF)
    mixed_o[...] = mixed.reshape(rows, t, cols.shape[0])


def forward_scan(after, starts, own, near, far, dtproj, dtbias, decay, skip, conv, z, cols):
    conv, z = still(conv, z)
    rows, length, ch = conv.shape
    t = length // 8
    seg = t // 2
    tok = lambda n: pl.BlockSpec((rows, t, n), lambda c, s, o: (0, c, 0))
    half = half_spec(rows, seg, MAPS, lambda c: c)
    return pl.pallas_call(
        forward_kernel,
        grid_spec=pltpu.PrefetchScalarGridSpec(
            num_scalar_prefetch=2,
            grid=(length // t,),
            in_specs=[
                half,
                half,
                fixed_block(dtproj.shape),
                fixed_block(dtbias.shape),
                fixed_block(decay.shape),
                fixed_block(skip.shape),
                tok(ch),
                tok(ch),
                fixed_block(cols.shape),
                *[pl.BlockSpec(memory_space=pl.ANY)] * len(after),
            ],
            out_specs=[
                tok(ch),
                tok(ch),
                pl.BlockSpec((rows, t, NSTATE, ch), lambda c, s, o: (0, c, 0, 0)),
                tok(cols.shape[0]),
                fixed_block((rows, NSTATE, ch)),
                fixed_block((8, ch)),
            ],
            scratch_shapes=[
                pltpu.VMEM((rows, NSTATE, ch), F32),
                pltpu.VMEM((rows * t, ch), F32),
                pltpu.VMEM((rows * t, ch), F32),
                pltpu.VMEM((rows * t, ch), F32),
                pltpu.VMEM((2 * NSTATE, rows * t), F32),
                pltpu.VMEM((rows * t, MAPS), F32),
                pltpu.VMEM((rows * t * NSTATE, ch), F32),
            ],
        ),
        out_shape=[
            large((rows, length, ch), BF),
            large((rows, length, ch), BF),
            large((rows, length, NSTATE, ch), F32),
            large((rows, length, cols.shape[0]), BF),
            jax.ShapeDtypeStruct((rows, NSTATE, ch), F32),
            jax.ShapeDtypeStruct((8, ch), F32),
        ],
        compiler_params=params(1),
        cost_estimate=pl.CostEstimate(flops=1, bytes_accessed=1, transcendentals=0),
        name="forward_scan",
    )(starts, own, near, far, dtproj, dtbias, decay, skip, conv, z, cols, *after)


def backward_kernel(
    starts, own, near, far, dtproj, dtbias, decay, skip, conv, z, y, gout, cols, states, wide,
    gdtproj_i, misc_i, back_i, next_i, *refs, top,
):
    (
        ggate_o, gxs_o, keep_o, send_o, gdtproj_o, misc_o, back_o, next_o,
        dtk_s, dt_s, dtx_s, gy_s, p1_s, p2_s, gb_s, gc_s, fold_s, across_s, low_s,
    ) = refs[-19:]
    c = pl.program_id(0)
    rows, t, ch = conv.shape
    count = rows * t

    @pl.when(c == 0)
    def _():
        back_o[...] = back_i[...]
        next_o[...] = next_i[...]
        gdtproj_o[...] = gdtproj_i[...]
        misc_o[...] = misc_i[...]

    neg = -jnp.exp(decay[...])
    rate = LOG2E * neg
    take_halves(own, near, far, low_s)
    low = low_s[...].astype(BF)
    pre = dot(low[:, :DT_RANK], dtproj[...], ((1,), (0,))) + dtbias[...]
    dt = softplus(pre)
    x = conv[...].astype(F32).reshape(count, ch)
    for r in range(rows):
        place = place_in_doc(starts, r, (top - c) * t, t)
        dtk_s[r * t : (r + 1) * t, :] = jnp.where(place >= 1, dt[r * t : (r + 1) * t], FAR)
    dt_s[...] = dt
    dtx_s[...] = dt * x
    zz = z[...].reshape(count, ch)
    ggv = dot(gout[...].reshape(count, gout.shape[2]), cols[...], ((1,), (0,)))
    sg = sigmoid(zz)
    gy = (ggv * (zz * sg)).astype(BF).astype(F32)
    yv = y[...].astype(F32).reshape(count, ch)
    ggate = (ggv * yv * (sg * (1.0 + zz * (1.0 - sg)))).astype(BF)
    ggate_o[...] = ggate.reshape(rows, t, ch)
    gy_s[...] = gy
    across_s[...] = maps_across(low)

    def every_step(carry):
        hs, s_nexts, acc = list(carry[0]), list(carry[1]), carry[2]
        p1s, p2s = [None] * rows, [None] * rows
        maps = [across_s[:, r * t : (r + 1) * t] for r in range(rows)]
        for i in range(t - 1, -1, -1):
            for r in range(rows):
                at = r * t + i
                gyr = gy_s[pl.ds(at, 1), :]
                g = gyr * jnp.broadcast_to(maps[r][NSTATE:, i : i + 1], (NSTATE, ch)) + hs[r]
                h = jnp.exp2(dtk_s[pl.ds(at, 1), :] * rate) * g
                s_prev = states[r, i]
                q = h * s_prev
                acc = acc + q * dt_s[pl.ds(at, 1), :]
                aq = q * neg
                bg = g * jnp.broadcast_to(maps[r][:NSTATE, i : i + 1], (NSTATE, ch))
                if i % 8 == 7:
                    p1s[r], p2s[r] = [], []
                p1s[r].insert(0, bg[:8] + bg[8:])
                p2s[r].insert(0, aq[:8] + aq[8:])
                if i % 8 == 0:
                    whole8 = pl.ds(at, 8)
                    p1_s[whole8, :] = fold(p1s[r])
                    p2_s[whole8, :] = fold(p2s[r])
                tile = pl.ds(at * NSTATE, NSTATE)
                gb_s[tile, :] = (g * dtx_s[pl.ds(at, 1), :]).astype(BF)
                gc_s[tile, :] = (gyr * s_nexts[r]).astype(BF)
                hs[r], s_nexts[r] = h, s_prev
        return tuple(hs), tuple(s_nexts), acc

    hs, s_nexts, acc = every_step(
        (
            tuple(back_o[r] for r in range(rows)),
            tuple(next_o[r] for r in range(rows)),
            jnp.zeros((NSTATE, ch), F32),
        ),
    )
    for r in range(rows):
        back_o[r] = hs[r]
        next_o[r] = s_nexts[r]
    p1, p2 = p1_s[...], p2_s[...]
    gxs_o[...] = (dt * p1 + skip[...] * gy).reshape(rows, t, ch)
    gpre = ((p2 + x * p1) * sigmoid(pre)).astype(BF)
    gdtproj_o[...] += dot(low[:, :DT_RANK], gpre, ((0,), (0,)))
    misc_o[0:NSTATE, :] += neg * acc
    misc_o[NSTATE : NSTATE + 1, :] += jnp.sum(gpre.astype(F32), axis=0, keepdims=True)
    misc_o[NSTATE + 1 : NSTATE + 2, :] += jnp.sum(gy * x, axis=0, keepdims=True)
    ones = jnp.ones((ch, ch), BF)
    entry = lax.broadcasted_iota(jnp.int32, (1, NSTATE, ch), 1) + DT_RANK
    lane = lax.broadcasted_iota(jnp.int32, (1, NSTATE, ch), 2)
    maps = jnp.zeros((count, NSTATE, ch), F32)
    for ref in (gb_s, gc_s):
        every = dot(ref[...], ones, ((1,), (0,))).reshape(count, NSTATE, ch)
        maps = jnp.where(lane == entry, every, maps)
        entry = entry + NSTATE
    fold_s[...] = (maps[:, :8] + maps[:, 8:]).reshape(count * 8, ch)
    total = dot(gpre, wide[...], ((1,), (0,)))
    for j in range(8):
        total = total + fold_s[pl.ds(j, count, stride=8), :][:, :MAPS]
    put_halves(own, total, keep_o, send_o)


def widened(dtproj):
    return jnp.pad(dtproj.T, ((0, 0), (0, 2 * NSTATE)))


def backward_scan(
    top, chunks, after, so_far, starts, own, near, far, dtproj, dtbias, decay, skip, conv, z, y,
    gout, cols, states, wide,
):
    conv, z, y, gout, states = still(conv, z, y, gout, states)
    rows, length, ch = conv.shape
    t = length // 8
    seg = t // 2
    done, passed = so_far
    fixed = 19
    tok = lambda n: pl.BlockSpec((rows, t, n), lambda c, s, o: (0, top - c, 0))
    half = half_spec(rows, seg, MAPS, lambda c: top - c)
    small = [(DT_RANK, ch), (24, ch), (rows, NSTATE, ch), (rows, NSTATE, ch)]
    return pl.pallas_call(
        partial(backward_kernel, top=top),
        grid_spec=pltpu.PrefetchScalarGridSpec(
            num_scalar_prefetch=2,
            grid=(chunks,),
            in_specs=[
                half,
                half,
                fixed_block(dtproj.shape),
                fixed_block(dtbias.shape),
                fixed_block(decay.shape),
                fixed_block(skip.shape),
                tok(ch),
                tok(ch),
                tok(ch),
                tok(gout.shape[2]),
                fixed_block(cols.shape),
                pl.BlockSpec((rows, t, NSTATE, ch), lambda c, s, o: (0, top - c, 0, 0)),
                fixed_block(wide.shape),
                *[fixed_block(s) for s in small],
                *[pl.BlockSpec(memory_space=pl.ANY)] * (len(done) + len(after)),
            ],
            out_specs=[tok(ch), tok(ch), half, half, *[fixed_block(s) for s in small]],
            scratch_shapes=[
                pltpu.VMEM((rows * t, ch), F32),
                pltpu.VMEM((rows * t, ch), F32),
                pltpu.VMEM((rows * t, ch), F32),
                pltpu.VMEM((rows * t, ch), F32),
                pltpu.VMEM((rows * t, ch), F32),
                pltpu.VMEM((rows * t, ch), F32),
                pltpu.VMEM((rows * t * NSTATE, ch), BF),
                pltpu.VMEM((rows * t * NSTATE, ch), BF),
                pltpu.VMEM((rows * t * 8, ch), F32),
                pltpu.VMEM((2 * NSTATE, rows * t), F32),
                pltpu.VMEM((rows * t, MAPS), F32),
            ],
        ),
        out_shape=[
            large((rows, length, ch), BF),
            large((rows, length, ch), F32),
            jax.ShapeDtypeStruct((2, 4, rows, seg, MAPS), F32),
            jax.ShapeDtypeStruct((2, 4, rows, seg, MAPS), F32),
            *[jax.ShapeDtypeStruct(s, F32) for s in small],
        ],
        input_output_aliases={fixed + i: i for i in range(len(done))},
        compiler_params=params(1),
        cost_estimate=pl.CostEstimate(flops=1, bytes_accessed=1, transcendentals=0),
        name="backward_scan",
    )(
        starts, own, near, far, dtproj, dtbias, decay, skip, conv, z, y, gout, cols, states, wide,
        *passed, *done, *after,
    )


def tail_kernel(
    starts, own, near, far, conv, gxs, ggate, x, before, normed, weight, conv_w, conv_b, xproj, *refs
):
    keep_o, send_o, gin_o, gxproj_o, misc_o, xs, gm_s, low_s, gx_s = refs[-9:]
    c = pl.program_id(0)
    chunks = pl.num_programs(0)
    rows, t, ch = conv.shape
    count = rows * t

    @pl.when(c == 0)
    def _():
        gin_o[...] = jnp.zeros_like(gin_o)
        gxproj_o[...] = jnp.zeros_like(gxproj_o)
        misc_o[...] = jnp.zeros_like(misc_o)
        gm_s[:, :, t : t + 8, :] = jnp.zeros((CONV - 1, rows, 8, ch), F32)

    @pl.when(c > 0)
    def _():
        gm_s[:, :, t : t + 8, :] = gm_s[:, :, 0:8, :]

    xs[:, 0:16, :] = before[...].astype(F32)
    xs[:, 16 : 16 + t, :] = x[...].astype(F32)
    take_pieces(own, near, far, low_s)
    low = low_s[...].astype(BF)
    gconv = gxs[...].reshape(count, ch) + dot(low, xproj[...], ((1,), (1,)))
    gxproj_o[...] += dot(conv[...].reshape(count, ch), low, ((0,), (0,)))
    for r in range(rows):
        place = place_in_doc(starts, r, (chunks - 1 - c) * t, t)
        lags = [xs[r, 16 : 16 + t, :]]
        pre = conv_b[...] + conv_w[CONV - 1 : CONV, :] * lags[0]
        for k in range(1, CONV):
            lags.append(jnp.where(place >= k, xs[r, 16 - k : 16 - k + t, :], 0.0))
            pre = pre + conv_w[CONV - 1 - k : CONV - k, :] * lags[k]
        gpre = gconv[r * t : (r + 1) * t] * silu_slope(pre)
        gx = conv_w[CONV - 1 : CONV, :] * gpre
        for k in range(CONV):
            misc_o[CONV - 1 - k : CONV - k, :] += jnp.sum(gpre * lags[k], axis=0, keepdims=True)
            if k:
                gm_s[k - 1, r, 0:t, :] = jnp.where(place >= k, gpre, 0.0)
                gx = gx + conv_w[CONV - 1 - k : CONV - k, :] * gm_s[k - 1, r, k : k + t, :]
        misc_o[CONV : CONV + 1, :] += jnp.sum(gpre, axis=0, keepdims=True)
        gx_s[r * t : (r + 1) * t, :] = gx.astype(BF)
    gproj = jnp.concatenate([gx_s[...], ggate[...].reshape(count, ch)], axis=1)
    gin_o[...] += dot(gproj, normed[...].reshape(count, normed.shape[2]), ((0,), (0,)))
    put_pieces(own, dot(gproj, weight[...], ((1,), (0,))), keep_o, send_o)


def tail(after, starts, own, near, far, conv, gxs, ggate, x, normed, weight, conv_w, conv_b, xproj):
    conv, gxs, ggate, x, normed = still(conv, gxs, ggate, x, normed)
    rows, length, width = normed.shape
    ch = conv.shape[2]
    t = length // 4
    seg = t // 4
    last = length // t - 1
    tok = lambda n: pl.BlockSpec((rows, t, n), lambda c, s, o: (0, last - c, 0))
    piece = lambda n: pieces_spec(rows, seg, n, lambda c: last - c)
    before = pl.BlockSpec(
        (rows, 16, ch), lambda c, s, o: (0, jnp.maximum((last - c) * (t // 16) - 1, 0), 0)
    )
    return pl.pallas_call(
        tail_kernel,
        grid_spec=pltpu.PrefetchScalarGridSpec(
            num_scalar_prefetch=2,
            grid=(length // t,),
            in_specs=[
                piece(MAPS),
                piece(MAPS),
                tok(ch),
                tok(ch),
                tok(ch),
                tok(ch),
                before,
                tok(width),
                fixed_block(weight.shape),
                fixed_block(conv_w.shape),
                fixed_block(conv_b.shape),
                fixed_block(xproj.shape),
                *[pl.BlockSpec(memory_space=pl.ANY)] * len(after),
            ],
            out_specs=[
                piece(width),
                piece(width),
                fixed_block(weight.shape),
                fixed_block((ch, MAPS)),
                fixed_block((8, ch)),
            ],
            scratch_shapes=[
                pltpu.VMEM((rows, t + 16, ch), F32),
                pltpu.VMEM((CONV - 1, rows, t + 8, ch), F32),
                pltpu.VMEM((rows * t, MAPS), F32),
                pltpu.VMEM((rows * t, ch), BF),
            ],
        ),
        out_shape=[
            large((2, 4, rows, seg, width), BF),
            large((2, 4, rows, seg, width), BF),
            jax.ShapeDtypeStruct(weight.shape, F32),
            jax.ShapeDtypeStruct((ch, MAPS), F32),
            jax.ShapeDtypeStruct((8, ch), F32),
        ],
        compiler_params=params(1),
        cost_estimate=pl.CostEstimate(flops=1, bytes_accessed=1, transcendentals=0),
        name="tail",
    )(starts, own, near, far, conv, gxs, ggate, x, x, normed, weight, conv_w, conv_b, xproj, *after)


def cross(v, bits):
    return lax.ppermute(v, "seq", [(s, s ^ bits) for s in range(16)])


def swap_row(v):
    return lax.ppermute(v, "row", [(0, 1), (1, 0)])


def total_of_all(v):
    v = v + swap_row(v)
    for bits in (1, 2, 4, 8):
        v = v + cross(v, bits)
    return v


def sum_pieces(keep, send, sent, others):
    (acc,) = gate([keep.astype(F32) + cross(send, 1).astype(F32)], others)
    acc = acc[0] + cross(acc[1].astype(sent), 2).astype(F32)
    total = acc[0]
    for k in (1, 2, 3):
        total = total + cross(acc[k].astype(sent), 4 * k).astype(F32)
    return total


def spread_pieces(own_piece):
    line = jnp.stack([own_piece] + [cross(own_piece, 4 * k) for k in (1, 2, 3)])
    near = jnp.stack([line, cross(line, 2)])
    return near, cross(near, 1)


def gather_tokens(v):
    return lax.all_gather(v, "seq", axis=1, tiled=True)


def up(v):
    return v.astype(F32)


class Sum:
    def __init__(self, keep, send):
        self.keep, self.near = keep, cross(send, 1)
        self.head = keep.shape[2] - keep.shape[2] // 3

    def part(self, *at):
        return up(self.keep[at]) + up(self.near[at])

    def first(self, others):
        (self.near,) = gate([self.near], others)
        a, b = slice(0, self.head), slice(self.head, None)
        sent = [self.part(1, slice(None), a).astype(BF)]
        sent += [self.part(slice(None), k, b).astype(BF) for k in (1, 2, 3)]
        self.second_of = [cross(sent[0], 2), *cross_z(sent[1:])]
        return sent

    def second(self, others):
        across, *line = gate(self.second_of, others)
        a, b = slice(0, self.head), slice(self.head, None)
        sent = [(self.part(0, k, a) + up(across[k])).astype(BF) for k in (1, 2, 3)]
        sent.append((self.part(1, 0, b) + sum(up(v[1]) for v in line)).astype(BF))
        self.third_of = [*cross_z(sent[:3]), cross(sent[3], 2)]
        self.a = self.part(0, 0, a) + up(across[0])
        self.b = self.part(0, 0, b) + sum(up(v[0]) for v in line)
        return sent

    def third(self, others):
        *line, across = gate(self.third_of, others)
        return jnp.concatenate([self.a + sum(up(v) for v in line), self.b + up(across)])


def cross_z(pieces):
    return [cross(v, 4 * k) for k, v in zip((1, 2, 3), pieces)]


def channel_plan(
    hidden_in, grad_out, doc_starts, norm_gain, in_proj, out_proj, conv_weight, conv_bias,
    x_proj, dt_proj, dt_bias, decay_log, skip_scale,
):
    row_count, seg_len, width = hidden_in.shape
    shards = lax.axis_size("seq")
    full_len = seg_len * shards
    ch = conv_weight.shape[1]
    first = lax.axis_index("row") == 0
    both = ("seq", "row")
    place = 2 * lax.axis_index("seq") + lax.axis_index("row")
    own = own_place()
    gain_len = norm_gain.shape[0]

    hid = gather_tokens(hidden_in)
    to_shard = [(i, 2 * (i % shards) + i // shards) for i in range(2 * shards)]
    mine = lax.ppermute(in_proj, both, to_shard)
    other = swap_row(mine)
    weight = jnp.concatenate([jnp.where(first, mine, other), jnp.where(first, other, mine)])
    other = swap_row(out_proj)
    pair = jnp.concatenate([jnp.where(first, out_proj, other), jnp.where(first, other, out_proj)])
    out_cols = lax.all_to_all(pair, "seq", split_axis=1, concat_axis=0, tiled=True)
    spot = jnp.zeros((2 * shards, gain_len), F32)
    spot = lax.dynamic_update_slice(spot, norm_gain.astype(F32)[None], (place, 0))
    gain_whole = total_of_all(spot).reshape(1, width)
    vectors = [
        conv_weight.astype(F32),
        conv_bias.astype(F32)[None],
        dt_bias.astype(F32)[None],
        decay_log.astype(F32),
        skip_scale.astype(F32)[None],
        widened(dt_proj),
        x_proj,
    ]
    weight, gain_whole, out_cols, *vectors = gate([weight, gain_whole, out_cols, *vectors], [])
    conv_w, conv_b, dtb, decay, skip, wide, x_proj = vectors

    normed, x, z, conv, keep, send = front(
        doc_starts, own, hid, gain_whole, weight, conv_w, conv_b, x_proj
    )
    gout = gather_tokens(gate([grad_out], [keep])[0])
    low = sum_pieces(keep, send, F32, []).astype(BF)
    near, far = spread_pieces(low)
    gated, y, states, mixed, last, stats = forward_scan(
        [], doc_starts, own, near, far, dt_proj, dtb, decay, skip, conv, z, out_cols
    )
    mixed = lax.psum_scatter(mixed, "seq", scatter_dimension=1, tiled=True)
    passed = [jnp.zeros((DT_RANK, ch), F32), jnp.zeros((24, ch), F32), jnp.zeros_like(last), last]
    ggate, gxs, keep, send, gdtproj, misc, _, _ = backward_scan(
        7, 8, [], ([], passed), doc_starts, own, near, far, dt_proj, dtb, decay, skip, conv, z, y,
        gout, out_cols, states, wide,
    )
    keep, send, gated = gate([keep, send, gated], [])
    low = sum_pieces(keep, send, BF, []).astype(BF)
    gout_cols = jnp.einsum("rtd,rtc->dc", gout, gated, preferred_element_type=F32)
    parts = gout_cols.reshape(shards, 2, width // (2 * shards), ch)
    keep = jnp.where(first, parts[:, 0], parts[:, 1])
    send = jnp.where(first, parts[:, 1], parts[:, 0])
    out_half = (keep + swap_row(send)).astype(BF)
    near, far = spread_pieces(low)
    keep, send, gin, gxproj, cmisc = tail(
        [out_half], doc_starts, own, near, far, conv, gxs, ggate, x, normed, weight, conv_w, conv_b,
        x_proj,
    )
    gnormed = Sum(keep, send)
    gnormed.first([])
    held = [gin, gdtproj, misc, stats, cmisc, gxproj]
    gin, gdtproj, misc, stats, cmisc, gxproj = gate(held, [gnormed.second_of[1]])
    grad_gain = jnp.sum(weight.astype(F32) * gin, axis=0) / gain_whole[0]
    grad_gain = grad_gain.reshape(2 * shards, gain_len)
    grad_gain = grad_gain + swap_row(grad_gain)
    grad_gain = grad_gain + cross(grad_gain, 1)
    keep = jnp.where(first, gin[:ch], gin[ch:])
    send = jnp.where(first, gin[ch:], gin[:ch])
    in_half = (keep + swap_row(send.astype(BF)).astype(F32)).astype(BF)
    small = jnp.concatenate([gdtproj, misc, stats, cmisc, jnp.transpose(gxproj)])
    small = small + swap_row(small)
    gnormed.second([in_half, small, grad_gain])
    grad_gain, out_half = gate([grad_gain, out_half], [gnormed.third_of[0]])
    out_share = lax.all_to_all(out_half, "seq", split_axis=0, concat_axis=0, tiled=True)
    grad_gain = grad_gain + cross(grad_gain, 2)
    *gnormed.third_of, grad_gain, in_half = gate([*gnormed.third_of, grad_gain, in_half], [])
    gnormed = gnormed.third([])
    to_owner = [(b, a) for a, b in to_shard]
    in_share = lax.ppermute(in_half, both, to_owner).astype(F32)
    grad_gain = grad_gain + sum(cross_z([grad_gain] * 3))
    out_share = jnp.transpose(out_share.astype(F32), (1, 0, 2)).reshape(width // (2 * shards), E)

    residual = hidden_in.astype(F32)
    hidden_out = (residual + mixed.astype(F32)).astype(BF)
    inv_rms = lax.rsqrt(jnp.mean(residual * residual, axis=-1, keepdims=True) + eps_norm)
    scaled = residual * inv_rms
    grad_scaled = gnormed * gain_whole
    grad_hidden = grad_out.astype(F32) + inv_rms * (
        grad_scaled - scaled * jnp.mean(grad_scaled * scaled, axis=-1, keepdims=True)
    )
    grad_gain = lax.dynamic_slice(grad_gain, (place, 0), (1, gain_len))[0]
    gdtproj, misc, stats, cmisc, gxproj = jnp.split(
        small, [DT_RANK, DT_RANK + 24, DT_RANK + 32, DT_RANK + 40]
    )
    token_count = full_len * row_count * 2
    mean_off = stats[0] / token_count
    spread = jnp.sqrt(stats[1] / token_count - mean_off * mean_off + eps_spread)
    centre = jnp.log(jax.nn.softplus(dt_bias.astype(F32)))
    return (
        hidden_out,
        grad_hidden,
        grad_gain,
        in_share,
        out_share,
        cmisc[:CONV],
        cmisc[CONV],
        jnp.transpose(gxproj),
        gdtproj,
        misc[NSTATE],
        misc[:NSTATE],
        misc[NSTATE + 1],
        jnp.stack([centre + mean_off, spread]),
    )


block_len = 16


def lagged(values, offset, filler):
    if offset == 0:
        return values
    widths = [(0, 0)] * values.ndim
    widths[1] = (offset, 0)
    return jnp.pad(values, widths, constant_values=filler)[:, : values.shape[1]]


def leading(values, offset):
    if offset == 0:
        return values
    widths = [(0, 0)] * values.ndim
    widths[1] = (0, offset)
    return jnp.pad(values, widths)[:, offset:]


def slope_of_silu(values):
    logistic = jax.nn.sigmoid(values)
    return logistic * (1.0 + values * (1.0 - logistic))


def block_scan(decay_rates, dt_row, x_row, b_row, c_row, keep_row):
    length, channels = dt_row.shape
    blocks = length // block_len

    def regroup(values):
        grouped = values.reshape((blocks, block_len) + values.shape[1:])
        return jnp.moveaxis(grouped, 0, -1)

    dt_q, x_q, b_q, c_q, keep_q = (regroup(v) for v in (dt_row, x_row, b_row, c_row, keep_row))

    def decay_at(dt_now, keep_now):
        return jnp.exp(dt_now[None, :, :] * decay_rates[:, :, None]) * keep_now[None, None, :]

    def local_pass(running, inputs):
        state_now, product = running
        dt_now, x_now, b_now, keep_now = inputs
        decay_now = decay_at(dt_now, keep_now)
        state_now = decay_now * state_now + b_now[:, None, :] * (dt_now * x_now)[None, :, :]
        return ((state_now, decay_now * product), None)

    empty_state = jnp.zeros((NSTATE, channels, blocks), jnp.float32)
    (block_ends, block_decay), _ = lax.scan(
        local_pass, (empty_state, jnp.ones_like(empty_state)), (dt_q, x_q, b_q, keep_q)
    )

    def combine(earlier, later):
        return (earlier[0] * later[0], later[0] * earlier[1] + later[1])

    _, reached = lax.associative_scan(combine, (block_decay, block_ends), axis=2)
    starting = jnp.concatenate([jnp.zeros_like(reached[:, :, :1]), reached[:, :, :-1]], axis=2)

    def full_pass(state_now, inputs):
        dt_now, x_now, b_now, c_now, keep_now = inputs
        state_now = (
            decay_at(dt_now, keep_now) * state_now
            + b_now[:, None, :] * (dt_now * x_now)[None, :, :]
        )
        return (state_now, jnp.sum(c_now[:, None, :] * state_now, axis=0))

    _, outputs = lax.scan(full_pass, starting, (dt_q, x_q, b_q, c_q, keep_q))
    return jnp.moveaxis(outputs, 2, 0).reshape(length, channels)


def scan_all(dt_vals, x_vals, b_vals, c_vals, decay_full, skip_full, keep_mask):
    decay_rates = -jnp.exp(decay_full)
    per_row = jax.checkpoint(block_scan)

    def one_row(row_items):
        return per_row(decay_rates, *row_items)

    outputs = lax.map(one_row, (dt_vals, x_vals, b_vals, c_vals, keep_mask))
    return outputs + skip_full * x_vals


def token_plan(
    hidden_in,
    grad_out,
    doc_starts,
    norm_gain,
    in_proj,
    out_proj,
    conv_weight,
    conv_bias,
    x_proj,
    dt_proj,
    dt_bias,
    decay_log,
    skip_scale,
):
    row_count, seg_len, model_width = hidden_in.shape
    full_len = seg_len * lax.axis_size("seq")
    gain_whole, in_whole, out_whole = (
        lax.all_gather(norm_gain, ("seq", "row"), axis=0, tiled=True),
        lax.all_gather(in_proj, ("seq", "row"), axis=0, tiled=True),
        lax.all_gather(out_proj, ("seq", "row"), axis=0, tiled=True),
    )
    residual = hidden_in.astype(jnp.float32)
    inv_rms = lax.rsqrt(jnp.mean(residual * residual, axis=-1, keepdims=True) + eps_norm)
    scaled = residual * inv_rms
    gain_full = gain_whole.astype(jnp.float32)
    normed = (scaled * gain_full).astype(jnp.bfloat16)
    proj_in = jnp.einsum("rtd,fd->rtf", normed, in_whole, preferred_element_type=jnp.float32)
    x_tokens = proj_in[..., :E].astype(jnp.bfloat16)
    gate_z = proj_in[..., E:]
    x_chan = lax.all_to_all(x_tokens, "seq", split_axis=2, concat_axis=1, tiled=True)
    positions = lax.broadcasted_iota(jnp.int32, (1, full_len, 1), 1)
    doc_ids = jnp.sum((doc_starts[:, None, :] <= positions).astype(jnp.int32), axis=2) - 1
    same_docs = [
        (lagged(doc_ids, offset, -1) == doc_ids).astype(jnp.float32)[..., None]
        for offset in range(CONV)
    ]
    keep_mask = same_docs[1][..., 0]
    x_vals = x_chan.astype(jnp.float32)
    conv_full = conv_weight.astype(jnp.float32)
    pre_conv = conv_bias.astype(jnp.float32) + jnp.zeros_like(x_vals)
    for offset in range(CONV):
        pre_conv = (
            pre_conv
            + conv_full[CONV - 1 - offset] * lagged(x_vals, offset, 0.0) * same_docs[offset]
        )
    conv_low = jax.nn.silu(pre_conv).astype(jnp.bfloat16)
    part_sums = jnp.einsum("rtc,cm->rtm", conv_low, x_proj, preferred_element_type=jnp.float32)
    dtbc = lax.psum(part_sums, "seq").astype(jnp.bfloat16)
    dt_low = dtbc[..., :DT_RANK]
    b_vals = dtbc[..., DT_RANK : DT_RANK + NSTATE].astype(jnp.float32)
    c_vals = dtbc[..., DT_RANK + NSTATE :].astype(jnp.float32)
    pre_dt = jnp.einsum(
        "rtk,kc->rtc", dt_low, dt_proj, preferred_element_type=jnp.float32
    ) + dt_bias.astype(jnp.float32)
    dt_vals = jax.nn.softplus(pre_dt)
    y_vals, pullback = jax.vjp(
        partial(scan_all, keep_mask=keep_mask),
        dt_vals,
        conv_low.astype(jnp.float32),
        b_vals,
        c_vals,
        decay_log.astype(jnp.float32),
        skip_scale.astype(jnp.float32),
    )
    y_tokens = lax.all_to_all(
        y_vals.astype(jnp.bfloat16), "seq", split_axis=1, concat_axis=2, tiled=True
    )
    y_token_vals = y_tokens.astype(jnp.float32)
    gate_act = jax.nn.silu(gate_z)
    gated = (y_token_vals * gate_act).astype(jnp.bfloat16)
    mixed = jnp.einsum("rte,de->rtd", gated, out_whole, preferred_element_type=jnp.float32)
    hidden_out = (residual + mixed).astype(jnp.bfloat16)
    grad_out_proj = jnp.einsum("rtd,rte->de", grad_out, gated, preferred_element_type=jnp.float32)
    grad_gated = jnp.einsum("rtd,de->rte", grad_out, out_whole, preferred_element_type=jnp.float32)
    grad_y = (grad_gated * gate_act).astype(jnp.bfloat16)
    grad_gate = (grad_gated * y_token_vals * slope_of_silu(gate_z)).astype(jnp.bfloat16)
    grad_y_chan = lax.all_to_all(grad_y, "seq", split_axis=2, concat_axis=1, tiled=True)
    grad_dt_scan, grad_x_scan, grad_b, grad_c, grad_decay, grad_skip = pullback(
        grad_y_chan.astype(jnp.float32)
    )
    grad_pre_dt = (grad_dt_scan * jax.nn.sigmoid(pre_dt)).astype(jnp.bfloat16)
    grad_dt_low = jnp.einsum(
        "rtc,kc->rtk", grad_pre_dt, dt_proj, preferred_element_type=jnp.float32
    )
    grad_dt_proj = jnp.einsum(
        "rtk,rtc->kc", dt_low, grad_pre_dt, preferred_element_type=jnp.float32
    )
    grad_dt_bias = jnp.sum(grad_pre_dt.astype(jnp.float32), axis=(0, 1))
    grad_parts = jnp.concatenate([grad_dt_low, grad_b, grad_c], axis=-1)
    grad_share = lax.psum_scatter(grad_parts, "seq", scatter_dimension=1, tiled=True)
    grad_dtbc = lax.all_gather(grad_share.astype(jnp.bfloat16), "seq", axis=1, tiled=True)
    grad_x_proj = jnp.einsum("rtc,rtm->cm", conv_low, grad_dtbc, preferred_element_type=jnp.float32)
    grad_conv_out = grad_x_scan + jnp.einsum(
        "rtm,cm->rtc", grad_dtbc, x_proj, preferred_element_type=jnp.float32
    )
    grad_pre_conv = grad_conv_out * slope_of_silu(pre_conv)
    grad_conv_bias = jnp.sum(grad_pre_conv, axis=(0, 1))
    conv_rows = [None] * CONV
    grad_x = jnp.zeros_like(grad_pre_conv)
    for offset in range(CONV):
        masked = grad_pre_conv * same_docs[offset]
        conv_rows[CONV - 1 - offset] = jnp.sum(masked * lagged(x_vals, offset, 0.0), axis=(0, 1))
        grad_x = grad_x + conv_full[CONV - 1 - offset] * leading(masked, offset)
    grad_conv_weight = jnp.stack(conv_rows)
    grad_x_tokens = lax.all_to_all(
        grad_x.astype(jnp.bfloat16), "seq", split_axis=1, concat_axis=2, tiled=True
    )
    grad_proj = jnp.concatenate([grad_x_tokens, grad_gate], axis=-1)
    grad_in_proj = jnp.einsum("rtf,rtd->fd", grad_proj, normed, preferred_element_type=jnp.float32)
    grad_normed = jnp.einsum("rtf,fd->rtd", grad_proj, in_whole, preferred_element_type=jnp.float32)
    grad_gain = jnp.sum(grad_normed * scaled, axis=(0, 1))
    grad_scaled = grad_normed * gain_full
    grad_hidden = grad_out.astype(jnp.float32) + inv_rms * (
        grad_scaled - scaled * jnp.mean(grad_scaled * scaled, axis=-1, keepdims=True)
    )
    gain_share, in_share, out_share = (
        lax.psum_scatter(grad_gain, ("seq", "row"), scatter_dimension=0, tiled=True),
        lax.psum_scatter(grad_in_proj, ("seq", "row"), scatter_dimension=0, tiled=True),
        lax.psum_scatter(grad_out_proj, ("seq", "row"), scatter_dimension=0, tiled=True),
    )
    centre = jnp.log(jax.nn.softplus(dt_bias.astype(jnp.float32)))
    offset_dt = jnp.log(dt_vals) - centre
    first_sum = jnp.sum(offset_dt, axis=(0, 1))
    second_sum = jnp.sum(offset_dt * offset_dt, axis=(0, 1))
    summed = lax.psum(
        (
            grad_conv_weight,
            grad_conv_bias,
            grad_x_proj,
            grad_dt_proj,
            grad_dt_bias,
            grad_decay,
            grad_skip,
            first_sum,
            second_sum,
        ),
        "row",
    )
    token_count = full_len * row_count * lax.axis_size("row")
    mean_off = summed[7] / token_count
    spread = jnp.sqrt(summed[8] / token_count - mean_off * mean_off + eps_spread)
    dt_stats = jnp.stack([centre + mean_off, spread])
    return (
        hidden_out,
        grad_hidden,
        gain_share,
        in_share,
        out_share,
        summed[0],
        summed[1],
        summed[2],
        summed[3],
        summed[4],
        summed[5],
        summed[6],
        dt_stats,
    )


def solution(mesh):
    fits = mesh.shape["seq"] == 16 and mesh.shape["row"] == 2
    plan = channel_plan if fits else token_plan
    return jax.shard_map(
        plan,
        mesh=mesh,
        in_specs=(
            P("row", "seq", None),
            P("row", "seq", None),
            P("row", None),
            P(("seq", "row")),
            P(("seq", "row"), None),
            P(("seq", "row"), None),
            P(None, "seq"),
            P("seq"),
            P("seq", None),
            P(None, "seq"),
            P("seq"),
            P(None, "seq"),
            P("seq"),
        ),
        out_specs=(
            P("row", "seq", None),
            P("row", "seq", None),
            P(("seq", "row")),
            P(("seq", "row"), None),
            P(("seq", "row"), None),
            P(None, "seq"),
            P("seq"),
            P("seq", None),
            P(None, "seq"),
            P("seq"),
            P(None, "seq"),
            P("seq"),
            P(None, "seq"),
        ),
        check_vma=False,
    )
```

```python
from functools import partial

import jax
import jax.numpy as jnp
from jax import lax
from jax.experimental import pallas as pl
from jax.experimental.pallas import tpu as pltpu
from jax.sharding import PartitionSpec as P

E = 2048
NSTATE = 16
CONV = 4
DT_RANK = 64
MAPS = DT_RANK + 2 * NSTATE

eps_norm = 1e-05
eps_spread = 1e-06
BF = jnp.bfloat16
F32 = jnp.float32
LOG2E = 1.4426950408889634
FAR = 1e4
LANES = 128
VMEM = 28 << 20


def params(dims=2):
    return pltpu.CompilerParams(
        dimension_semantics=("arbitrary",) * dims, vmem_limit_bytes=VMEM
    )


def place_in_doc(starts_ref, row, first, count):
    pos = lax.broadcasted_iota(jnp.int32, (count, LANES), 0) + first
    base = jnp.zeros_like(pos)
    for j in range(1, starts_ref.shape[1]):
        start = starts_ref[row, j]
        base = jnp.where(pos >= start, start, base)
    return pos - base


def large(shape, dtype):
    return pltpu.HBM(shape, dtype)


def still(*values):
    return [pltpu.with_memory_space_constraint(v, pltpu.HBM) for v in values]


def sigmoid(v):
    return 1.0 / (1.0 + jnp.exp2(v * -LOG2E))


def silu_slope(v):
    s = sigmoid(v)
    return s * (1.0 + v * (1.0 - s))


def softplus(v):
    return jnp.maximum(v, 0.0) + jnp.log1p(jnp.exp2(jnp.abs(v) * -LOG2E))


def dot(a, b, dims):
    return lax.dot_general(a, b, (dims, ((), ())), preferred_element_type=F32)


def own_place():
    s = lax.axis_index("seq")
    return jnp.stack([s // 4, s // 2 % 2, s % 2]).astype(jnp.int32)


def gate_kernel(*refs):
    pass


def gate(values, others):
    place = pl.BlockSpec(memory_space=pl.ANY)
    return pl.pallas_call(
        gate_kernel,
        in_specs=[place] * (len(values) + len(others)),
        out_specs=[place] * len(values),
        out_shape=[jax.ShapeDtypeStruct(v.shape, v.dtype) for v in values],
        input_output_aliases={i: i for i in range(len(values))},
        compiler_params=pltpu.CompilerParams(vmem_limit_bytes=1 << 16),
        cost_estimate=pl.CostEstimate(flops=1, bytes_accessed=1, transcendentals=0),
        name="gate",
    )(*values, *others)


def put_pieces(own, value, keep, send):
    rows, seg = keep.shape[2], keep.shape[3]
    first = own[2] == 0
    for r in range(rows):
        for x in range(2):
            at = (r * 4 + 2 * x) * seg
            even, odd = value[at : at + seg], value[at + seg : at + 2 * seg]
            keep[x ^ own[1], 0, r] = jnp.where(first, even, odd).astype(keep.dtype)
            send[x ^ own[1], 0, r] = jnp.where(first, odd, even).astype(send.dtype)


def take_pieces(own, near, far, out):
    rows, seg = near.shape[2], near.shape[3]
    first = own[2] == 0
    for r in range(rows):
        for x in range(2):
            at = (r * 4 + 2 * x) * seg
            a = near[x ^ own[1], 0, r].astype(F32)
            b = far[x ^ own[1], 0, r].astype(F32)
            out[at : at + seg, :] = jnp.where(first, a, b)
            out[at + seg : at + 2 * seg, :] = jnp.where(first, b, a)


def pieces_spec(rows, seg, n, at):
    return pl.BlockSpec((2, 1, rows, seg, n), lambda c, s, o: (0, at(c) ^ o[0], 0, 0, 0))


def fixed_block(shape):
    return pl.BlockSpec(shape, lambda c, s, o: (0,) * len(shape))


def front_kernel(
    starts, own, hid, gain, weight, conv_w, conv_b, xproj,
    normed_o, x_o, z_o, conv_o, keep_o, send_o,
    xs,
):
    c = pl.program_id(0)
    rows, t, ch = x_o.shape
    width = normed_o.shape[2]

    @pl.when(c == 0)
    def _():
        xs[:, 0:8, :] = jnp.zeros((rows, 8, ch), F32)

    @pl.when(c > 0)
    def _():
        xs[:, 0:8, :] = xs[:, t : t + 8, :]

    res = hid[...].reshape(rows * t, width).astype(F32)
    inv = lax.rsqrt(jnp.mean(res * res, axis=-1, keepdims=True) + eps_norm)
    normed = (res * inv * gain[...]).astype(BF)
    normed_o[...] = normed.reshape(rows, t, width)
    proj = dot(normed, weight[...], ((1,), (1,)))
    z_o[...] = proj[:, ch:].reshape(rows, t, ch)
    x_low = proj[:, :ch].astype(BF).reshape(rows, t, ch)
    x_o[...] = x_low
    xs[:, 8 : 8 + t, :] = x_low.astype(F32)
    for r in range(rows):
        place = place_in_doc(starts, r, c * t, t)
        pre = conv_b[...] + conv_w[CONV - 1 : CONV, :] * xs[r, 8 : 8 + t, :]
        for k in range(1, CONV):
            lag = conv_w[CONV - 1 - k : CONV - k, :] * xs[r, 8 - k : 8 - k + t, :]
            pre = pre + jnp.where(place >= k, lag, 0.0)
        conv_o[r] = (pre * sigmoid(pre)).astype(BF)
    conv = conv_o[...].reshape(rows * t, ch)
    put_pieces(own, dot(conv, xproj[...], ((1,), (0,))), keep_o, send_o)


def front(starts, own, hid, gain, weight, conv_w, conv_b, xproj):
    (hid,) = still(hid)
    rows, length, width = hid.shape
    ch = conv_w.shape[1]
    t = length // 4
    seg = t // 4
    tok = lambda n: pl.BlockSpec((rows, t, n), lambda c, s, o: (0, c, 0))
    piece = pieces_spec(rows, seg, MAPS, lambda c: c)
    return pl.pallas_call(
        front_kernel,
        grid_spec=pltpu.PrefetchScalarGridSpec(
            num_scalar_prefetch=2,
            grid=(length // t,),
            in_specs=[
                tok(width),
                fixed_block(gain.shape),
                fixed_block(weight.shape),
                fixed_block(conv_w.shape),
                fixed_block(conv_b.shape),
                fixed_block(xproj.shape),
            ],
            out_specs=[tok(width), tok(ch), tok(ch), tok(ch), piece, piece],
            scratch_shapes=[pltpu.VMEM((rows, t + 8, ch), F32)],
        ),
        out_shape=[
            large((rows, length, width), BF),
            large((rows, length, ch), BF),
            large((rows, length, ch), F32),
            large((rows, length, ch), BF),
            jax.ShapeDtypeStruct((2, 4, rows, seg, MAPS), F32),
            jax.ShapeDtypeStruct((2, 4, rows, seg, MAPS), F32),
        ],
        compiler_params=params(1),
        cost_estimate=pl.CostEstimate(flops=1, bytes_accessed=1, transcendentals=0),
        name="front",
    )(starts, own, hid, gain, weight, conv_w, conv_b, xproj)


def maps_across(low):
    pick = lax.broadcasted_iota(jnp.int32, (2 * NSTATE, MAPS), 0) + DT_RANK
    pick = (pick == lax.broadcasted_iota(jnp.int32, (2 * NSTATE, MAPS), 1)).astype(BF)
    return dot(pick, low, ((1,), (1,)))


def half_spec(rows, seg, n, at):
    return pl.BlockSpec(
        (1, 1, rows, seg, n),
        lambda c, s, o: (at(c) % 2 ^ o[1], at(c) // 2 ^ o[0], 0, 0, 0),
    )


def put_halves(own, value, keep, send):
    rows, seg = keep.shape[2], keep.shape[3]
    first = own[2] == 0
    for r in range(rows):
        even = value[2 * r * seg : (2 * r + 1) * seg]
        odd = value[(2 * r + 1) * seg : (2 * r + 2) * seg]
        keep[0, 0, r] = jnp.where(first, even, odd).astype(keep.dtype)
        send[0, 0, r] = jnp.where(first, odd, even).astype(send.dtype)


def take_halves(own, near, far, out):
    rows, seg = near.shape[2], near.shape[3]
    first = own[2] == 0
    for r in range(rows):
        a = near[0, 0, r].astype(F32)
        b = far[0, 0, r].astype(F32)
        out[2 * r * seg : (2 * r + 1) * seg, :] = jnp.where(first, a, b)
        out[(2 * r + 1) * seg : (2 * r + 2) * seg, :] = jnp.where(first, b, a)


def fold(parts):
    row = lax.broadcasted_iota(jnp.int32, parts[0].shape, 0)
    upper = row < 4
    parts = [
        jnp.where(upper, a, b) + pltpu.roll(jnp.where(upper, b, a), 4, 0)
        for a, b in zip(parts[:4], parts[4:])
    ]
    for step in (2, 1):
        half = len(parts) // 2
        upper = row & step == 0
        parts = [
            jnp.where(upper, a + pltpu.roll(a, 8 - step, 0), b + pltpu.roll(b, step, 0))
            for a, b in zip(parts[:half], parts[half:])
        ]
    return parts[0]


def spread_maps(low, first, out):
    count, ch = low.shape[0], out.shape[1]
    pick = lax.broadcasted_iota(jnp.int32, (MAPS, NSTATE * ch), 1) // ch + first
    pick = (pick == lax.broadcasted_iota(jnp.int32, (MAPS, NSTATE * ch), 0)).astype(BF)
    wide = dot(low, pick, ((1,), (0,)))
    for b in range(count // 8):
        for n in range(NSTATE):
            row = (b * NSTATE + n) * 8
            out[row : row + 8, :] = wide[b * 8 : b * 8 + 8, n * ch : (n + 1) * ch]


def forward_kernel(starts, own, near, far, dtproj, dtbias, decay, skip, conv, z, cols, *refs):
    (
        gated_o, y_o, states_o, mixed_o, last_o, stats_o,
        state, dtk_s, dtx_s, y_s, across_s, low_s, cm_s,
    ) = refs[-13:]
    c = pl.program_id(0)
    rows, t, ch = conv.shape

    @pl.when(c == 0)
    def _():
        state[...] = jnp.zeros_like(state)
        stats_o[...] = jnp.zeros_like(stats_o)

    rate = -LOG2E * jnp.exp(decay[...])
    take_halves(own, near, far, low_s)
    low = low_s[...].astype(BF)
    dt = softplus(dot(low[:, :DT_RANK], dtproj[...], ((1,), (0,))) + dtbias[...])
    off = jnp.log(dt) - jnp.log(softplus(dtbias[...]))
    stats_o[0:1, :] += jnp.sum(off, axis=0, keepdims=True)
    stats_o[1:2, :] += jnp.sum(off * off, axis=0, keepdims=True)
    x = conv[...].astype(F32).reshape(rows * t, ch)
    for r in range(rows):
        place = place_in_doc(starts, r, c * t, t)
        dtk_s[r * t : (r + 1) * t, :] = jnp.where(place >= 1, dt[r * t : (r + 1) * t], FAR)
    dtx_s[...] = dt * x
    across_s[...] = maps_across(low)
    spread_maps(low, DT_RANK + NSTATE, cm_s)

    def every_step(states):
        states, sums = list(states), [None] * rows
        maps = [across_s[:, r * t : (r + 1) * t] for r in range(rows)]
        for i in range(t):
            for r in range(rows):
                if i % 8 == 0:
                    sums[r] = []
                at = r * t + i
                s = states[r]
                a = jnp.exp2(dtk_s[pl.ds(at, 1), :] * rate)
                states_o[r, i] = s
                b = jnp.broadcast_to(maps[r][:NSTATE, i : i + 1], (NSTATE, ch))
                s = a * s + dtx_s[pl.ds(at, 1), :] * b
                ys = s * cm_s[pl.ds(at // 8 * 8 * NSTATE + at % 8, NSTATE, stride=8), :]
                sums[r].append(ys[:8] + ys[8:])
                if i % 8 == 7:
                    y_s[pl.ds(r * t + i - 7, 8), :] = fold(sums[r])
                states[r] = s
        return tuple(states)

    states = every_step(tuple(state[r] for r in range(rows)))
    for r in range(rows):
        state[r] = states[r]
        last_o[r] = states[r]
    y_low = (y_s[...] + skip[...] * x).astype(BF)
    y_o[...] = y_low.reshape(rows, t, ch)
    zz = z[...].reshape(rows * t, ch)
    gated = (y_low.astype(F32) * (zz * sigmoid(zz))).astype(BF)
    gated_o[...] = gated.reshape(rows, t, ch)
    mixed = dot(gated, cols[...], ((1,), (1,))).astype(BF)
    mixed_o[...] = mixed.reshape(rows, t, cols.shape[0])


def forward_scan(after, starts, own, near, far, dtproj, dtbias, decay, skip, conv, z, cols):
    conv, z = still(conv, z)
    rows, length, ch = conv.shape
    t = length // 8
    seg = t // 2
    tok = lambda n: pl.BlockSpec((rows, t, n), lambda c, s, o: (0, c, 0))
    half = half_spec(rows, seg, MAPS, lambda c: c)
    return pl.pallas_call(
        forward_kernel,
        grid_spec=pltpu.PrefetchScalarGridSpec(
            num_scalar_prefetch=2,
            grid=(length // t,),
            in_specs=[
                half,
                half,
                fixed_block(dtproj.shape),
                fixed_block(dtbias.shape),
                fixed_block(decay.shape),
                fixed_block(skip.shape),
                tok(ch),
                tok(ch),
                fixed_block(cols.shape),
                *[pl.BlockSpec(memory_space=pl.ANY)] * len(after),
            ],
            out_specs=[
                tok(ch),
                tok(ch),
                pl.BlockSpec((rows, t, NSTATE, ch), lambda c, s, o: (0, c, 0, 0)),
                tok(cols.shape[0]),
                fixed_block((rows, NSTATE, ch)),
                fixed_block((8, ch)),
            ],
            scratch_shapes=[
                pltpu.VMEM((rows, NSTATE, ch), F32),
                pltpu.VMEM((rows * t, ch), F32),
                pltpu.VMEM((rows * t, ch), F32),
                pltpu.VMEM((rows * t, ch), F32),
                pltpu.VMEM((2 * NSTATE, rows * t), F32),
                pltpu.VMEM((rows * t, MAPS), F32),
                pltpu.VMEM((rows * t * NSTATE, ch), F32),
            ],
        ),
        out_shape=[
            large((rows, length, ch), BF),
            large((rows, length, ch), BF),
            large((rows, length, NSTATE, ch), F32),
            large((rows, length, cols.shape[0]), BF),
            jax.ShapeDtypeStruct((rows, NSTATE, ch), F32),
            jax.ShapeDtypeStruct((8, ch), F32),
        ],
        compiler_params=params(1),
        cost_estimate=pl.CostEstimate(flops=1, bytes_accessed=1, transcendentals=0),
        name="forward_scan",
    )(starts, own, near, far, dtproj, dtbias, decay, skip, conv, z, cols, *after)


def backward_kernel(
    starts, own, near, far, dtproj, dtbias, decay, skip, conv, z, y, gout, cols, states, wide,
    gdtproj_i, misc_i, back_i, next_i, *refs, top,
):
    (
        ggate_o, gxs_o, keep_o, send_o, gdtproj_o, misc_o, back_o, next_o,
        dtk_s, dt_s, dtx_s, gy_s, p1_s, p2_s, gb_s, gc_s, fold_s, across_s, low_s,
    ) = refs[-19:]
    c = pl.program_id(0)
    rows, t, ch = conv.shape
    count = rows * t

    @pl.when(c == 0)
    def _():
        back_o[...] = back_i[...]
        next_o[...] = next_i[...]
        gdtproj_o[...] = gdtproj_i[...]
        misc_o[...] = misc_i[...]

    neg = -jnp.exp(decay[...])
    rate = LOG2E * neg
    take_halves(own, near, far, low_s)
    low = low_s[...].astype(BF)
    pre = dot(low[:, :DT_RANK], dtproj[...], ((1,), (0,))) + dtbias[...]
    dt = softplus(pre)
    x = conv[...].astype(F32).reshape(count, ch)
    for r in range(rows):
        place = place_in_doc(starts, r, (top - c) * t, t)
        dtk_s[r * t : (r + 1) * t, :] = jnp.where(place >= 1, dt[r * t : (r + 1) * t], FAR)
    dt_s[...] = dt
    dtx_s[...] = dt * x
    zz = z[...].reshape(count, ch)
    ggv = dot(gout[...].reshape(count, gout.shape[2]), cols[...], ((1,), (0,)))
    sg = sigmoid(zz)
    gy = (ggv * (zz * sg)).astype(BF).astype(F32)
    yv = y[...].astype(F32).reshape(count, ch)
    ggate = (ggv * yv * (sg * (1.0 + zz * (1.0 - sg)))).astype(BF)
    ggate_o[...] = ggate.reshape(rows, t, ch)
    gy_s[...] = gy
    across_s[...] = maps_across(low)

    def every_step(carry):
        hs, s_nexts, acc = list(carry[0]), list(carry[1]), carry[2]
        p1s, p2s = [None] * rows, [None] * rows
        maps = [across_s[:, r * t : (r + 1) * t] for r in range(rows)]
        for i in range(t - 1, -1, -1):
            for r in range(rows):
                at = r * t + i
                gyr = gy_s[pl.ds(at, 1), :]
                g = gyr * jnp.broadcast_to(maps[r][NSTATE:, i : i + 1], (NSTATE, ch)) + hs[r]
                h = jnp.exp2(dtk_s[pl.ds(at, 1), :] * rate) * g
                s_prev = states[r, i]
                q = h * s_prev
                acc = acc + q * dt_s[pl.ds(at, 1), :]
                aq = q * neg
                bg = g * jnp.broadcast_to(maps[r][:NSTATE, i : i + 1], (NSTATE, ch))
                if i % 8 == 7:
                    p1s[r], p2s[r] = [], []
                p1s[r].insert(0, bg[:8] + bg[8:])
                p2s[r].insert(0, aq[:8] + aq[8:])
                if i % 8 == 0:
                    whole8 = pl.ds(at, 8)
                    p1_s[whole8, :] = fold(p1s[r])
                    p2_s[whole8, :] = fold(p2s[r])
                tile = pl.ds(at * NSTATE, NSTATE)
                gb_s[tile, :] = (g * dtx_s[pl.ds(at, 1), :]).astype(BF)
                gc_s[tile, :] = (gyr * s_nexts[r]).astype(BF)
                hs[r], s_nexts[r] = h, s_prev
        return tuple(hs), tuple(s_nexts), acc

    hs, s_nexts, acc = every_step(
        (
            tuple(back_o[r] for r in range(rows)),
            tuple(next_o[r] for r in range(rows)),
            jnp.zeros((NSTATE, ch), F32),
        ),
    )
    for r in range(rows):
        back_o[r] = hs[r]
        next_o[r] = s_nexts[r]
    p1, p2 = p1_s[...], p2_s[...]
    gxs_o[...] = (dt * p1 + skip[...] * gy).reshape(rows, t, ch)
    gpre = ((p2 + x * p1) * sigmoid(pre)).astype(BF)
    gdtproj_o[...] += dot(low[:, :DT_RANK], gpre, ((0,), (0,)))
    misc_o[0:NSTATE, :] += neg * acc
    misc_o[NSTATE : NSTATE + 1, :] += jnp.sum(gpre.astype(F32), axis=0, keepdims=True)
    misc_o[NSTATE + 1 : NSTATE + 2, :] += jnp.sum(gy * x, axis=0, keepdims=True)
    ones = jnp.ones((ch, ch), BF)
    entry = lax.broadcasted_iota(jnp.int32, (1, NSTATE, ch), 1) + DT_RANK
    lane = lax.broadcasted_iota(jnp.int32, (1, NSTATE, ch), 2)
    maps = jnp.zeros((count, NSTATE, ch), F32)
    for ref in (gb_s, gc_s):
        every = dot(ref[...], ones, ((1,), (0,))).reshape(count, NSTATE, ch)
        maps = jnp.where(lane == entry, every, maps)
        entry = entry + NSTATE
    fold_s[...] = (maps[:, :8] + maps[:, 8:]).reshape(count * 8, ch)
    total = dot(gpre, wide[...], ((1,), (0,)))
    for j in range(8):
        total = total + fold_s[pl.ds(j, count, stride=8), :][:, :MAPS]
    put_halves(own, total, keep_o, send_o)


def widened(dtproj):
    return jnp.pad(dtproj.T, ((0, 0), (0, 2 * NSTATE)))


def backward_scan(
    top, chunks, after, so_far, starts, own, near, far, dtproj, dtbias, decay, skip, conv, z, y,
    gout, cols, states, wide,
):
    conv, z, y, gout, states = still(conv, z, y, gout, states)
    rows, length, ch = conv.shape
    t = length // 8
    seg = t // 2
    done, passed = so_far
    fixed = 19
    tok = lambda n: pl.BlockSpec((rows, t, n), lambda c, s, o: (0, top - c, 0))
    half = half_spec(rows, seg, MAPS, lambda c: top - c)
    small = [(DT_RANK, ch), (24, ch), (rows, NSTATE, ch), (rows, NSTATE, ch)]
    return pl.pallas_call(
        partial(backward_kernel, top=top),
        grid_spec=pltpu.PrefetchScalarGridSpec(
            num_scalar_prefetch=2,
            grid=(chunks,),
            in_specs=[
                half,
                half,
                fixed_block(dtproj.shape),
                fixed_block(dtbias.shape),
                fixed_block(decay.shape),
                fixed_block(skip.shape),
                tok(ch),
                tok(ch),
                tok(ch),
                tok(gout.shape[2]),
                fixed_block(cols.shape),
                pl.BlockSpec((rows, t, NSTATE, ch), lambda c, s, o: (0, top - c, 0, 0)),
                fixed_block(wide.shape),
                *[fixed_block(s) for s in small],
                *[pl.BlockSpec(memory_space=pl.ANY)] * (len(done) + len(after)),
            ],
            out_specs=[tok(ch), tok(ch), half, half, *[fixed_block(s) for s in small]],
            scratch_shapes=[
                pltpu.VMEM((rows * t, ch), F32),
                pltpu.VMEM((rows * t, ch), F32),
                pltpu.VMEM((rows * t, ch), F32),
                pltpu.VMEM((rows * t, ch), F32),
                pltpu.VMEM((rows * t, ch), F32),
                pltpu.VMEM((rows * t, ch), F32),
                pltpu.VMEM((rows * t * NSTATE, ch), BF),
                pltpu.VMEM((rows * t * NSTATE, ch), BF),
                pltpu.VMEM((rows * t * 8, ch), F32),
                pltpu.VMEM((2 * NSTATE, rows * t), F32),
                pltpu.VMEM((rows * t, MAPS), F32),
            ],
        ),
        out_shape=[
            large((rows, length, ch), BF),
            large((rows, length, ch), F32),
            jax.ShapeDtypeStruct((2, 4, rows, seg, MAPS), F32),
            jax.ShapeDtypeStruct((2, 4, rows, seg, MAPS), F32),
            *[jax.ShapeDtypeStruct(s, F32) for s in small],
        ],
        input_output_aliases={fixed + i: i for i in range(len(done))},
        compiler_params=params(1),
        cost_estimate=pl.CostEstimate(flops=1, bytes_accessed=1, transcendentals=0),
        name="backward_scan",
    )(
        starts, own, near, far, dtproj, dtbias, decay, skip, conv, z, y, gout, cols, states, wide,
        *passed, *done, *after,
    )


def tail_kernel(
    starts, own, near, far, conv, gxs, ggate, x, before, normed, weight, conv_w, conv_b, xproj, *refs
):
    keep_o, send_o, gin_o, gxproj_o, misc_o, xs, gm_s, low_s, gx_s = refs[-9:]
    c = pl.program_id(0)
    chunks = pl.num_programs(0)
    rows, t, ch = conv.shape
    count = rows * t

    @pl.when(c == 0)
    def _():
        gin_o[...] = jnp.zeros_like(gin_o)
        gxproj_o[...] = jnp.zeros_like(gxproj_o)
        misc_o[...] = jnp.zeros_like(misc_o)
        gm_s[:, :, t : t + 8, :] = jnp.zeros((CONV - 1, rows, 8, ch), F32)

    @pl.when(c > 0)
    def _():
        gm_s[:, :, t : t + 8, :] = gm_s[:, :, 0:8, :]

    xs[:, 0:16, :] = before[...].astype(F32)
    xs[:, 16 : 16 + t, :] = x[...].astype(F32)
    take_pieces(own, near, far, low_s)
    low = low_s[...].astype(BF)
    gconv = gxs[...].reshape(count, ch) + dot(low, xproj[...], ((1,), (1,)))
    gxproj_o[...] += dot(conv[...].reshape(count, ch), low, ((0,), (0,)))
    for r in range(rows):
        place = place_in_doc(starts, r, (chunks - 1 - c) * t, t)
        lags = [xs[r, 16 : 16 + t, :]]
        pre = conv_b[...] + conv_w[CONV - 1 : CONV, :] * lags[0]
        for k in range(1, CONV):
            lags.append(jnp.where(place >= k, xs[r, 16 - k : 16 - k + t, :], 0.0))
            pre = pre + conv_w[CONV - 1 - k : CONV - k, :] * lags[k]
        gpre = gconv[r * t : (r + 1) * t] * silu_slope(pre)
        gx = conv_w[CONV - 1 : CONV, :] * gpre
        for k in range(CONV):
            misc_o[CONV - 1 - k : CONV - k, :] += jnp.sum(gpre * lags[k], axis=0, keepdims=True)
            if k:
                gm_s[k - 1, r, 0:t, :] = jnp.where(place >= k, gpre, 0.0)
                gx = gx + conv_w[CONV - 1 - k : CONV - k, :] * gm_s[k - 1, r, k : k + t, :]
        misc_o[CONV : CONV + 1, :] += jnp.sum(gpre, axis=0, keepdims=True)
        gx_s[r * t : (r + 1) * t, :] = gx.astype(BF)
    gproj = jnp.concatenate([gx_s[...], ggate[...].reshape(count, ch)], axis=1)
    gin_o[...] += dot(gproj, normed[...].reshape(count, normed.shape[2]), ((0,), (0,)))
    put_pieces(own, dot(gproj, weight[...], ((1,), (0,))), keep_o, send_o)


def tail(after, starts, own, near, far, conv, gxs, ggate, x, normed, weight, conv_w, conv_b, xproj):
    conv, gxs, ggate, x, normed = still(conv, gxs, ggate, x, normed)
    rows, length, width = normed.shape
    ch = conv.shape[2]
    t = length // 4
    seg = t // 4
    last = length // t - 1
    tok = lambda n: pl.BlockSpec((rows, t, n), lambda c, s, o: (0, last - c, 0))
    piece = lambda n: pieces_spec(rows, seg, n, lambda c: last - c)
    before = pl.BlockSpec(
        (rows, 16, ch), lambda c, s, o: (0, jnp.maximum((last - c) * (t // 16) - 1, 0), 0)
    )
    return pl.pallas_call(
        tail_kernel,
        grid_spec=pltpu.PrefetchScalarGridSpec(
            num_scalar_prefetch=2,
            grid=(length // t,),
            in_specs=[
                piece(MAPS),
                piece(MAPS),
                tok(ch),
                tok(ch),
                tok(ch),
                tok(ch),
                before,
                tok(width),
                fixed_block(weight.shape),
                fixed_block(conv_w.shape),
                fixed_block(conv_b.shape),
                fixed_block(xproj.shape),
                *[pl.BlockSpec(memory_space=pl.ANY)] * len(after),
            ],
            out_specs=[
                piece(width),
                piece(width),
                fixed_block(weight.shape),
                fixed_block((ch, MAPS)),
                fixed_block((8, ch)),
            ],
            scratch_shapes=[
                pltpu.VMEM((rows, t + 16, ch), F32),
                pltpu.VMEM((CONV - 1, rows, t + 8, ch), F32),
                pltpu.VMEM((rows * t, MAPS), F32),
                pltpu.VMEM((rows * t, ch), BF),
            ],
        ),
        out_shape=[
            large((2, 4, rows, seg, width), BF),
            large((2, 4, rows, seg, width), BF),
            jax.ShapeDtypeStruct(weight.shape, F32),
            jax.ShapeDtypeStruct((ch, MAPS), F32),
            jax.ShapeDtypeStruct((8, ch), F32),
        ],
        compiler_params=params(1),
        cost_estimate=pl.CostEstimate(flops=1, bytes_accessed=1, transcendentals=0),
        name="tail",
    )(starts, own, near, far, conv, gxs, ggate, x, x, normed, weight, conv_w, conv_b, xproj, *after)


def cross(v, bits):
    return lax.ppermute(v, "seq", [(s, s ^ bits) for s in range(16)])


def swap_row(v):
    return lax.ppermute(v, "row", [(0, 1), (1, 0)])


def total_of_all(v):
    v = v + swap_row(v)
    for bits in (1, 2, 4, 8):
        v = v + cross(v, bits)
    return v


def sum_pieces(keep, send, sent, held):
    near = cross(send, 1)
    acc = keep.astype(F32) + near.astype(F32)
    far = cross(acc[1].astype(sent), 2)
    if held is not None:
        (held,) = gate([held], [near])
    acc = acc[0] + far.astype(F32)
    total = acc[0]
    for k in (1, 2, 3):
        total = total + cross(acc[k].astype(sent), 4 * k).astype(F32)
    return total, held


def spread_pieces(own_piece):
    line = jnp.stack([own_piece] + [cross(own_piece, 4 * k) for k in (1, 2, 3)])
    near = jnp.stack([line, cross(line, 2)])
    return near, cross(near, 1)


def gather_tokens(v):
    return lax.all_gather(v, "seq", axis=1, tiled=True)


def up(v):
    return v.astype(F32)


class Sum:
    def __init__(self, keep, send):
        self.keep, self.near = keep, cross(send, 1)
        self.head = keep.shape[2] - keep.shape[2] // 3

    def part(self, *at):
        return up(self.keep[at]) + up(self.near[at])

    def first(self, others):
        (self.near,) = gate([self.near], others)
        a, b = slice(0, self.head), slice(self.head, None)
        sent = [self.part(1, slice(None), a).astype(BF)]
        sent += [self.part(slice(None), k, b).astype(BF) for k in (1, 2, 3)]
        self.second_of = [cross(sent[0], 2), *cross_z(sent[1:])]
        return sent

    def second(self, others):
        across, *line = gate(self.second_of, others)
        a, b = slice(0, self.head), slice(self.head, None)
        sent = [(self.part(0, k, a) + up(across[k])).astype(BF) for k in (1, 2, 3)]
        sent.append((self.part(1, 0, b) + sum(up(v[1]) for v in line)).astype(BF))
        self.third_of = [*cross_z(sent[:3]), cross(sent[3], 2)]
        self.a = self.part(0, 0, a) + up(across[0])
        self.b = self.part(0, 0, b) + sum(up(v[0]) for v in line)
        return sent

    def third(self, others):
        *line, across = gate(self.third_of, others)
        return jnp.concatenate([self.a + sum(up(v) for v in line), self.b + up(across)])


def cross_z(pieces):
    return [cross(v, 4 * k) for k, v in zip((1, 2, 3), pieces)]


def channel_plan(
    hidden_in, grad_out, doc_starts, norm_gain, in_proj, out_proj, conv_weight, conv_bias,
    x_proj, dt_proj, dt_bias, decay_log, skip_scale,
):
    row_count, seg_len, width = hidden_in.shape
    shards = lax.axis_size("seq")
    full_len = seg_len * shards
    ch = conv_weight.shape[1]
    first = lax.axis_index("row") == 0
    both = ("seq", "row")
    place = 2 * lax.axis_index("seq") + lax.axis_index("row")
    own = own_place()
    gain_len = norm_gain.shape[0]

    hid = gather_tokens(hidden_in)
    to_shard = [(i, 2 * (i % shards) + i // shards) for i in range(2 * shards)]
    mine = lax.ppermute(in_proj, both, to_shard)
    other = swap_row(mine)
    weight = jnp.concatenate([jnp.where(first, mine, other), jnp.where(first, other, mine)])
    other = swap_row(out_proj)
    pair = jnp.concatenate([jnp.where(first, out_proj, other), jnp.where(first, other, out_proj)])
    out_cols = lax.all_to_all(pair, "seq", split_axis=1, concat_axis=0, tiled=True)
    spot = jnp.zeros((2 * shards, gain_len), F32)
    spot = lax.dynamic_update_slice(spot, norm_gain.astype(F32)[None], (place, 0))
    gain_whole = total_of_all(spot).reshape(1, width)
    vectors = [
        conv_weight.astype(F32),
        conv_bias.astype(F32)[None],
        dt_bias.astype(F32)[None],
        decay_log.astype(F32),
        skip_scale.astype(F32)[None],
        widened(dt_proj),
        x_proj,
    ]
    weight, gain_whole, out_cols, *vectors = gate([weight, gain_whole, out_cols, *vectors], [])
    conv_w, conv_b, dtb, decay, skip, wide, x_proj = vectors

    normed, x, z, conv, keep, send = front(
        doc_starts, own, hid, gain_whole, weight, conv_w, conv_b, x_proj
    )
    low, gout = sum_pieces(keep, send, F32, grad_out)
    low, gout = low.astype(BF), gather_tokens(gout)
    near, far = spread_pieces(low)
    gated, y, states, mixed, last, stats = forward_scan(
        [], doc_starts, own, near, far, dt_proj, dtb, decay, skip, conv, z, out_cols
    )
    mixed = lax.psum_scatter(mixed, "seq", scatter_dimension=1, tiled=True)
    passed = [jnp.zeros((DT_RANK, ch), F32), jnp.zeros((24, ch), F32), jnp.zeros_like(last), last]
    ggate, gxs, keep, send, gdtproj, misc, _, _ = backward_scan(
        7, 8, [], ([], passed), doc_starts, own, near, far, dt_proj, dtb, decay, skip, conv, z, y,
        gout, out_cols, states, wide,
    )
    keep, send, gated = gate([keep, send, gated], [])
    low = sum_pieces(keep, send, BF, None)[0].astype(BF)
    gout_cols = jnp.einsum("rtd,rtc->dc", gout, gated, preferred_element_type=F32)
    parts = gout_cols.reshape(shards, 2, width // (2 * shards), ch)
    keep = jnp.where(first, parts[:, 0], parts[:, 1])
    send = jnp.where(first, parts[:, 1], parts[:, 0])
    out_half = (keep + swap_row(send)).astype(BF)
    near, far = spread_pieces(low)
    keep, send, gin, gxproj, cmisc = tail(
        [out_half], doc_starts, own, near, far, conv, gxs, ggate, x, normed, weight, conv_w, conv_b,
        x_proj,
    )
    gnormed = Sum(keep, send)
    gnormed.first([])
    held = [gin, gdtproj, misc, stats, cmisc, gxproj]
    gin, gdtproj, misc, stats, cmisc, gxproj = gate(held, [gnormed.second_of[1]])
    grad_gain = jnp.sum(weight.astype(F32) * gin, axis=0) / gain_whole[0]
    grad_gain = grad_gain.reshape(2 * shards, gain_len)
    grad_gain = grad_gain + swap_row(grad_gain)
    grad_gain = grad_gain + cross(grad_gain, 1)
    keep = jnp.where(first, gin[:ch], gin[ch:])
    send = jnp.where(first, gin[ch:], gin[:ch])
    in_half = (keep + swap_row(send.astype(BF)).astype(F32)).astype(BF)
    small = jnp.concatenate([gdtproj, misc, stats, cmisc, jnp.transpose(gxproj)])
    small = small + swap_row(small)
    gnormed.second([in_half, small, grad_gain])
    grad_gain, out_half = gate([grad_gain, out_half], [gnormed.third_of[0]])
    out_share = lax.all_to_all(out_half, "seq", split_axis=0, concat_axis=0, tiled=True)
    grad_gain = grad_gain + cross(grad_gain, 2)
    *gnormed.third_of, grad_gain, in_half = gate([*gnormed.third_of, grad_gain, in_half], [])
    gnormed = gnormed.third([])
    to_owner = [(b, a) for a, b in to_shard]
    in_share = lax.ppermute(in_half, both, to_owner).astype(F32)
    grad_gain = grad_gain + sum(cross_z([grad_gain] * 3))
    out_share = jnp.transpose(out_share.astype(F32), (1, 0, 2)).reshape(width // (2 * shards), E)

    residual = hidden_in.astype(F32)
    hidden_out = (residual + mixed.astype(F32)).astype(BF)
    inv_rms = lax.rsqrt(jnp.mean(residual * residual, axis=-1, keepdims=True) + eps_norm)
    scaled = residual * inv_rms
    grad_scaled = gnormed * gain_whole
    grad_hidden = grad_out.astype(F32) + inv_rms * (
        grad_scaled - scaled * jnp.mean(grad_scaled * scaled, axis=-1, keepdims=True)
    )
    grad_gain = lax.dynamic_slice(grad_gain, (place, 0), (1, gain_len))[0]
    gdtproj, misc, stats, cmisc, gxproj = jnp.split(
        small, [DT_RANK, DT_RANK + 24, DT_RANK + 32, DT_RANK + 40]
    )
    token_count = full_len * row_count * 2
    mean_off = stats[0] / token_count
    spread = jnp.sqrt(stats[1] / token_count - mean_off * mean_off + eps_spread)
    centre = jnp.log(jax.nn.softplus(dt_bias.astype(F32)))
    return (
        hidden_out,
        grad_hidden,
        grad_gain,
        in_share,
        out_share,
        cmisc[:CONV],
        cmisc[CONV],
        jnp.transpose(gxproj),
        gdtproj,
        misc[NSTATE],
        misc[:NSTATE],
        misc[NSTATE + 1],
        jnp.stack([centre + mean_off, spread]),
    )


block_len = 16


def lagged(values, offset, filler):
    if offset == 0:
        return values
    widths = [(0, 0)] * values.ndim
    widths[1] = (offset, 0)
    return jnp.pad(values, widths, constant_values=filler)[:, : values.shape[1]]


def leading(values, offset):
    if offset == 0:
        return values
    widths = [(0, 0)] * values.ndim
    widths[1] = (0, offset)
    return jnp.pad(values, widths)[:, offset:]


def slope_of_silu(values):
    logistic = jax.nn.sigmoid(values)
    return logistic * (1.0 + values * (1.0 - logistic))


def block_scan(decay_rates, dt_row, x_row, b_row, c_row, keep_row):
    length, channels = dt_row.shape
    blocks = length // block_len

    def regroup(values):
        grouped = values.reshape((blocks, block_len) + values.shape[1:])
        return jnp.moveaxis(grouped, 0, -1)

    dt_q, x_q, b_q, c_q, keep_q = (regroup(v) for v in (dt_row, x_row, b_row, c_row, keep_row))

    def decay_at(dt_now, keep_now):
        return jnp.exp(dt_now[None, :, :] * decay_rates[:, :, None]) * keep_now[None, None, :]

    def local_pass(running, inputs):
        state_now, product = running
        dt_now, x_now, b_now, keep_now = inputs
        decay_now = decay_at(dt_now, keep_now)
        state_now = decay_now * state_now + b_now[:, None, :] * (dt_now * x_now)[None, :, :]
        return ((state_now, decay_now * product), None)

    empty_state = jnp.zeros((NSTATE, channels, blocks), jnp.float32)
    (block_ends, block_decay), _ = lax.scan(
        local_pass, (empty_state, jnp.ones_like(empty_state)), (dt_q, x_q, b_q, keep_q)
    )

    def combine(earlier, later):
        return (earlier[0] * later[0], later[0] * earlier[1] + later[1])

    _, reached = lax.associative_scan(combine, (block_decay, block_ends), axis=2)
    starting = jnp.concatenate([jnp.zeros_like(reached[:, :, :1]), reached[:, :, :-1]], axis=2)

    def full_pass(state_now, inputs):
        dt_now, x_now, b_now, c_now, keep_now = inputs
        state_now = (
            decay_at(dt_now, keep_now) * state_now
            + b_now[:, None, :] * (dt_now * x_now)[None, :, :]
        )
        return (state_now, jnp.sum(c_now[:, None, :] * state_now, axis=0))

    _, outputs = lax.scan(full_pass, starting, (dt_q, x_q, b_q, c_q, keep_q))
    return jnp.moveaxis(outputs, 2, 0).reshape(length, channels)


def scan_all(dt_vals, x_vals, b_vals, c_vals, decay_full, skip_full, keep_mask):
    decay_rates = -jnp.exp(decay_full)
    per_row = jax.checkpoint(block_scan)

    def one_row(row_items):
        return per_row(decay_rates, *row_items)

    outputs = lax.map(one_row, (dt_vals, x_vals, b_vals, c_vals, keep_mask))
    return outputs + skip_full * x_vals


def token_plan(
    hidden_in,
    grad_out,
    doc_starts,
    norm_gain,
    in_proj,
    out_proj,
    conv_weight,
    conv_bias,
    x_proj,
    dt_proj,
    dt_bias,
    decay_log,
    skip_scale,
):
    row_count, seg_len, model_width = hidden_in.shape
    full_len = seg_len * lax.axis_size("seq")
    gain_whole, in_whole, out_whole = (
        lax.all_gather(norm_gain, ("seq", "row"), axis=0, tiled=True),
        lax.all_gather(in_proj, ("seq", "row"), axis=0, tiled=True),
        lax.all_gather(out_proj, ("seq", "row"), axis=0, tiled=True),
    )
    residual = hidden_in.astype(jnp.float32)
    inv_rms = lax.rsqrt(jnp.mean(residual * residual, axis=-1, keepdims=True) + eps_norm)
    scaled = residual * inv_rms
    gain_full = gain_whole.astype(jnp.float32)
    normed = (scaled * gain_full).astype(jnp.bfloat16)
    proj_in = jnp.einsum("rtd,fd->rtf", normed, in_whole, preferred_element_type=jnp.float32)
    x_tokens = proj_in[..., :E].astype(jnp.bfloat16)
    gate_z = proj_in[..., E:]
    x_chan = lax.all_to_all(x_tokens, "seq", split_axis=2, concat_axis=1, tiled=True)
    positions = lax.broadcasted_iota(jnp.int32, (1, full_len, 1), 1)
    doc_ids = jnp.sum((doc_starts[:, None, :] <= positions).astype(jnp.int32), axis=2) - 1
    same_docs = [
        (lagged(doc_ids, offset, -1) == doc_ids).astype(jnp.float32)[..., None]
        for offset in range(CONV)
    ]
    keep_mask = same_docs[1][..., 0]
    x_vals = x_chan.astype(jnp.float32)
    conv_full = conv_weight.astype(jnp.float32)
    pre_conv = conv_bias.astype(jnp.float32) + jnp.zeros_like(x_vals)
    for offset in range(CONV):
        pre_conv = (
            pre_conv
            + conv_full[CONV - 1 - offset] * lagged(x_vals, offset, 0.0) * same_docs[offset]
        )
    conv_low = jax.nn.silu(pre_conv).astype(jnp.bfloat16)
    part_sums = jnp.einsum("rtc,cm->rtm", conv_low, x_proj, preferred_element_type=jnp.float32)
    dtbc = lax.psum(part_sums, "seq").astype(jnp.bfloat16)
    dt_low = dtbc[..., :DT_RANK]
    b_vals = dtbc[..., DT_RANK : DT_RANK + NSTATE].astype(jnp.float32)
    c_vals = dtbc[..., DT_RANK + NSTATE :].astype(jnp.float32)
    pre_dt = jnp.einsum(
        "rtk,kc->rtc", dt_low, dt_proj, preferred_element_type=jnp.float32
    ) + dt_bias.astype(jnp.float32)
    dt_vals = jax.nn.softplus(pre_dt)
    y_vals, pullback = jax.vjp(
        partial(scan_all, keep_mask=keep_mask),
        dt_vals,
        conv_low.astype(jnp.float32),
        b_vals,
        c_vals,
        decay_log.astype(jnp.float32),
        skip_scale.astype(jnp.float32),
    )
    y_tokens = lax.all_to_all(
        y_vals.astype(jnp.bfloat16), "seq", split_axis=1, concat_axis=2, tiled=True
    )
    y_token_vals = y_tokens.astype(jnp.float32)
    gate_act = jax.nn.silu(gate_z)
    gated = (y_token_vals * gate_act).astype(jnp.bfloat16)
    mixed = jnp.einsum("rte,de->rtd", gated, out_whole, preferred_element_type=jnp.float32)
    hidden_out = (residual + mixed).astype(jnp.bfloat16)
    grad_out_proj = jnp.einsum("rtd,rte->de", grad_out, gated, preferred_element_type=jnp.float32)
    grad_gated = jnp.einsum("rtd,de->rte", grad_out, out_whole, preferred_element_type=jnp.float32)
    grad_y = (grad_gated * gate_act).astype(jnp.bfloat16)
    grad_gate = (grad_gated * y_token_vals * slope_of_silu(gate_z)).astype(jnp.bfloat16)
    grad_y_chan = lax.all_to_all(grad_y, "seq", split_axis=2, concat_axis=1, tiled=True)
    grad_dt_scan, grad_x_scan, grad_b, grad_c, grad_decay, grad_skip = pullback(
        grad_y_chan.astype(jnp.float32)
    )
    grad_pre_dt = (grad_dt_scan * jax.nn.sigmoid(pre_dt)).astype(jnp.bfloat16)
    grad_dt_low = jnp.einsum(
        "rtc,kc->rtk", grad_pre_dt, dt_proj, preferred_element_type=jnp.float32
    )
    grad_dt_proj = jnp.einsum(
        "rtk,rtc->kc", dt_low, grad_pre_dt, preferred_element_type=jnp.float32
    )
    grad_dt_bias = jnp.sum(grad_pre_dt.astype(jnp.float32), axis=(0, 1))
    grad_parts = jnp.concatenate([grad_dt_low, grad_b, grad_c], axis=-1)
    grad_share = lax.psum_scatter(grad_parts, "seq", scatter_dimension=1, tiled=True)
    grad_dtbc = lax.all_gather(grad_share.astype(jnp.bfloat16), "seq", axis=1, tiled=True)
    grad_x_proj = jnp.einsum("rtc,rtm->cm", conv_low, grad_dtbc, preferred_element_type=jnp.float32)
    grad_conv_out = grad_x_scan + jnp.einsum(
        "rtm,cm->rtc", grad_dtbc, x_proj, preferred_element_type=jnp.float32
    )
    grad_pre_conv = grad_conv_out * slope_of_silu(pre_conv)
    grad_conv_bias = jnp.sum(grad_pre_conv, axis=(0, 1))
    conv_rows = [None] * CONV
    grad_x = jnp.zeros_like(grad_pre_conv)
    for offset in range(CONV):
        masked = grad_pre_conv * same_docs[offset]
        conv_rows[CONV - 1 - offset] = jnp.sum(masked * lagged(x_vals, offset, 0.0), axis=(0, 1))
        grad_x = grad_x + conv_full[CONV - 1 - offset] * leading(masked, offset)
    grad_conv_weight = jnp.stack(conv_rows)
    grad_x_tokens = lax.all_to_all(
        grad_x.astype(jnp.bfloat16), "seq", split_axis=1, concat_axis=2, tiled=True
    )
    grad_proj = jnp.concatenate([grad_x_tokens, grad_gate], axis=-1)
    grad_in_proj = jnp.einsum("rtf,rtd->fd", grad_proj, normed, preferred_element_type=jnp.float32)
    grad_normed = jnp.einsum("rtf,fd->rtd", grad_proj, in_whole, preferred_element_type=jnp.float32)
    grad_gain = jnp.sum(grad_normed * scaled, axis=(0, 1))
    grad_scaled = grad_normed * gain_full
    grad_hidden = grad_out.astype(jnp.float32) + inv_rms * (
        grad_scaled - scaled * jnp.mean(grad_scaled * scaled, axis=-1, keepdims=True)
    )
    gain_share, in_share, out_share = (
        lax.psum_scatter(grad_gain, ("seq", "row"), scatter_dimension=0, tiled=True),
        lax.psum_scatter(grad_in_proj, ("seq", "row"), scatter_dimension=0, tiled=True),
        lax.psum_scatter(grad_out_proj, ("seq", "row"), scatter_dimension=0, tiled=True),
    )
    centre = jnp.log(jax.nn.softplus(dt_bias.astype(jnp.float32)))
    offset_dt = jnp.log(dt_vals) - centre
    first_sum = jnp.sum(offset_dt, axis=(0, 1))
    second_sum = jnp.sum(offset_dt * offset_dt, axis=(0, 1))
    summed = lax.psum(
        (
            grad_conv_weight,
            grad_conv_bias,
            grad_x_proj,
            grad_dt_proj,
            grad_dt_bias,
            grad_decay,
            grad_skip,
            first_sum,
            second_sum,
        ),
        "row",
    )
    token_count = full_len * row_count * lax.axis_size("row")
    mean_off = summed[7] / token_count
    spread = jnp.sqrt(summed[8] / token_count - mean_off * mean_off + eps_spread)
    dt_stats = jnp.stack([centre + mean_off, spread])
    return (
        hidden_out,
        grad_hidden,
        gain_share,
        in_share,
        out_share,
        summed[0],
        summed[1],
        summed[2],
        summed[3],
        summed[4],
        summed[5],
        summed[6],
        dt_stats,
    )


def solution(mesh):
    fits = mesh.shape["seq"] == 16 and mesh.shape["row"] == 2
    plan = channel_plan if fits else token_plan
    return jax.shard_map(
        plan,
        mesh=mesh,
        in_specs=(
            P("row", "seq", None),
            P("row", "seq", None),
            P("row", None),
            P(("seq", "row")),
            P(("seq", "row"), None),
            P(("seq", "row"), None),
            P(None, "seq"),
            P("seq"),
            P("seq", None),
            P(None, "seq"),
            P("seq"),
            P(None, "seq"),
            P("seq"),
        ),
        out_specs=(
            P("row", "seq", None),
            P("row", "seq", None),
            P(("seq", "row")),
            P(("seq", "row"), None),
            P(("seq", "row"), None),
            P(None, "seq"),
            P("seq"),
            P("seq", None),
            P(None, "seq"),
            P("seq"),
            P(None, "seq"),
            P("seq"),
            P(None, "seq"),
        ),
        check_vma=False,
    )
```
